32 devices in a mesh: fsdp: 8 (over y, x, core), tp: 4 (over z).
Axes of the slice: x: 2, y: 2, z: 4, core: 2. Of those that a mesh axis runs over, the one named last changes fastest.
Arguments:
- stream: bfloat16 [8, 1024, 2048], P('fsdp', 'tp'), may hold values from -6 to 6
- attn_gain: bfloat16 [2048], P('fsdp'), may hold values from 0.099609375 to 1.8984375
- w_query: bfloat16 [2048, 2048], P('fsdp', 'tp'), may hold values from -0.1875 to 0.1875
- w_key: bfloat16 [2048, 2048], P('fsdp', 'tp'), may hold values from -0.1875 to 0.1875
- w_value: bfloat16 [2048, 2048], P('fsdp', 'tp'), may hold values from -0.125 to 0.125
- w_out: bfloat16 [2048, 2048], P('fsdp', 'tp'), may hold values from -0.5 to 0.5
- mem_gate: float32 [16], P('tp'), may hold values from -3 to 3
- mlp_gain: bfloat16 [2048], P('fsdp'), may hold values from 0.099609375 to 1.8984375
- w_gate: bfloat16 [2048, 8192], P('fsdp', 'tp'), may hold values from -0.125 to 0.125
- w_up: bfloat16 [2048, 8192], P('fsdp', 'tp'), may hold values from -0.125 to 0.125
- w_down: bfloat16 [2048, 8192], P('fsdp', 'tp'), may hold values from -0.125 to 0.125
- memory: float32 [8, 16, 128, 128], P('fsdp', 'tp'), may hold values from -48 to 48
- normalizer: float32 [8, 16, 128], P('fsdp', 'tp'), may hold values from 0.5 to 4
- prefix: int32 [8], replicated, may hold values from 0 to 511
- valid: int32 [8], replicated, may hold values from 513 to 1024, as said below
- cotangent: bfloat16 [8, 1024, 2048], P('fsdp', 'tp'), may hold values from -6 to 6
Outputs:
- stream_out: bfloat16 [8, 1024, 2048], P('fsdp', 'tp')
- stream_grad: float32 [8, 1024, 2048], P('fsdp', 'tp')
- attn_gain_grad: float32 [2048], P('fsdp')
- w_query_grad: float32 [2048, 2048], P('fsdp', 'tp')
- w_key_grad: float32 [2048, 2048], P('fsdp', 'tp')
- w_value_grad: float32 [2048, 2048], P('fsdp', 'tp')
- w_out_grad: float32 [2048, 2048], P('fsdp', 'tp')
- mem_gate_grad: float32 [16], P('tp')
- mlp_gain_grad: float32 [2048], P('fsdp')
- w_gate_grad: float32 [2048, 8192], P('fsdp', 'tp')
- w_up_grad: float32 [2048, 8192], P('fsdp', 'tp')
- w_down_grad: float32 [2048, 8192], P('fsdp', 'tp')
- memory_next: float32 [8, 16, 128, 128], P('fsdp', 'tp')
- normalizer_next: float32 [8, 16, 128], P('fsdp', 'tp')
- memory_grad: float32 [8, 16, 128, 128], P('fsdp', 'tp')
- normalizer_grad: float32 [8, 16, 128], P('fsdp', 'tp')
- rms_stats: float32 [8, 3], P('fsdp')
The draws below stay inside these ranges and needn't reach their ends.
Inputs may be any that keep to these rules, and one draw needn't show every extreme that they name: Every sequence has more valid tokens than half its length; in every draw some sequence has all 1024 tokens valid.
All inputs are finite; a program needn't handle non-finite values.
Results may differ from the reference program's by a relative error of at most 0.015.
Values may be sent and summed in bfloat16 or wider, within the bound.
A program may use at most 256 MiB of HBM per device.

```python
import math
import jax
import jax.numpy as jnp
from jax import lax

D = 2048
H = 16
HD = 128
FF = 8192
LEN = 1024
SEQS = 8


def draw_valid(key, part):
    offsets = jax.random.randint(key, (SEQS,), 0, LEN // 2)
    return (LEN - (offsets - jnp.min(offsets))).astype(jnp.int32)


def with_ends(array, stream_key, low, high):
    place = [jax.random.randint(jax.random.fold_in(stream_key, axis), (), 0, length) for axis, length in enumerate(array.shape)]
    longest = array.shape.index(max(array.shape))
    next_to = place[:longest] + [(place[longest] + 1) % array.shape[longest]] + place[longest + 1:]
    return array.at[tuple(place)].set(low).at[tuple(next_to)].set(high)


def steps_of(stream_key, dims, pieces, smallest, high):
    gain, own = 1.0, jax.random.fold_in(stream_key, 6)
    for axis_at, shards_of in pieces:
        heights = jnp.exp(jax.random.uniform(jax.random.fold_in(own, axis_at), (shards_of,), jnp.float32, smallest / len(pieces), high / len(pieces)))
        gain = gain * jnp.repeat(heights, dims[axis_at] // shards_of).reshape([-1 if axis == axis_at else 1 for axis in range(len(dims))])
    return gain


def scatter_about(rng, extent, width, most, pieces=(), kind=jnp.bfloat16):
    values = width * jax.random.normal(rng, extent, jnp.float32)
    if pieces:
        values = values * steps_of(rng, extent, pieces, -0.22, 0.18)
    return jnp.clip(values, -most, most).astype(kind)


def setup_inputs(seed: int = 0) -> dict:
    arg_keys = jax.random.split(jax.random.key(seed), 17)
    return {
        "stream": scatter_about(arg_keys[0], (SEQS, LEN, D), 1.0, 6.0, ((0, 8), (1, 4))),
        "attn_gain": jnp.clip(1.0 + 0.18 * jax.random.normal(arg_keys[1], (D,), jnp.float32), 0.099609375, 1.8984375).astype(jnp.bfloat16),
        "w_query": scatter_about(arg_keys[2], (D, H * HD), (D // 2) ** -0.5, 0.1875, ((0, 8), (1, 4))),
        "w_key": scatter_about(arg_keys[3], (D, H * HD), (D // 2) ** -0.5, 0.1875, ((0, 8), (1, 4))),
        "w_value": scatter_about(arg_keys[4], (D, H * HD), D ** -0.5, 0.125, ((0, 8), (1, 4))),
        "w_out": scatter_about(arg_keys[5], (D, H * HD), HD ** -0.5, 0.5, ((0, 8), (1, 4))),
        "mem_gate": scatter_about(arg_keys[6], (H,), 1.0, 3.0, ((0, 4),), jnp.float32),
        "mlp_gain": jnp.clip(1.0 + 0.18 * jax.random.normal(arg_keys[7], (D,), jnp.float32), 0.099609375, 1.8984375).astype(jnp.bfloat16),
        "w_gate": scatter_about(arg_keys[8], (D, FF), D ** -0.5, 0.125, ((0, 8), (1, 4))),
        "w_up": scatter_about(arg_keys[9], (D, FF), D ** -0.5, 0.125, ((0, 8), (1, 4))),
        "w_down": scatter_about(arg_keys[10], (D, FF), (FF // 4) ** -0.5, 0.125, ((0, 8), (1, 4))),
        "memory": scatter_about(arg_keys[11], (SEQS, H, HD, HD), 8.0, 48.0, ((0, 8), (1, 4)), jnp.float32),
        "normalizer": jnp.clip(jnp.exp(math.log(4.0) - 2.0794415 * jax.random.uniform(arg_keys[12], (SEQS, H, HD), jnp.float32) ** steps_of(arg_keys[12], (SEQS, H, HD), ((0, 8), (1, 4)), -0.2, 0.2)), 0.5, 4.0),
        "prefix": with_ends(jax.random.randint(arg_keys[13], (SEQS,), 0, LEN // 2), jax.random.fold_in(arg_keys[13], 1), 0, (LEN // 2) - 1).astype(jnp.int32),
        "valid": draw_valid(jax.random.fold_in(arg_keys[16], 71), 0),
        "cotangent": scatter_about(arg_keys[15], (SEQS, LEN, D), 1.0, 6.0, ((0, 8), (1, 4))),
    }


norm_eps = 1e-06
rms_eps = 1e-06
neg_fill = -1e+30

@jax.custom_vjp
def low(v):
    return lax.optimization_barrier(v.astype(jnp.bfloat16)).astype(jnp.float32)

@jax.custom_vjp
def low_back(v):
    return v

def low_keep(v):
    return (low(v), None)

def low_pass(kept, grad):
    return (grad,)

def back_keep(v):
    return (v, None)

def back_low(kept, grad):
    return (low(grad),)
low.defvjp(low_keep, low_pass)
low_back.defvjp(back_keep, back_low)

def both_round(values_in):
    return low(low_back(values_in))

def matmul(first_mat, second_mat):
    return jnp.dot(first_mat, second_mat, precision=lax.Precision.HIGHEST)

def normalize(rows_in):
    return rows_in * lax.rsqrt(lax.optimization_barrier(jnp.mean(rows_in * rows_in, axis=-1, keepdims=True)) + norm_eps)

def norm_gain(rows_in, gain_full):
    return normalize(rows_in) * gain_full

def glu_product(gate_pre, up_pre):
    return jax.nn.gelu(gate_pre) * up_pre

def memory_mix(query_f, local_f, memory_s, normalizer_s, gate_logit):
    mapped = jax.nn.elu(query_f) + 1.0
    numerator = jnp.einsum('lhd,hde->lhe', mapped, memory_s, precision=lax.Precision.HIGHEST)
    denominator = jnp.einsum('lhd,hd->lh', mapped, normalizer_s, precision=lax.Precision.HIGHEST)
    gate_open = jax.nn.sigmoid(gate_logit)[None, :, None]
    return gate_open * (numerator / denominator[:, :, None]) + (1.0 - gate_open) * local_f

def allowed_keys(row_first, row_count, key_count, prefix_len, valid_len):
    row_index = row_first + jnp.arange(row_count, dtype=jnp.int32)
    key_index = jnp.arange(key_count, dtype=jnp.int32)
    causal = key_index[None, :] <= row_index[:, None]
    return (key_index[None, :] < valid_len) & (causal | (key_index[None, :] < prefix_len))

def attend_block(query_block, row_first, key_rows, value_rows, prefix_len, valid_len):
    raw_scores = jnp.einsum('qhd,khd->hqk', query_block, key_rows, precision=lax.Precision.HIGHEST)
    scores = low_back(raw_scores * HD ** (-0.5))
    allowed = allowed_keys(row_first, query_block.shape[0], key_rows.shape[0], prefix_len, valid_len)
    masked = jnp.where(allowed[None], scores, neg_fill)
    attn_probs = jax.nn.softmax(masked, axis=-1)
    mixed_rows = jnp.einsum('hqk,khd->qhd', low(attn_probs), value_rows, precision=lax.Precision.HIGHEST)
    return low_back(mixed_rows)

def layer_forward(stream_rows, attn_gain, w_query, w_key, w_value, w_out, mem_gate, mlp_gain, w_gate, w_up, w_down, memory_s, normalizer_s, prefix_len, valid_len):
    length = stream_rows.shape[0]
    normed_one = low(norm_gain(stream_rows, attn_gain))
    query_rows = both_round(matmul(normed_one, w_query)).reshape(length, H, HD)
    key_rows = both_round(matmul(normed_one, w_key)).reshape(length, H, HD)
    value_rows = both_round(matmul(normed_one, w_value)).reshape(length, H, HD)
    block_rows = min(512, length)
    query_blocks = query_rows.reshape(length // block_rows, block_rows, H, HD)
    block_first = jnp.arange(length // block_rows, dtype=jnp.int32) * block_rows
    checked_block = jax.checkpoint(attend_block)
    local_mix = lax.map(lambda block_pair: checked_block(block_pair[0], block_pair[1], key_rows, value_rows, prefix_len, valid_len), (query_blocks, block_first)).reshape(length, H, HD)
    combined = low(memory_mix(query_rows, local_mix, memory_s, normalizer_s, mem_gate)).reshape(length, H * HD)
    attn_branch = low_back(matmul(combined, w_out.T))
    middle = stream_rows + attn_branch
    normed_two = low(norm_gain(middle, mlp_gain))
    gate_pre = low_back(matmul(normed_two, w_gate))
    up_pre = low_back(matmul(normed_two, w_up))
    hidden = low(glu_product(gate_pre, up_pre))
    mlp_branch = low_back(matmul(hidden, w_down.T))
    result = middle + mlp_branch
    position = jnp.arange(length, dtype=jnp.int32)
    live = (position < valid_len).astype(jnp.float32)
    keys_mapped = (jax.nn.elu(key_rows) + 1.0) * live[:, None, None]
    memory_next = memory_s + jnp.einsum('lhd,lhe->hde', keys_mapped, value_rows, precision=lax.Precision.HIGHEST)
    normalizer_next = normalizer_s + lax.optimization_barrier(jnp.sum(keys_mapped, axis=0))
    token_count = jnp.sum(live) * D

    def rms_all(values_in):
        return jnp.sqrt(jnp.sum(values_in * values_in * live[:, None]) / token_count + rms_eps)
    rms_stats = jnp.stack([rms_all(result), rms_all(attn_branch), rms_all(mlp_branch)])
    return (result, (memory_next, normalizer_next, rms_stats))

def reference(stream, attn_gain, w_query, w_key, w_value, w_out, mem_gate, mlp_gain, w_gate, w_up, w_down, memory, normalizer, prefix, valid, cotangent):
    params = tuple((weight.astype(jnp.float32) for weight in (attn_gain, w_query, w_key, w_value, w_out, mem_gate, mlp_gain, w_gate, w_up, w_down)))

    def one_sequence(grad_totals, inputs):
        seq_stream, seq_memory, seq_normalizer, seq_prefix, seq_valid, seq_cot = inputs

        def forward(stream_in, params_in, memory_in, normalizer_in):
            return layer_forward(stream_in, *params_in, memory_in, normalizer_in, seq_prefix, seq_valid)
        result, pullback, extras = jax.vjp(forward, seq_stream.astype(jnp.float32), params, seq_memory, seq_normalizer, has_aux=True)
        grad_stream, grad_params, grad_memory, grad_normalizer = pullback(seq_cot.astype(jnp.float32))
        grad_totals = jax.tree.map(lambda total_grad, new_grad: total_grad + new_grad, grad_totals, grad_params)
        return (grad_totals, (result.astype(jnp.bfloat16), grad_stream, extras[0], extras[1], grad_memory, grad_normalizer, extras[2]))
    zero_grads = jax.tree.map(jnp.zeros_like, params)
    grad_totals, outputs = lax.scan(one_sequence, zero_grads, (stream, memory, normalizer, prefix, valid, cotangent))
    stream_out, stream_grad, memory_next, normalizer_next, memory_grad, normalizer_grad, rms_stats = outputs
    return (stream_out, stream_grad, grad_totals[0], grad_totals[1], grad_totals[2], grad_totals[3], grad_totals[4], grad_totals[5], grad_totals[6], grad_totals[7], grad_totals[8], grad_totals[9], memory_next, normalizer_next, memory_grad, normalizer_grad, rms_stats)
```

```python
import functools

import jax
import jax.numpy as jnp
from jax import lax
from jax.experimental import pallas as pl
from jax.experimental.pallas import tpu as pltpu
from jax.sharding import PartitionSpec as P

NEG = -1e30
LOG2E = 1.4426950408889634


def split_two(x):
    high = x.astype(jnp.bfloat16)
    return high, (x - high.astype(jnp.float32)).astype(jnp.bfloat16)


def dot32(a, b, dims):
    return lax.dot_general(a, b, (dims, ((), ())), preferred_element_type=jnp.float32)


def dot_three(a, b, dims):
    ah, al = split_two(a)
    bh, bl = split_two(b)
    return dot32(ah, bh, dims) + dot32(ah, bl, dims) + dot32(al, bh, dims)


NN, NT, TN = ((1,), (0,)), ((1,), (1,)), ((0,), (0,))


def mapped(v):
    return jnp.where(v > 0, v + 1.0, jnp.exp(jnp.minimum(v, 0.0)))


def key_reach(first, rows, keys):
    return min(keys, max(keys // 2, first + rows))


def key_limit(first, rows, prefix, valid):
    row = first + lax.broadcasted_iota(jnp.int32, (1, rows), 1)
    return jnp.minimum(valid - 1, jnp.maximum(row, prefix - 1))


def forward_kernel(bounds, q_ref, k_ref, v_ref, mem_ref, norm_ref, gate_ref, comb_ref, mix_ref, lse_ref, memo_ref, normo_ref, *, block):
    keys, hd = k_ref.shape
    prefix, valid = bounds[0], bounds[1]
    scale = hd ** -0.5 * LOG2E
    gate = jax.nn.sigmoid(gate_ref[0])
    memory = mem_ref[0]
    norm = norm_ref[0]
    for first in range(0, keys, block):
        reach = key_reach(first, block, keys)
        q = q_ref[first : first + block, :]
        s = dot32(k_ref[:reach, :], q, NT) * scale
        limit = key_limit(first, block, prefix, valid)
        s = jnp.where(lax.broadcasted_iota(jnp.int32, s.shape, 0) <= limit, s, NEG)
        top = jnp.max(s, axis=0, keepdims=True)
        p = jnp.exp2(s - top)
        total = jnp.sum(p, axis=0, keepdims=True)
        mixed = dot32(v_ref[:reach, :], p.astype(jnp.bfloat16), TN) / total
        mixed = mixed.T
        lse_ref[0, :, first : first + block] = top + jnp.log2(total)
        qm = mapped(q.astype(jnp.float32))
        denominator = jnp.sum(qm * norm, axis=-1, keepdims=True)
        retrieved = dot_three(qm, memory, NN) / denominator
        mix_ref[first : first + block, :] = mixed
        comb_ref[first : first + block, :] = (gate * retrieved + (1.0 - gate) * mixed).astype(jnp.bfloat16)
    km = mapped(k_ref[...].astype(jnp.float32))
    km = jnp.where(lax.broadcasted_iota(jnp.int32, km.shape, 0) < valid, km, 0.0)
    kh, kl = split_two(km)
    memo_ref[0] = memory + dot32(kh, v_ref[...], TN) + dot32(kl, v_ref[...], TN)
    normo_ref[0] = norm + jnp.sum(km, axis=0, keepdims=True)


def backward_kernel(bounds, q_ref, k_ref, v_ref, gc_ref, mix_ref, lse_ref, mem_ref, norm_ref, gate_ref, dq_ref, dk_ref, dv_ref, dmem_ref, dnorm_ref, dgate_ref, dk_acc, dv_acc, *, block):
    keys, hd = k_ref.shape
    prefix, valid = bounds[0], bounds[1]
    scale = hd ** -0.5
    gate = jax.nn.sigmoid(gate_ref[0])
    memory = mem_ref[0]
    norm = norm_ref[0]
    dmem = jnp.zeros((hd, hd), jnp.float32)
    dnorm = jnp.zeros((1, hd), jnp.float32)
    dgate = jnp.zeros((1, hd), jnp.float32)
    for first in range(keys - block, -1, -block):
        reach = key_reach(first, block, keys)
        rows = slice(first, first + block)
        q = q_ref[rows, :]
        gc = gc_ref[rows, :].astype(jnp.float32)
        mixed = mix_ref[rows, :]
        qm = mapped(q.astype(jnp.float32))
        inverse = 1.0 / jnp.sum(qm * norm, axis=-1, keepdims=True)
        retrieved = dot_three(qm, memory, NN) * inverse
        dgate = dgate + jnp.sum(gc * (retrieved - mixed), axis=0, keepdims=True)
        gnum = gate * gc * inverse
        gden = -jnp.sum(gnum * retrieved, axis=-1, keepdims=True)
        dmem = dmem + dot_three(qm, gnum, TN)
        dnorm = dnorm + jnp.sum(gden * qm, axis=0, keepdims=True)
        dq_mem = (dot_three(gnum, memory, NT) + gden * norm) * jnp.minimum(qm, 1.0)
        low = ((1.0 - gate) * gc).astype(jnp.bfloat16)
        delta = jnp.sum((low.astype(jnp.float32) * mixed).T, axis=0, keepdims=True)
        s = dot32(k_ref[:reach, :], q, NT) * (scale * LOG2E)
        limit = key_limit(first, block, prefix, valid)
        s = jnp.where(lax.broadcasted_iota(jnp.int32, s.shape, 0) <= limit, s - lse_ref[0, :, rows], NEG)
        p = jnp.exp2(s)
        gp = dot32(v_ref[:reach, :], low, NT)
        gs = (p * (gp - delta)).astype(jnp.bfloat16)
        dv = dot32(p.astype(jnp.bfloat16), low, NN)
        dk = dot32(gs, q, NN)
        if first == keys - block:
            dv_acc[...] = dv
            dk_acc[...] = dk
        else:
            dv_acc[:reach, :] += dv
            dk_acc[:reach, :] += dk
        dq = dot32(k_ref[:reach, :], gs, TN).T * scale
        dq_ref[rows, :] = (dq + dq_mem).astype(jnp.bfloat16)
    dk_ref[...] = (dk_acc[...] * scale).astype(jnp.bfloat16)
    dv_ref[...] = dv_acc[...].astype(jnp.bfloat16)
    dmem_ref[0] = dmem
    dnorm_ref[0] = dnorm
    dgate_ref[0] = dgate * (gate * (1.0 - gate))


def head_specs(keys, hd):
    rows = pl.BlockSpec((keys, hd), lambda h: (0, h))
    square = pl.BlockSpec((1, hd, hd), lambda h: (h, 0, 0))
    line = pl.BlockSpec((1, 1, hd), lambda h: (h, 0, 0))
    long = pl.BlockSpec((1, 1, keys), lambda h: (h, 0, 0))
    return rows, square, line, long


def attend(bounds, q, k, v, memory, norm, gate, block=256):
    keys = q.shape[0]
    heads, hd = memory.shape[:2]
    rows, square, line, long = head_specs(keys, hd)
    f32 = jnp.float32
    S = jax.ShapeDtypeStruct
    return pl.pallas_call(
        functools.partial(forward_kernel, block=block),
        grid=(heads,),
        in_specs=[pl.BlockSpec(memory_space=pltpu.SMEM), rows, rows, rows, square, line, line],
        out_specs=[rows, rows, long, square, line],
        out_shape=[S(q.shape, jnp.bfloat16), S(q.shape, f32), S((heads, 1, keys), f32), S((heads, hd, hd), f32), S((heads, 1, hd), f32)],
        compiler_params=pltpu.CompilerParams(vmem_limit_bytes=48 * 2**20),
        name="attend_forward",
    )(bounds, q, k, v, memory, norm.reshape(heads, 1, hd), jnp.broadcast_to(gate[:, None, None], (heads, 1, hd)))


def attend_back(bounds, q, k, v, gc, mix, lse, memory, norm, gate, block=256):
    keys = q.shape[0]
    heads, hd = memory.shape[:2]
    rows, square, line, long = head_specs(keys, hd)
    f32 = jnp.float32
    S = jax.ShapeDtypeStruct
    low = S(q.shape, jnp.bfloat16)
    return pl.pallas_call(
        functools.partial(backward_kernel, block=block),
        grid=(heads,),
        in_specs=[pl.BlockSpec(memory_space=pltpu.SMEM), rows, rows, rows, rows, rows, long, square, line, line],
        out_specs=[rows, rows, rows, square, line, line],
        out_shape=[low, low, low, S((heads, hd, hd), f32), S((heads, 1, hd), f32), S((heads, 1, hd), f32)],
        scratch_shapes=[pltpu.VMEM((keys, hd), f32), pltpu.VMEM((keys, hd), f32)],
        compiler_params=pltpu.CompilerParams(vmem_limit_bytes=48 * 2**20),
        name="attend_backward",
    )(bounds, q, k, v, gc, mix, lse, memory, norm.reshape(heads, 1, hd), jnp.broadcast_to(gate[:, None, None], (heads, 1, hd)))

norm_eps = 1e-06
rms_eps = 1e-06


def normalize(rows_in):
    return rows_in * lax.rsqrt(jnp.mean(rows_in * rows_in, axis=-1, keepdims=True) + norm_eps)


def norm_gain(rows_in, gain_full):
    return normalize(rows_in) * gain_full


def glu_product(gate_pre, up_pre):
    return jax.nn.gelu(gate_pre) * up_pre


def contract_rows(first_mat, second_mat):
    return lax.dot_general(
        first_mat, second_mat, (((0,), (0,)), ((), ())), preferred_element_type=jnp.float32
    )


def times_transpose(first_mat, second_mat):
    return lax.dot_general(
        first_mat, second_mat, (((1,), (1,)), ((), ())), preferred_element_type=jnp.float32
    )


def scatter_low(terms, axis, dim):
    return lax.psum_scatter(
        terms.astype(jnp.bfloat16), axis, scatter_dimension=dim, tiled=True
    ).astype(jnp.float32)


def fetch_attention(attn_gain, w_query, w_key, w_value, w_out):
    return (
        lax.all_gather(attn_gain, "fsdp", axis=0, tiled=True),
        lax.all_gather(w_query, "fsdp", axis=0, tiled=True),
        lax.all_gather(w_key, "fsdp", axis=0, tiled=True),
        lax.all_gather(w_value, "fsdp", axis=0, tiled=True),
        lax.all_gather(w_out, "fsdp", axis=0, tiled=True),
    )


def fetch_mlp(mlp_gain, w_gate, w_up, w_down):
    return (
        lax.all_gather(mlp_gain, "fsdp", axis=0, tiled=True),
        lax.all_gather(w_gate, "fsdp", axis=0, tiled=True),
        lax.all_gather(w_up, "fsdp", axis=0, tiled=True),
        lax.all_gather(w_down, "fsdp", axis=0, tiled=True),
    )


def on_device(
    stream,
    attn_gain,
    w_query,
    w_key,
    w_value,
    w_out,
    mem_gate,
    mlp_gain,
    w_gate,
    w_up,
    w_down,
    memory,
    normalizer,
    prefix,
    valid,
    cotangent,
):
    len_dev, width = (stream.shape[1], stream.shape[2])
    seq_len = len_dev * lax.axis_size("tp")
    seq_here = lax.axis_index("fsdp")
    prefix_len = prefix[seq_here]
    valid_len = valid[seq_here]
    full_shape = (1, seq_len, width)
    gain_one, query_full, key_full, value_full, out_full = fetch_attention(
        attn_gain, w_query, w_key, w_value, w_out
    )
    stream_f = stream.astype(jnp.float32)
    normed_local, norm_one_back = jax.vjp(norm_gain, stream_f, gain_one.astype(jnp.float32))
    normed_one = lax.all_gather(normed_local.astype(jnp.bfloat16), "tp", axis=1, tiled=True)
    flat_one = normed_one.reshape(seq_len, width)
    def project(weight):
        return jnp.dot(flat_one, weight, preferred_element_type=jnp.float32).astype(jnp.bfloat16)

    query_rows, key_rows, value_rows = project(query_full), project(key_full), project(value_full)
    bounds = jnp.stack([prefix_len, valid_len])
    combined, local_mix, log_total, memory_next, normalizer_next = attend(
        bounds, query_rows, key_rows, value_rows, memory[0], normalizer[0], mem_gate
    )
    attn_branch = scatter_low(times_transpose(combined, out_full).reshape(full_shape), "tp", 1)
    middle = stream_f + attn_branch
    gain_two, gate_full, up_full, down_full = fetch_mlp(mlp_gain, w_gate, w_up, w_down)
    normed_mid, norm_two_back = jax.vjp(norm_gain, middle, gain_two.astype(jnp.float32))
    normed_two = lax.all_gather(normed_mid.astype(jnp.bfloat16), "tp", axis=1, tiled=True)
    flat_two = normed_two.reshape(seq_len, width)
    gate_pre = jnp.dot(flat_two, gate_full, preferred_element_type=jnp.float32)
    up_pre = jnp.dot(flat_two, up_full, preferred_element_type=jnp.float32)
    hidden_f, glu_back = jax.vjp(glu_product, gate_pre, up_pre)
    hidden = hidden_f.astype(jnp.bfloat16)
    mlp_branch = scatter_low(times_transpose(hidden, down_full).reshape(full_shape), "tp", 1)
    result = middle + mlp_branch
    stream_out = result.astype(jnp.bfloat16)
    local_position = lax.axis_index("tp") * len_dev + jnp.arange(len_dev, dtype=jnp.int32)
    live_here = (local_position < valid_len).astype(jnp.float32)[None, :, None]

    def square_sum(values_in):
        return jnp.sum(values_in * values_in * live_here, axis=(1, 2))

    stat_terms = jnp.stack(
        [square_sum(result), square_sum(attn_branch), square_sum(mlp_branch)], axis=1
    )
    gain_two, gate_full, up_full, down_full = fetch_mlp(mlp_gain, w_gate, w_up, w_down)
    cot_all = lax.all_gather(cotangent, "tp", axis=1, tiled=True).reshape(seq_len, width)
    grad_hidden = jnp.dot(cot_all, down_full, preferred_element_type=jnp.float32)
    grad_down = contract_rows(cot_all, hidden)
    grad_gate_pre, grad_up_pre = glu_back(grad_hidden)
    gate_low = grad_gate_pre.astype(jnp.bfloat16)
    up_low = grad_up_pre.astype(jnp.bfloat16)
    two_terms = times_transpose(gate_low, gate_full) + times_transpose(up_low, up_full)
    grad_normed_two = scatter_low(two_terms.reshape(full_shape), "tp", 1)
    grad_gate = contract_rows(flat_two, gate_low)
    grad_up = contract_rows(flat_two, up_low)
    grad_middle_in, grad_gain_two = norm_two_back(grad_normed_two)
    grad_middle = cotangent.astype(jnp.float32) + grad_middle_in
    gain_one, query_full, key_full, value_full, out_full = fetch_attention(
        attn_gain, w_query, w_key, w_value, w_out
    )
    branch_low = lax.all_gather(grad_middle.astype(jnp.bfloat16), "tp", axis=1, tiled=True).reshape(
        seq_len, width
    )
    grad_out = contract_rows(branch_low, combined)
    grad_combined = jnp.dot(branch_low, out_full, preferred_element_type=jnp.float32)
    query_low, key_low, value_low, grad_memory, grad_normalizer, gate_parts = attend_back(
        bounds, query_rows, key_rows, value_rows, grad_combined, local_mix, log_total,
        memory[0], normalizer[0], mem_gate,
    )
    grad_gate_logit = jnp.sum(gate_parts, axis=(1, 2))
    one_terms = (
        times_transpose(query_low, query_full)
        + times_transpose(key_low, key_full)
        + times_transpose(value_low, value_full)
    )
    grad_normed_one = scatter_low(one_terms.reshape(full_shape), "tp", 1)
    grad_query = contract_rows(flat_one, query_low)
    grad_key = contract_rows(flat_one, key_low)
    grad_value = contract_rows(flat_one, value_low)
    grad_stream_in, grad_gain_one = norm_one_back(grad_normed_one)
    stream_grad = grad_middle + grad_stream_in
    gate_tiled = jnp.tile(grad_gate_logit, lax.axis_size("fsdp"))
    joined = (
        lax.psum_scatter(grad_gain_one, "fsdp", scatter_dimension=0, tiled=True),
        scatter_low(grad_query, "fsdp", 0),
        scatter_low(grad_key, "fsdp", 0),
        scatter_low(grad_value, "fsdp", 0),
        scatter_low(grad_out, "fsdp", 0),
        lax.psum_scatter(gate_tiled, "fsdp", scatter_dimension=0, tiled=True),
        lax.psum_scatter(grad_gain_two, "fsdp", scatter_dimension=0, tiled=True),
        scatter_low(grad_gate, "fsdp", 0),
        scatter_low(grad_up, "fsdp", 0),
        scatter_low(grad_down, "fsdp", 0),
    )
    stat_sums, gain_one_grad, gain_two_grad = lax.psum((stat_terms, joined[0], joined[6]), "tp")
    token_count = valid_len.astype(jnp.float32) * width
    rms_stats = jnp.sqrt(stat_sums / token_count + rms_eps)
    return (
        stream_out,
        stream_grad,
        gain_one_grad,
        joined[1],
        joined[2],
        joined[3],
        joined[4],
        joined[5],
        gain_two_grad,
        joined[7],
        joined[8],
        joined[9],
        memory_next[None],
        normalizer_next[:, 0][None],
        grad_memory[None],
        grad_normalizer[:, 0][None],
        rms_stats,
    )


def solution(mesh):
    placed = (
        P("fsdp", "tp", None),
        P("fsdp"),
        P("fsdp", "tp"),
        P("fsdp", "tp"),
        P("fsdp", "tp"),
        P("fsdp", "tp"),
        P("tp"),
        P("fsdp"),
        P("fsdp", "tp"),
        P("fsdp", "tp"),
        P("fsdp", "tp"),
        P("fsdp", "tp", None, None),
        P("fsdp", "tp", None),
        P(),
        P(),
        P("fsdp", "tp", None),
    )
    return jax.shard_map(
        on_device,
        mesh=mesh,
        in_specs=placed,
        out_specs=(
            P("fsdp", "tp", None),
            P("fsdp", "tp", None),
            P("fsdp"),
            P("fsdp", "tp"),
            P("fsdp", "tp"),
            P("fsdp", "tp"),
            P("fsdp", "tp"),
            P("tp"),
            P("fsdp"),
            P("fsdp", "tp"),
            P("fsdp", "tp"),
            P("fsdp", "tp"),
            P("fsdp", "tp", None, None),
            P("fsdp", "tp", None),
            P("fsdp", "tp", None, None),
            P("fsdp", "tp", None),
            P("fsdp", None),
        ),
        check_vma=False,
    )
```

```python
import functools

import jax
import jax.numpy as jnp
from jax import lax
from jax.experimental import pallas as pl
from jax.experimental.pallas import tpu as pltpu
from jax.sharding import PartitionSpec as P

rms_eps = 1e-06
NEG = -1e30
LOG2E = 1.4426950408889634


def split_two(x):
    high = x.astype(jnp.bfloat16)
    return high, (x - high.astype(jnp.float32)).astype(jnp.bfloat16)


def dot32(a, b, dims):
    return lax.dot_general(a, b, (dims, ((), ())), preferred_element_type=jnp.float32)


def dot_three(a, b, dims):
    ah, al = split_two(a)
    bh, bl = split_two(b)
    return dot32(ah, bh, dims) + dot32(ah, bl, dims) + dot32(al, bh, dims)


NN, NT, TN = ((1,), (0,)), ((1,), (1,)), ((0,), (0,))


def mapped(v):
    return jnp.where(v > 0, v + 1.0, jnp.exp(jnp.minimum(v, 0.0)))


def key_reach(first, rows, keys):
    return min(keys, max(keys // 2, first + rows))


def key_limit(first, rows, prefix, valid):
    row = first + lax.broadcasted_iota(jnp.int32, (1, rows), 1)
    return jnp.minimum(valid - 1, jnp.maximum(row, prefix - 1))


def forward_kernel(bounds, q_ref, k_ref, v_ref, mem_ref, norm_ref, gate_ref, comb_ref, mix_ref, lse_ref, memo_ref, normo_ref, *, block):
    keys, hd = k_ref.shape
    prefix, valid = bounds[0], bounds[1]
    scale = hd ** -0.5 * LOG2E
    gate = jax.nn.sigmoid(gate_ref[0])
    memory = mem_ref[0]
    norm = norm_ref[0]
    for first in range(0, keys, block):
        reach = key_reach(first, block, keys)
        q = q_ref[first : first + block, :]
        s = dot32(k_ref[:reach, :], q, NT) * scale
        limit = key_limit(first, block, prefix, valid)
        s = jnp.where(lax.broadcasted_iota(jnp.int32, s.shape, 0) <= limit, s, NEG)
        top = jnp.max(s, axis=0, keepdims=True)
        p = jnp.exp2(s - top)
        total = jnp.sum(p, axis=0, keepdims=True)
        mixed = dot32(v_ref[:reach, :], p.astype(jnp.bfloat16), TN) / total
        mixed = mixed.T
        lse_ref[0, :, first : first + block] = top + jnp.log2(total)
        qm = mapped(q.astype(jnp.float32))
        denominator = jnp.sum(qm * norm, axis=-1, keepdims=True)
        retrieved = dot_three(qm, memory, NN) / denominator
        mix_ref[first : first + block, :] = mixed
        comb_ref[first : first + block, :] = (gate * retrieved + (1.0 - gate) * mixed).astype(jnp.bfloat16)
    km = mapped(k_ref[...].astype(jnp.float32))
    km = jnp.where(lax.broadcasted_iota(jnp.int32, km.shape, 0) < valid, km, 0.0)
    kh, kl = split_two(km)
    memo_ref[0] = memory + dot32(kh, v_ref[...], TN) + dot32(kl, v_ref[...], TN)
    normo_ref[0] = norm + jnp.sum(km, axis=0, keepdims=True)


def backward_kernel(bounds, q_ref, k_ref, v_ref, gc_ref, mix_ref, lse_ref, mem_ref, norm_ref, gate_ref, dq_ref, dk_ref, dv_ref, dmem_ref, dnorm_ref, dgate_ref, dk_acc, dv_acc, *, block):
    keys, hd = k_ref.shape
    prefix, valid = bounds[0], bounds[1]
    scale = hd ** -0.5
    gate = jax.nn.sigmoid(gate_ref[0])
    memory = mem_ref[0]
    norm = norm_ref[0]
    dmem = jnp.zeros((hd, hd), jnp.float32)
    dnorm = jnp.zeros((1, hd), jnp.float32)
    dgate = jnp.zeros((1, hd), jnp.float32)
    for first in range(keys - block, -1, -block):
        reach = key_reach(first, block, keys)
        rows = slice(first, first + block)
        q = q_ref[rows, :]
        gc = gc_ref[rows, :].astype(jnp.float32)
        mixed = mix_ref[rows, :]
        qm = mapped(q.astype(jnp.float32))
        inverse = 1.0 / jnp.sum(qm * norm, axis=-1, keepdims=True)
        retrieved = dot_three(qm, memory, NN) * inverse
        dgate = dgate + jnp.sum(gc * (retrieved - mixed), axis=0, keepdims=True)
        gnum = gate * gc * inverse
        gden = -jnp.sum(gnum * retrieved, axis=-1, keepdims=True)
        dmem = dmem + dot_three(qm, gnum, TN)
        dnorm = dnorm + jnp.sum(gden * qm, axis=0, keepdims=True)
        dq_mem = (dot_three(gnum, memory, NT) + gden * norm) * jnp.minimum(qm, 1.0)
        low = ((1.0 - gate) * gc).astype(jnp.bfloat16)
        delta = jnp.sum((low.astype(jnp.float32) * mixed).T, axis=0, keepdims=True)
        s = dot32(k_ref[:reach, :], q, NT) * (scale * LOG2E)
        limit = key_limit(first, block, prefix, valid)
        s = jnp.where(lax.broadcasted_iota(jnp.int32, s.shape, 0) <= limit, s - lse_ref[0, :, rows], NEG)
        p = jnp.exp2(s)
        gp = dot32(v_ref[:reach, :], low, NT)
        gs = (p * (gp - delta)).astype(jnp.bfloat16)
        dv = dot32(p.astype(jnp.bfloat16), low, NN)
        dk = dot32(gs, q, NN)
        if first == keys - block:
            dv_acc[...] = dv
            dk_acc[...] = dk
        else:
            dv_acc[:reach, :] += dv
            dk_acc[:reach, :] += dk
        dq = dot32(k_ref[:reach, :], gs, TN).T * scale
        dq_ref[rows, :] = (dq + dq_mem).astype(jnp.bfloat16)
    dk_ref[...] = (dk_acc[...] * scale).astype(jnp.bfloat16)
    dv_ref[...] = dv_acc[...].astype(jnp.bfloat16)
    dmem_ref[0] = dmem
    dnorm_ref[0] = dnorm
    dgate_ref[0] = dgate * (gate * (1.0 - gate))


def head_specs(keys, hd):
    rows = pl.BlockSpec((keys, hd), lambda h: (0, h))
    square = pl.BlockSpec((1, hd, hd), lambda h: (h, 0, 0))
    line = pl.BlockSpec((1, 1, hd), lambda h: (h, 0, 0))
    long = pl.BlockSpec((1, 1, keys), lambda h: (h, 0, 0))
    return rows, square, line, long


def attend(bounds, q, k, v, memory, norm, gate, block=256):
    keys = q.shape[0]
    heads, hd = memory.shape[:2]
    rows, square, line, long = head_specs(keys, hd)
    f32 = jnp.float32
    S = jax.ShapeDtypeStruct
    return pl.pallas_call(
        functools.partial(forward_kernel, block=block),
        grid=(heads,),
        in_specs=[pl.BlockSpec(memory_space=pltpu.SMEM), rows, rows, rows, square, line, line],
        out_specs=[rows, rows, long, square, line],
        out_shape=[S(q.shape, jnp.bfloat16), S(q.shape, f32), S((heads, 1, keys), f32), S((heads, hd, hd), f32), S((heads, 1, hd), f32)],
        compiler_params=pltpu.CompilerParams(vmem_limit_bytes=48 * 2**20),
        name="attend_forward",
    )(bounds, q, k, v, memory, norm.reshape(heads, 1, hd), jnp.broadcast_to(gate[:, None, None], (heads, 1, hd)))


def attend_back(bounds, q, k, v, gc, mix, lse, memory, norm, gate, block=256):
    keys = q.shape[0]
    heads, hd = memory.shape[:2]
    rows, square, line, long = head_specs(keys, hd)
    f32 = jnp.float32
    S = jax.ShapeDtypeStruct
    low = S(q.shape, jnp.bfloat16)
    return pl.pallas_call(
        functools.partial(backward_kernel, block=block),
        grid=(heads,),
        in_specs=[pl.BlockSpec(memory_space=pltpu.SMEM), rows, rows, rows, rows, rows, long, square, line, line],
        out_specs=[rows, rows, rows, square, line, line],
        out_shape=[low, low, low, S((heads, hd, hd), f32), S((heads, 1, hd), f32), S((heads, 1, hd), f32)],
        scratch_shapes=[pltpu.VMEM((keys, hd), f32), pltpu.VMEM((keys, hd), f32)],
        compiler_params=pltpu.CompilerParams(vmem_limit_bytes=48 * 2**20),
        name="attend_backward",
    )(bounds, q, k, v, gc, mix, lse, memory, norm.reshape(heads, 1, hd), jnp.broadcast_to(gate[:, None, None], (heads, 1, hd)))


norm_eps = 1e-06
MESH = pl.DeviceIdType.MESH
RIGHT, LEFT = 0, 1


class Line:
    def __init__(self, size, send_sem, recv_sem):
        self.size, self.send_sem, self.recv_sem = size, send_sem, recv_sem
        self.here = lax.axis_index("tp")

    def meet(self):
        barrier = pltpu.get_barrier_semaphore()
        last = self.size - 1

        @pl.when(self.here > 0)
        def _():
            pl.semaphore_signal(barrier, inc=1, device_id={"tp": self.here - 1}, device_id_type=MESH)

        @pl.when(self.here < last)
        def _():
            pl.semaphore_signal(barrier, inc=1, device_id={"tp": self.here + 1}, device_id_type=MESH)

        peers = (self.here > 0).astype(jnp.int32) + (self.here < last).astype(jnp.int32)
        pl.semaphore_wait(barrier, peers)

    def copy(self, phase, way, slot, src, dst):
        to = self.here + 1 if way == RIGHT else self.here - 1
        return pltpu.make_async_remote_copy(
            src_ref=src,
            dst_ref=dst,
            send_sem=self.send_sem.at[phase, way, slot],
            recv_sem=self.recv_sem.at[phase, way, slot],
            device_id={"tp": to},
            device_id_type=MESH,
        )

    def arrived(self, phase, way, slot, dst):
        self.copy(phase, way, slot, dst, dst).wait_recv()

    def scatter_step(self, phase, k, part, land_right, land_left):
        n, t = self.size, self.here
        far, near = n - 1 - k, k

        def pass_on(way, shard, land, first):
            @pl.when(jnp.logical_not(first))
            def _():
                self.arrived(phase, way, k, land)
                part[shard] = (part[shard].astype(jnp.float32) + land[...].astype(jnp.float32)).astype(part.dtype)

            self.copy(phase, way, k, part.at[shard], land).start()

        @pl.when(t < far)
        def _():
            pass_on(RIGHT, far, land_right.at[far - 1], t == 0)

        @pl.when(t > near)
        def _():
            pass_on(LEFT, near, land_left.at[near], t == n - 1)

    def scatter_end(self, phase, part, land_right, land_left, total):
        n, t = self.size, self.here
        total[...] = part[t].astype(jnp.float32)

        @pl.when(t > 0)
        def _():
            self.arrived(phase, RIGHT, n - 1 - t, land_right.at[t - 1])
            total[...] += land_right[t - 1].astype(jnp.float32)

        @pl.when(t < n - 1)
        def _():
            self.arrived(phase, LEFT, t, land_left.at[t])
            total[...] += land_left[t].astype(jnp.float32)

    def scatter_sent(self, phase, part, land_right, land_left):
        n, t = self.size, self.here
        for k in range(n - 1):
            far, near = n - 1 - k, k

            @pl.when(t < far)
            def _():
                self.copy(phase, RIGHT, k, part.at[far], land_right.at[far - 1]).wait_send()

            @pl.when(t > near)
            def _():
                self.copy(phase, LEFT, k, part.at[near], land_left.at[near]).wait_send()

    def gather_step(self, phase, k, rows):
        n, t = self.size, self.here

        @pl.when(t >= k)
        def _():
            shard = rows.at[t - k]
            if k > 0:
                self.arrived(phase, RIGHT, k - 1, shard)
            if k < n - 1:
                @pl.when(t < n - 1)
                def _():
                    self.copy(phase, RIGHT, k, shard, shard).start()

        @pl.when(t + k <= n - 1)
        def _():
            shard = rows.at[t + k]
            if k > 0:
                self.arrived(phase, LEFT, k - 1, shard)
            if k < n - 1:
                @pl.when(t > 0)
                def _():
                    self.copy(phase, LEFT, k, shard, shard).start()

    def gather_sent(self, phase, rows):
        n, t = self.size, self.here
        for k in range(n - 1):
            @pl.when((t >= k) & (t < n - 1))
            def _():
                self.copy(phase, RIGHT, k, rows.at[t - k], rows.at[t - k]).wait_send()

            @pl.when((t + k <= n - 1) & (t > 0))
            def _():
                self.copy(phase, LEFT, k, rows.at[t + k], rows.at[t + k]).wait_send()


GELU_A, GELU_B = 0.7978845608028654, 0.044715


def gelu_pair(v):
    square = v * v
    curve = jnp.tanh(v * (GELU_A + GELU_A * GELU_B * square))
    half = 0.5 + 0.5 * curve
    slope = half + (0.5 * v) * (1.0 - curve * curve) * (GELU_A + 3.0 * GELU_A * GELU_B * square)
    return v * half, slope


def middle_kernel(
    blocks, comb_hbm, wout_hbm, stream_hbm, cot_hbm, cot_all_hbm, gain_ref, *rest,
    chunks, size, masks, halves, tile,
):
    weights_in = rest[:blocks]
    (x_out, hid_out, gl_out, ul_out, mlp_out, mid_out, gmid_out, ggain_ref, stat_ref,
     w_three, x, cot, hid, gl, ul, part, land_r, land_l, stream, mid, total,
     load_sem, weight_sem, comb_sem, wout_sem, out_sem, send_sem, recv_sem, live_ref) = rest[blocks:]
    n, c_rows = size, x.shape[2]
    t, f = lax.axis_index("tp"), lax.axis_index("fsdp")
    width = x.shape[3]
    units = hid.shape[1]
    line = Line(n, send_sem, recv_sem)

    inner = comb_hbm.shape[-1]
    loads = [pltpu.make_async_copy(stream_hbm, stream, load_sem.at[2])]
    for c in range(chunks):
        for s in range(n):
            loads.append(
                pltpu.make_async_copy(
                    comb_hbm.at[s * chunks + c],
                    hid.at[s * c_rows : (s + 1) * c_rows, c * inner : (c + 1) * inner],
                    comb_sem.at[c * n + s],
                )
            )
    for j in range(width // tile):
        loads.append(
            pltpu.make_async_copy(
                wout_hbm.at[j * tile : (j + 1) * tile, :], gl.at[:, j * inner : (j + 1) * inner], wout_sem.at[j]
            )
        )
    for item in loads:
        item.start()
    cot_own = stream
    cot_load = pltpu.make_async_copy(cot_hbm, cot_own, load_sem.at[3])
    cot_loads = [pltpu.make_async_copy(cot_all_hbm.at[c], cot, load_sem.at[4 + c]) for c in range(chunks)]
    cot_loads[0].start()
    weight_loads = []
    half_rows = width // (len(masks) * halves)
    for b, block in enumerate(weights_in):
        mask, half = masks[b // halves], b % halves
        owner = lax.bitwise_xor(f, mask) if mask else f
        rows = pl.ds(pl.multiple_of(owner * (half_rows * halves) + half * half_rows, half_rows), half_rows)
        weight_loads.append(pltpu.make_async_copy(block, w_three.at[:, rows, :], weight_sem.at[b]))
    for item in weight_loads:
        item.start()
    line.meet()
    for item in loads[1:]:
        item.wait()

    def project(c):
        flat = part.at[c].reshape(n * c_rows, width)

        @pl.loop(0, width // tile)
        def _(j):
            cols = pl.ds(pl.multiple_of(j * tile, tile), tile)
            weight = gl[:, pl.ds(pl.multiple_of(j * inner, inner), inner)]
            flat[:, cols] = dot32(hid[:, c * inner : (c + 1) * inner], weight, NT).astype(jnp.bfloat16)

    def inverse_rms(v):
        return lax.rsqrt(jnp.mean(v * v, axis=-1, keepdims=True) + norm_eps)

    def norm_two(c):
        rows = slice(c * c_rows, (c + 1) * c_rows)
        branch = total[...]
        live = live_ref[rows, :]
        stat_ref[...] += jnp.sum(jnp.sum(branch * branch, axis=-1, keepdims=True) * live, axis=0, keepdims=True)
        m = stream[rows, :].astype(jnp.float32) + branch
        mid[rows, :] = m
        x[c, t] = (m * inverse_rms(m) * gain_ref[...]).astype(jnp.bfloat16)

    def first_half(c, service):
        flat = x.at[c].reshape(n * c_rows, width)
        @pl.loop(0, units // tile)
        def _(j):
            cols = pl.ds(pl.multiple_of(j * tile, tile), tile)
            gate_pre = dot32(flat[...], w_three[0, :, cols], NN)
            up_pre = dot32(flat[...], w_three[1, :, cols], NN)
            grad_hidden = dot32(cot[...], w_three[2, :, cols], NN)
            value, slope = gelu_pair(gate_pre)
            hid[:, cols] = (value * up_pre).astype(jnp.bfloat16)
            ul[:, cols] = (grad_hidden * value).astype(jnp.bfloat16)
            gl[:, cols] = (grad_hidden * up_pre * slope).astype(jnp.bfloat16)
            service(j)

    def second_half(c, service):
        flat = part.at[c].reshape(n * c_rows, width)

        @pl.loop(0, width // tile)
        def _(j):
            cols = pl.ds(pl.multiple_of(j * tile, tile), tile)
            terms = dot32(gl[...], w_three[0, cols, :], NT) + dot32(ul[...], w_three[1, cols, :], NT)
            flat[:, cols] = terms.astype(jnp.bfloat16)
            service(j)

    def branch_terms(c):
        @pl.loop(0, width // tile)
        def _(j):
            cols = pl.ds(pl.multiple_of(j * tile, tile), tile)
            terms = dot32(hid[...], w_three[2, cols, :], NT).astype(jnp.bfloat16)
            ul[:, cols] = terms

    def norm_back(c):
        rows = slice(c * c_rows, (c + 1) * c_rows)
        m = mid[rows, :]
        inv = inverse_rms(m)
        u = m * inv
        gn = total[...]
        e = gn * gain_ref[...]
        ggain_ref[...] += jnp.sum(gn * u, axis=0, keepdims=True)
        total[...] = cot_own[rows, :].astype(jnp.float32) + inv * (e - u * jnp.mean(e * u, axis=-1, keepdims=True))

    RS1, AG2, RS3 = 0, 1, 2

    def ph(kind, c):
        return kind * chunks + c

    def lands(c):
        return part.at[c], land_r.at[c], land_l.at[c]

    ggain_ref[...] = jnp.zeros_like(ggain_ref)
    stat_ref[...] = jnp.zeros_like(stat_ref)
    for c in range(chunks):
        project(c)
        line.scatter_step(ph(RS1, c), 0, *lands(c))
    loads[0].wait()
    for k in range(1, n - 1):
        line.scatter_step(ph(RS1, 0), k, *lands(0))
    for c in range(chunks):
        line.scatter_end(ph(RS1, c), *lands(c), total)
        norm_two(c)
        line.gather_step(ph(AG2, c), 0, x.at[c])
        if c + 1 < chunks:
            for k in range(1, n):
                if k < n - 1:
                    line.scatter_step(ph(RS1, c + 1), k, *lands(c + 1))
                line.gather_step(ph(AG2, c), k, x.at[c])
    cot_load.start()
    for item in weight_loads:
        item.wait()
    cot_load.wait()
    outs = {}

    def send_out(name, c, src, dst, sem):
        outs[name, c] = pltpu.make_async_copy(src, dst.at[c], out_sem.at[sem])
        outs[name, c].start()

    last = chunks - 1
    for c in range(chunks):
        cot_loads[c].wait()

        def during_first(j, c=c):
            for k in range(1, n):
                @pl.when(j == k - 1)
                def _():
                    if c == last - 1:
                        line.gather_step(ph(AG2, last), k, x.at[last])
                    if c > 0 and k < n - 1:
                        line.scatter_step(ph(RS3, c - 1), k, *lands(c - 1))

        if chunks == 1:
            for k in range(1, n):
                line.gather_step(ph(AG2, 0), k, x.at[0])
        if c > 0:
            for name in ("hid", "gl", "ul"):
                outs[name, c - 1].wait()
        first_half(c, during_first)
        if c + 1 < chunks:
            cot_loads[c + 1].start()
        send_out("x", c, x.at[c], x_out, 0)
        send_out("hid", c, hid, hid_out, 1)
        send_out("gl", c, gl, gl_out, 2)
        send_out("ulk", c, ul, ul_out, 3)
        line.scatter_sent(ph(RS1, c), *lands(c))

        def finish(c):
            rows = pl.ds(c * c_rows, c_rows)
            line.scatter_end(ph(RS3, c), *lands(c), total)
            norm_back(c)
            out = pltpu.make_async_copy(total, gmid_out.at[rows, :], out_sem.at[5])
            out.start()
            out.wait()

        second_half(c, lambda j: None)
        line.scatter_step(ph(RS3, c), 0, *lands(c))
        outs["ulk", c].wait()
        if c > 0:
            finish(c - 1)
        branch_terms(c)
        send_out("ul", c, ul, mlp_out, 4)
        outs["x", c].wait()
    for k in range(1, n - 1):
        line.scatter_step(ph(RS3, last), k, *lands(last))
    out = pltpu.make_async_copy(mid, mid_out, out_sem.at[6])
    out.start()
    finish(last)
    out.wait()
    for name in ("hid", "gl", "ul"):
        outs[name, last].wait()
    for c in range(chunks):
        line.scatter_sent(ph(RS3, c), *lands(c))
        line.gather_sent(ph(AG2, c), x.at[c])


def middle(combined, w_out, stream, cot, cot_all, gain, live, blocks, masks, halves, size, collective_id, chunks=2, tile=512):
    rows, width = stream.shape
    units = blocks[0].shape[-1]
    inner = combined.shape[1]
    c_rows = rows // chunks
    bf, f32 = jnp.bfloat16, jnp.float32
    S = jax.ShapeDtypeStruct
    any_space = pl.BlockSpec(memory_space=pl.ANY)
    vmem = pl.BlockSpec(memory_space=pltpu.VMEM)
    all_rows = (chunks, size * c_rows)
    phases = 3 * chunks
    V = pltpu.VMEM

    def body(comb, wout, st, ct, ct_all, gain_ref, live_ref, *rest):
        middle_kernel(
            len(blocks), comb, wout, st, ct, ct_all, gain_ref, *rest, live_ref,
            chunks=chunks, size=size, masks=masks, halves=halves, tile=tile,
        )

    return pl.pallas_call(
        body,
        in_specs=[any_space] * 5 + [vmem, vmem] + [any_space] * len(blocks),
        out_specs=[any_space] * 7 + [vmem, vmem],
        out_shape=[
            S((chunks, size, c_rows, width), bf),
            S(all_rows + (units,), bf), S(all_rows + (units,), bf), S(all_rows + (units,), bf),
            S(all_rows + (width,), bf),
            S((rows, width), f32), S((rows, width), f32),
            S((1, width), f32), S((1, 1), f32),
        ],
        scratch_shapes=[
            V((3, width, units), bf),
            V((chunks, size, c_rows, width), bf),
            V((size * c_rows, width), bf),
            V((size * c_rows, units), bf), V((size * c_rows, units), bf), V((size * c_rows, units), bf),
            V((chunks, size, c_rows, width), bf),
            V((chunks, size - 1, c_rows, width), bf), V((chunks, size - 1, c_rows, width), bf),
            V((rows, width), bf),
            V((rows, width), f32), V((c_rows, width), f32),
            pltpu.SemaphoreType.DMA((4 + chunks,)),
            pltpu.SemaphoreType.DMA((len(blocks),)),
            pltpu.SemaphoreType.DMA((chunks * size,)),
            pltpu.SemaphoreType.DMA((width // tile,)),
            pltpu.SemaphoreType.DMA((7,)),
            pltpu.SemaphoreType.DMA((phases, 2, size - 1)),
            pltpu.SemaphoreType.DMA((phases, 2, size - 1)),
        ],
        compiler_params=pltpu.CompilerParams(
            collective_id=collective_id, has_side_effects=True, vmem_limit_bytes=60 * 2**20
        ),
        name="middle_layer",
    )(combined.reshape(size * chunks, c_rows, inner), w_out, stream, cot, cot_all, gain, live, *blocks)


def project_kernel(stream_ref, gain_ref, *rest, masks, halves, parts, tile):
    blocks = rest[: len(masks) * halves]
    weights_out, x_ref, *outs, weights, weight_sem, out_sem = rest[len(masks) * halves :]
    f = lax.axis_index("fsdp")
    width = stream_ref.shape[1]
    half_rows = width // (len(masks) * halves)
    loads = []
    for b, block in enumerate(blocks):
        mask, half = masks[b // halves], b % halves
        owner = lax.bitwise_xor(f, mask) if mask else f
        rows = pl.ds(pl.multiple_of(owner * (half_rows * halves) + half * half_rows, half_rows), half_rows)
        loads.append(pltpu.make_async_copy(block, weights.at[:, rows, :], weight_sem.at[b]))
    for item in loads:
        item.start()
    for first in range(0, stream_ref.shape[0], tile):
        v = stream_ref[first : first + tile, :].astype(jnp.float32)
        inv = lax.rsqrt(jnp.mean(v * v, axis=-1, keepdims=True) + norm_eps)
        x_ref[first : first + tile, :] = (v * inv * gain_ref[...]).astype(jnp.bfloat16)
    for item in loads:
        item.wait()
    out = pltpu.make_async_copy(weights, weights_out, out_sem)
    out.start()
    for p in range(parts):
        outs[p][...] = dot32(x_ref[...], weights[p], NN).astype(jnp.bfloat16)
    out.wait()


def project_rows(stream_all, gain, blocks, masks, halves, parts=3, tile=256):
    length, width = stream_all.shape
    inner = blocks[0].shape[-1]
    kinds = blocks[0].shape[0]
    S = jax.ShapeDtypeStruct
    bf = jnp.bfloat16
    any_space, vmem = pl.BlockSpec(memory_space=pl.ANY), pl.BlockSpec(memory_space=pltpu.VMEM)
    return pl.pallas_call(
        functools.partial(project_kernel, masks=masks, halves=halves, parts=parts, tile=tile),
        in_specs=[vmem, vmem] + [any_space] * len(blocks),
        out_specs=[any_space] + [vmem] * (1 + parts),
        out_shape=[S((kinds, width, inner), bf), S((length, width), bf)] + [S((length, inner), bf)] * parts,
        scratch_shapes=[
            pltpu.VMEM((kinds, width, inner), bf),
            pltpu.SemaphoreType.DMA((len(blocks),)),
            pltpu.SemaphoreType.DMA,
        ],
        compiler_params=pltpu.CompilerParams(vmem_limit_bytes=48 * 2**20),
        name="project_rows",
    )(stream_all, gain, *blocks)


def contract_rows(first_mat, second_mat):
    return lax.dot_general(
        first_mat, second_mat, (((0,), (0,)), ((), ())), preferred_element_type=jnp.float32
    )


def times_transpose(first_mat, second_mat):
    return lax.dot_general(
        first_mat, second_mat, (((1,), (1,)), ((), ())), preferred_element_type=jnp.float32
    )


def exchange(own, axis, bits):
    size = lax.axis_size(axis)
    got = {0: own}
    for bit in bits:
        for mask in list(got):
            got[mask ^ bit] = lax.ppermute(got[mask], axis, [(i, i ^ bit) for i in range(size)])
    return got


def gather_blocks(stacked, axis):
    size = lax.axis_size(axis)
    ups = [1 << b for b in range(1, size.bit_length() - 1)]
    rows = stacked.shape[1] // 2
    first = exchange(stacked[:, :rows], axis, ups[::-1] + [1])
    second = exchange(stacked[:, rows:], axis, ups + [1])
    masks = sorted(first)
    return masks, [half[mask] for mask in masks for half in (first, second)]


def ring_gather(own, axis):
    size = lax.axis_size(axis)
    here = lax.axis_index(axis)
    whole = jnp.zeros((size,) + own.shape, own.dtype)
    moving = own
    for k in range(size):
        if k:
            moving = lax.ppermute(moving, axis, [(i, (i + 1) % size) for i in range(size)])
        whole = lax.dynamic_update_index_in_dim(whole, moving, lax.rem(here - k + size, size), 0)
    return whole


def halve(terms, axis, bits):
    size = lax.axis_size(axis)
    here = lax.axis_index(axis)
    left = [1 << b for b in range(size.bit_length() - 2, -1, -1)]
    for bit in bits:
        at = left.index(bit)
        mine = lax.rem(here // bit, 2)
        kept = lax.dynamic_index_in_dim(terms, mine, at, keepdims=False)
        sent = lax.dynamic_index_in_dim(terms, 1 - mine, at, keepdims=False)
        came = lax.ppermute(sent, axis, [(i, i ^ bit) for i in range(size)])
        total = kept.astype(jnp.float32) + came.astype(jnp.float32)
        left.pop(at)
        terms = total if not left else total.astype(jnp.bfloat16)
    return terms


def scatter_blocks(grad, axis):
    size = lax.axis_size(axis)
    levels = size.bit_length() - 1
    ups = [1 << b for b in range(1, levels)]
    rows = grad.shape[0] // size
    split = grad.reshape((2,) * levels + (2, rows // 2, grad.shape[1]))
    first = halve(lax.index_in_dim(split, 0, levels, keepdims=False), axis, [1] + ups)
    second = halve(lax.index_in_dim(split, 1, levels, keepdims=False), axis, [1] + ups[::-1])
    return jnp.concatenate([first, second], axis=0)


def on_device(
    stream,
    attn_gain,
    w_query,
    w_key,
    w_value,
    w_out,
    mem_gate,
    mlp_gain,
    w_gate,
    w_up,
    w_down,
    memory,
    normalizer,
    prefix,
    valid,
    cotangent,
):
    f32, bf16 = jnp.float32, jnp.bfloat16
    len_dev, width = (stream.shape[1], stream.shape[2])
    tp_size, fsdp_size = lax.axis_size("tp"), lax.axis_size("fsdp")
    tp_here, seq_here = lax.axis_index("tp"), lax.axis_index("fsdp")
    seq_len = len_dev * tp_size
    heads_here = mem_gate.shape[0]
    prefix_len = prefix[seq_here]
    valid_len = valid[seq_here]
    chunks = 2
    stream, cotangent = stream[0], cotangent[0]

    gains = lax.all_gather(jnp.stack([attn_gain, mlp_gain]), "fsdp", axis=1, tiled=True).astype(f32)
    masks, attn_blocks = gather_blocks(jnp.stack([w_query, w_key, w_value, w_out]), "fsdp")
    stream_all = ring_gather(stream, "tp").reshape(seq_len, width)
    masks, mlp_blocks = gather_blocks(jnp.stack([w_gate, w_up, w_down]), "fsdp")
    cot_all = ring_gather(cotangent, "tp")
    cot_all = (
        cot_all.reshape(tp_size, chunks, len_dev // chunks, width).swapaxes(0, 1).reshape(chunks, seq_len // chunks, width)
    )
    weights, flat_one, query_rows, key_rows, value_rows = project_rows(
        stream_all, gains[:1], attn_blocks, masks, 2
    )
    query_full, key_full, value_full, out_full = weights[0], weights[1], weights[2], weights[3]
    bounds = jnp.stack([prefix_len, valid_len])
    combined, local_mix, log_total, memory_next, normalizer_next = attend(
        bounds, query_rows, key_rows, value_rows, memory[0], normalizer[0], mem_gate
    )
    local_position = tp_here * len_dev + jnp.arange(len_dev, dtype=jnp.int32)
    live_here = (local_position < valid_len).astype(f32)[:, None]
    flat_two, hidden, gate_low, up_low, mlp_terms, middle_rows, grad_middle, gain_two_terms, branch_squares = middle(
        combined, out_full, stream, cotangent, cot_all, gains[1:], live_here, mlp_blocks, masks, 2, tp_size, 1
    )
    branch_low = ring_gather(grad_middle.astype(bf16), "tp").reshape(seq_len, width)
    mlp_branch = lax.psum_scatter(
        mlp_terms.reshape(chunks, tp_size, len_dev // chunks, width), "tp", scatter_dimension=1, tiled=True
    ).reshape(len_dev, width).astype(f32)
    result = middle_rows + mlp_branch
    stream_out = result.astype(bf16)

    def rows_of(chunked):
        return chunked.reshape(seq_len, chunked.shape[-1])

    down_grad = scatter_blocks(contract_rows(rows_of(cot_all), rows_of(hidden)).astype(bf16), "fsdp")
    gate_grad = scatter_blocks(contract_rows(rows_of(flat_two), rows_of(gate_low)).astype(bf16), "fsdp")
    up_grad = scatter_blocks(contract_rows(rows_of(flat_two), rows_of(up_low)).astype(bf16), "fsdp")

    out_grad = scatter_blocks(contract_rows(branch_low, combined).astype(bf16), "fsdp")
    grad_combined = jnp.dot(branch_low, out_full, preferred_element_type=f32)
    query_low, key_low, value_low, grad_memory, grad_normalizer, gate_parts = attend_back(
        bounds, query_rows, key_rows, value_rows, grad_combined, local_mix, log_total,
        memory[0], normalizer[0], mem_gate,
    )
    one_terms = (
        times_transpose(query_low, query_full)
        + times_transpose(key_low, key_full)
        + times_transpose(value_low, value_full)
    )
    grad_normed_one = lax.psum_scatter(one_terms.astype(bf16), "tp", scatter_dimension=0, tiled=True).astype(f32)
    query_grad = scatter_blocks(contract_rows(flat_one, query_low).astype(bf16), "fsdp")
    key_grad = scatter_blocks(contract_rows(flat_one, key_low).astype(bf16), "fsdp")
    value_grad = scatter_blocks(contract_rows(flat_one, value_low).astype(bf16), "fsdp")

    stream_f = stream.astype(f32)
    inverse = lax.rsqrt(jnp.mean(stream_f * stream_f, axis=-1, keepdims=True) + norm_eps)
    unit = stream_f * inverse
    gain_one_terms = jnp.sum(grad_normed_one * unit, axis=0)
    scaled = grad_normed_one * gains[0]
    stream_grad = grad_middle + inverse * (scaled - unit * jnp.mean(scaled * unit, axis=-1, keepdims=True))

    stats = jnp.stack(
        [jnp.sum(result * result * live_here), branch_squares[0, 0], jnp.sum(mlp_branch * mlp_branch * live_here)]
    )
    gate_terms = jnp.zeros((tp_size, heads_here), f32).at[tp_here].set(jnp.sum(gate_parts, axis=(1, 2)))
    stat_terms = jnp.zeros((fsdp_size, 3), f32).at[seq_here].set(stats)
    joined = lax.psum(
        jnp.concatenate([gain_one_terms, gain_two_terms[0], gate_terms.reshape(-1), stat_terms.reshape(-1)]),
        ("fsdp", "tp"),
    )
    shard = width // fsdp_size
    gain_one_grad = lax.dynamic_slice_in_dim(joined[:width], seq_here * shard, shard)
    gain_two_grad = lax.dynamic_slice_in_dim(joined[width : 2 * width], seq_here * shard, shard)
    gates = joined[2 * width : 2 * width + tp_size * heads_here].reshape(tp_size, heads_here)
    sums = joined[2 * width + tp_size * heads_here :].reshape(fsdp_size, 3)
    gate_grad_logit = lax.dynamic_index_in_dim(gates, tp_here, 0, keepdims=False)
    stat_sums = lax.dynamic_index_in_dim(sums, seq_here, 0)
    token_count = valid_len.astype(f32) * width
    rms_stats = jnp.sqrt(stat_sums / token_count + rms_eps)
    return (
        stream_out[None],
        stream_grad[None],
        gain_one_grad,
        query_grad,
        key_grad,
        value_grad,
        out_grad,
        gate_grad_logit,
        gain_two_grad,
        gate_grad,
        up_grad,
        down_grad,
        memory_next[None],
        normalizer_next[:, 0][None],
        grad_memory[None],
        grad_normalizer[:, 0][None],
        rms_stats,
    )


def solution(mesh):
    placed = (
        P("fsdp", "tp", None),
        P("fsdp"),
        P("fsdp", "tp"),
        P("fsdp", "tp"),
        P("fsdp", "tp"),
        P("fsdp", "tp"),
        P("tp"),
        P("fsdp"),
        P("fsdp", "tp"),
        P("fsdp", "tp"),
        P("fsdp", "tp"),
        P("fsdp", "tp", None, None),
        P("fsdp", "tp", None),
        P(),
        P(),
        P("fsdp", "tp", None),
    )
    return jax.shard_map(
        on_device,
        mesh=mesh,
        in_specs=placed,
        out_specs=(
            P("fsdp", "tp", None),
            P("fsdp", "tp", None),
            P("fsdp"),
            P("fsdp", "tp"),
            P("fsdp", "tp"),
            P("fsdp", "tp"),
            P("fsdp", "tp"),
            P("tp"),
            P("fsdp"),
            P("fsdp", "tp"),
            P("fsdp", "tp"),
            P("fsdp", "tp"),
            P("fsdp", "tp", None, None),
            P("fsdp", "tp", None),
            P("fsdp", "tp", None, None),
            P("fsdp", "tp", None),
            P("fsdp", None),
        ),
        check_vma=False,
    )
```

```python
import functools

import jax
import jax.numpy as jnp
from jax import lax
from jax.experimental import pallas as pl
from jax.experimental.pallas import tpu as pltpu
from jax.sharding import PartitionSpec as P

rms_eps = 1e-06
NEG = -1e30
LOG2E = 1.4426950408889634


def split_two(x):
    high = x.astype(jnp.bfloat16)
    return high, (x - high.astype(jnp.float32)).astype(jnp.bfloat16)


def dot32(a, b, dims):
    return lax.dot_general(a, b, (dims, ((), ())), preferred_element_type=jnp.float32)


def dot_three(a, b, dims):
    ah, al = split_two(a)
    bh, bl = split_two(b)
    return dot32(ah, bh, dims) + dot32(ah, bl, dims) + dot32(al, bh, dims)


NN, NT, TN = ((1,), (0,)), ((1,), (1,)), ((0,), (0,))


def mapped(v):
    return jnp.where(v > 0, v + 1.0, jnp.exp(jnp.minimum(v, 0.0)))


def key_reach(first, rows, keys):
    return min(keys, max(keys // 2, first + rows))


def key_limit(first, rows, prefix, valid):
    row = first + lax.broadcasted_iota(jnp.int32, (1, rows), 1)
    return jnp.minimum(valid - 1, jnp.maximum(row, prefix - 1))


def backward_kernel(bounds, q_ref, k_ref, v_ref, gc_ref, mix_ref, lse_ref, mem_ref, norm_ref, gate_ref, dq_ref, dk_ref, dv_ref, dmem_ref, dnorm_ref, dgate_ref, dk_acc, dv_acc, *, block):
    keys, hd = k_ref.shape
    prefix, valid = bounds[0], bounds[1]
    scale = hd ** -0.5
    gate = jax.nn.sigmoid(gate_ref[0])
    memory = mem_ref[0]
    norm = norm_ref[0]
    dmem = jnp.zeros((hd, hd), jnp.float32)
    dnorm = jnp.zeros((1, hd), jnp.float32)
    dgate = jnp.zeros((1, hd), jnp.float32)
    for first in range(keys - block, -1, -block):
        reach = key_reach(first, block, keys)
        rows = slice(first, first + block)
        q = q_ref[rows, :]
        gc = gc_ref[rows, :].astype(jnp.float32)
        mixed = mix_ref[rows, :]
        qm = mapped(q.astype(jnp.float32))
        inverse = 1.0 / jnp.sum(qm * norm, axis=-1, keepdims=True)
        retrieved = dot_three(qm, memory, NN) * inverse
        dgate = dgate + jnp.sum(gc * (retrieved - mixed), axis=0, keepdims=True)
        gnum = gate * gc * inverse
        gden = -jnp.sum(gnum * retrieved, axis=-1, keepdims=True)
        dmem = dmem + dot_three(qm, gnum, TN)
        dnorm = dnorm + jnp.sum(gden * qm, axis=0, keepdims=True)
        dq_mem = (dot_three(gnum, memory, NT) + gden * norm) * jnp.minimum(qm, 1.0)
        low = ((1.0 - gate) * gc).astype(jnp.bfloat16)
        delta = jnp.sum((low.astype(jnp.float32) * mixed).T, axis=0, keepdims=True)
        s = dot32(k_ref[:reach, :], q, NT) * (scale * LOG2E)
        limit = key_limit(first, block, prefix, valid)
        s = jnp.where(lax.broadcasted_iota(jnp.int32, s.shape, 0) <= limit, s - lse_ref[0, :, rows], NEG)
        p = jnp.exp2(s)
        gp = dot32(v_ref[:reach, :], low, NT)
        gs = (p * (gp - delta)).astype(jnp.bfloat16)
        dv = dot32(p.astype(jnp.bfloat16), low, NN)
        dk = dot32(gs, q, NN)
        if first == keys - block:
            dv_acc[...] = dv
            dk_acc[...] = dk
        else:
            dv_acc[:reach, :] += dv
            dk_acc[:reach, :] += dk
        dq = dot32(k_ref[:reach, :], gs, TN).T * scale
        dq_ref[rows, :] = (dq + dq_mem).astype(jnp.bfloat16)
    dk_ref[...] = (dk_acc[...] * scale).astype(jnp.bfloat16)
    dv_ref[...] = dv_acc[...].astype(jnp.bfloat16)
    dmem_ref[0] = dmem
    dnorm_ref[0] = dnorm
    dgate_ref[0] = dgate * (gate * (1.0 - gate))


def head_specs(keys, hd):
    rows = pl.BlockSpec((keys, hd), lambda h: (0, h))
    square = pl.BlockSpec((1, hd, hd), lambda h: (h, 0, 0))
    line = pl.BlockSpec((1, 1, hd), lambda h: (h, 0, 0))
    long = pl.BlockSpec((1, 1, keys), lambda h: (h, 0, 0))
    return rows, square, line, long


def attend_back(bounds, qkv, gc, mix, lse, memory, norm, gate, block=256):
    keys = qkv.shape[0]
    heads, hd = memory.shape[:2]
    rows, square, line, long = head_specs(keys, hd)
    key_rows = pl.BlockSpec((keys, hd), lambda h: (0, heads + h))
    value_rows = pl.BlockSpec((keys, hd), lambda h: (0, 2 * heads + h))
    f32 = jnp.float32
    S = jax.ShapeDtypeStruct
    low = S(gc.shape, jnp.bfloat16)
    return pl.pallas_call(
        functools.partial(backward_kernel, block=block),
        grid=(heads,),
        in_specs=[pl.BlockSpec(memory_space=pltpu.SMEM), rows, key_rows, value_rows, rows, rows, long, square, line, line],
        out_specs=[rows, rows, rows, square, line, line],
        out_shape=[low, low, low, S((heads, hd, hd), f32), S((heads, 1, hd), f32), S((heads, 1, hd), f32)],
        scratch_shapes=[pltpu.VMEM((keys, hd), f32), pltpu.VMEM((keys, hd), f32)],
        compiler_params=pltpu.CompilerParams(vmem_limit_bytes=48 * 2**20),
        name="attend_backward",
    )(bounds, qkv, qkv, qkv, gc, mix, lse, memory, norm.reshape(heads, 1, hd), jnp.broadcast_to(gate[:, None, None], (heads, 1, hd)))


norm_eps = 1e-06
MESH = pl.DeviceIdType.MESH
RIGHT, LEFT = 0, 1


class Line:
    def __init__(self, size, send_sem, recv_sem):
        self.size, self.send_sem, self.recv_sem = size, send_sem, recv_sem
        self.here = lax.axis_index("tp")

    def copy(self, phase, way, slot, src, dst):
        to = self.here + 1 if way == RIGHT else self.here - 1
        return pltpu.make_async_remote_copy(
            src_ref=src,
            dst_ref=dst,
            send_sem=self.send_sem.at[phase, way, slot],
            recv_sem=self.recv_sem.at[phase, way, slot],
            device_id={"tp": to},
            device_id_type=MESH,
        )

    def arrived(self, phase, way, slot, dst):
        self.copy(phase, way, slot, dst, dst).wait_recv()

    def scatter_step(self, phase, k, part, land_right, land_left):
        n, t = self.size, self.here
        far, near = n - 1 - k, k

        def pass_on(way, shard, land, first):
            @pl.when(jnp.logical_not(first))
            def _():
                self.arrived(phase, way, k, land)
                part[shard] = (part[shard].astype(jnp.float32) + land[...].astype(jnp.float32)).astype(part.dtype)

            self.copy(phase, way, k, part.at[shard], land).start()

        @pl.when(t < far)
        def _():
            pass_on(RIGHT, far, land_right.at[far - 1], t == 0)

        @pl.when(t > near)
        def _():
            pass_on(LEFT, near, land_left.at[near], t == n - 1)

    def scatter_end(self, phase, part, land_right, land_left, total):
        n, t = self.size, self.here
        total[...] = part[t].astype(jnp.float32)

        @pl.when(t > 0)
        def _():
            self.arrived(phase, RIGHT, n - 1 - t, land_right.at[t - 1])
            total[...] += land_right[t - 1].astype(jnp.float32)

        @pl.when(t < n - 1)
        def _():
            self.arrived(phase, LEFT, t, land_left.at[t])
            total[...] += land_left[t].astype(jnp.float32)

    def scatter_sent(self, phase, part, land_right, land_left):
        n, t = self.size, self.here
        for k in range(n - 1):
            far, near = n - 1 - k, k

            @pl.when(t < far)
            def _():
                self.copy(phase, RIGHT, k, part.at[far], land_right.at[far - 1]).wait_send()

            @pl.when(t > near)
            def _():
                self.copy(phase, LEFT, k, part.at[near], land_left.at[near]).wait_send()

    def gather_step(self, phase, k, shard_at):
        n, t = self.size, self.here

        @pl.when(t >= k)
        def _():
            shard = shard_at(t - k)
            if k > 0:
                self.arrived(phase, RIGHT, k - 1, shard)
            if k < n - 1:
                @pl.when(t < n - 1)
                def _():
                    self.copy(phase, RIGHT, k, shard, shard).start()

        @pl.when(t + k <= n - 1)
        def _():
            shard = shard_at(t + k)
            if k > 0:
                self.arrived(phase, LEFT, k - 1, shard)
            if k < n - 1:
                @pl.when(t > 0)
                def _():
                    self.copy(phase, LEFT, k, shard, shard).start()

    def gather_sent(self, phase, shard_at):
        n, t = self.size, self.here
        for k in range(n - 1):
            @pl.when((t >= k) & (t < n - 1))
            def _():
                self.copy(phase, RIGHT, k, shard_at(t - k), shard_at(t - k)).wait_send()

            @pl.when((t + k <= n - 1) & (t > 0))
            def _():
                self.copy(phase, LEFT, k, shard_at(t + k), shard_at(t + k)).wait_send()


class Cube:
    def __init__(self, size, send_sem, recv_sem):
        self.size, self.send_sem, self.recv_sem = size, send_sem, recv_sem
        self.here = lax.axis_index("fsdp")
        self.levels = size.bit_length() - 1
        ups = [1 << b for b in range(1, self.levels)]
        self.orders = [ups[::-1] + [1], ups + [1]]

    def peer(self, bit):
        return lax.bitwise_xor(self.here, bit)

    def held(self, half, stage):
        masks = [0]
        for bit in self.orders[half][:stage]:
            masks += [mask ^ bit for mask in masks]
        return masks

    def copy(self, item, half, mask, bit, block_at):
        owner = self.peer(mask) if mask else self.here
        block = block_at(owner, half)
        return pltpu.make_async_remote_copy(
            src_ref=block,
            dst_ref=block,
            send_sem=self.send_sem.at[item, half, mask ^ bit],
            recv_sem=self.recv_sem.at[item, half, mask ^ bit],
            device_id={"fsdp": self.peer(bit)},
            device_id_type=MESH,
        )

    def await_stage(self, item, stage, block_at):
        for half in range(2):
            bit = self.orders[half][stage]
            for mask in self.held(half, stage):
                block = block_at(self.peer(mask ^ bit), half)
                pltpu.make_async_remote_copy(
                    src_ref=block,
                    dst_ref=block,
                    send_sem=self.send_sem.at[item, half, mask ^ bit],
                    recv_sem=self.recv_sem.at[item, half, mask ^ bit],
                    device_id={"fsdp": self.peer(bit)},
                    device_id_type=MESH,
                ).wait_recv()

    def stage(self, item, stage, block_at):
        if stage > 0:
            self.await_stage(item, stage - 1, block_at)
        if stage == self.levels:
            return
        for half in range(2):
            bit = self.orders[half][stage]
            for mask in self.held(half, stage):
                self.copy(item, half, mask, bit, block_at).start()

    def sent(self, item, block_at):
        for stage in range(self.levels):
            for half in range(2):
                bit = self.orders[half][stage]
                for mask in self.held(half, stage):
                    self.copy(item, half, mask, bit, block_at).wait_send()


GELU_A, GELU_B = 0.7978845608028654, 0.044715


def gelu_pair(v):
    square = v * v
    curve = jnp.tanh(v * (GELU_A + GELU_A * GELU_B * square))
    half = 0.5 + 0.5 * curve
    slope = half + (0.5 * v) * (1.0 - curve * curve) * (GELU_A + 3.0 * GELU_A * GELU_B * square)
    return v * half, slope


def inverse_rms(v):
    return lax.rsqrt(jnp.mean(v * v, axis=-1, keepdims=True) + norm_eps)


def layer_kernel(
    bounds, gain_in, live_ref, mem_ref, norm_ref, gate_ref,
    stream_hbm, cot_hbm, wq_hbm, wk_hbm, wv_hbm, wo_hbm, wg_hbm, wu_hbm, wd_hbm,
    mlp_hbm, attn_out, one_out, qkv_out, comb_out, mix_out, cot_all, x_out, hid_out, gl_out, ul_out, terms_hbm,
    result_out, gmid_out, branch_out, kept_out, land,
    ggain_ref, stat_ref, lse_ref, memo_ref, normo_ref, gain,
    w_three, x, cot, hid, gl, ul, part, land_r, land_l, stream, mid, total,
    own_sem, load_sem, out_sem, term_sem, grad_sem, trade_send, trade_recv, gain_send, gain_recv, cube_send, cube_recv, line_send, line_recv,
    *, chunks, tp_size, fsdp_size, tile,
):
    n = tp_size
    bf16, f32 = jnp.bfloat16, jnp.float32
    t, f = lax.axis_index("tp"), lax.axis_index("fsdp")
    c_rows, width = x.shape[2], x.shape[3]
    units = hid.shape[1]
    rows_dev = stream.shape[0]
    length = rows_dev * n
    heads, hd = mem_ref.shape[0], mem_ref.shape[2]
    inner = heads * hd
    shard = width // fsdp_size
    line = Line(n, line_send, line_recv)
    cube = Cube(fsdp_size, cube_send, cube_recv)
    bits = [1 << b for b in range(cube.levels)]
    AG1 = 0

    def ph(kind, c):
        return 1 + kind * chunks + c

    COT, RS1, AG2, RS3, AG4, RS2 = range(6)

    attn_w = w_three.at[0]
    qkv = w_three.at[1]
    flat_one = w_three.at[2]

    def stream_at(s):
        return w_three.at[2, pl.ds(pl.multiple_of(length + s * rows_dev, rows_dev), rows_dev), :]

    def x_at(c):
        return lambda s: x.at[c, s]

    def cot_at(c):
        return lambda s: cot_all.at[c, s]

    def lands(c):
        return part.at[c], land_r.at[c], land_l.at[c]

    def block_of(item):
        whole = attn_w if item == 0 else mlp_hbm.at[item - 1]

        def at(owner, half):
            rows = shard // 2
            return whole.at[pl.ds(pl.multiple_of(owner * shard + half * rows, rows), rows), :]

        return at

    def push(item, stage):
        cube.stage(item, stage, block_of(item))

    own_rows = pl.ds(pl.multiple_of(f * shard, shard), shard)
    own = [
        pltpu.make_async_copy(w, w_three.at[0, own_rows, p * inner : (p + 1) * inner], own_sem.at[p])
        for p, w in enumerate((wq_hbm, wk_hbm, wv_hbm, wo_hbm))
    ]
    own += [pltpu.make_async_copy(stream_hbm, stream_at(t), own_sem.at[4]), pltpu.make_async_copy(stream_hbm, stream, own_sem.at[5])]
    homes = [hid.at[0:shard, :], hid.at[shard : 2 * shard, :], gl.at[0:shard, :]]
    own += [pltpu.make_async_copy(w, homes[m], own_sem.at[6 + m]) for m, w in enumerate((wg_hbm, wu_hbm, wd_hbm))]
    own.append(pltpu.make_async_copy(cot_hbm, ul.at[0:rows_dev, :], own_sem.at[9]))
    placed = [pltpu.make_async_copy(homes[m], mlp_hbm.at[m, own_rows, :], own_sem.at[6 + m]) for m in range(3)]
    placed += [
        pltpu.make_async_copy(ul.at[c * c_rows : (c + 1) * c_rows, :], cot_all.at[c, t], own_sem.at[9 + c])
        for c in range(chunks)
    ]
    for item in own:
        item.start()
    gain[...] = gain_in[...]
    ggain_ref[...] = jnp.zeros_like(ggain_ref)
    stat_ref[...] = jnp.zeros_like(stat_ref)

    barrier = pltpu.get_barrier_semaphore()

    @pl.when(t > 0)
    def _():
        pl.semaphore_signal(barrier, inc=1, device_id={"tp": t - 1}, device_id_type=MESH)

    @pl.when(t < n - 1)
    def _():
        pl.semaphore_signal(barrier, inc=1, device_id={"tp": t + 1}, device_id_type=MESH)

    for bit in bits:
        pl.semaphore_signal(barrier, inc=1, device_id={"fsdp": cube.peer(bit)}, device_id_type=MESH)
    peers = (t > 0).astype(jnp.int32) + (t < n - 1).astype(jnp.int32) + len(bits)
    pl.semaphore_wait(barrier, peers)

    for item in own[:6]:
        item.wait()
    push(0, 0)
    line.gather_step(AG1, 0, stream_at)
    for item in own[6:]:
        item.wait()
    for item in placed:
        item.start()
    for level, bit in enumerate(bits):
        trade = pltpu.make_async_remote_copy(
            src_ref=gain,
            dst_ref=total.at[8 * level : 8 * level + 8, :],
            send_sem=gain_send.at[level],
            recv_sem=gain_recv.at[level],
            device_id={"fsdp": cube.peer(bit)},
            device_id_type=MESH,
        )
        trade.start()
        trade.wait()
        gain[...] += total[8 * level : 8 * level + 8, :]
    for item in placed:
        item.wait()

    def norm_one(s):
        v = stream_at(s)[...].astype(f32)
        flat_one[pl.ds(pl.multiple_of(s * rows_dev, rows_dev), rows_dev), :] = (
            v * inverse_rms(v) * gain[0:1, :]
        ).astype(bf16)

    def project_one(s):
        rows = pl.ds(pl.multiple_of(s * rows_dev, rows_dev), rows_dev)

        @pl.loop(0, 3)
        def _(p):
            cols = pl.ds(pl.multiple_of(p * inner, inner), inner)
            qkv[rows, cols] = dot32(flat_one[rows, :], attn_w[:, cols], NN).astype(bf16)

    def arrived_pair(k, work):
        @pl.when(t >= k)
        def _():
            work(t - k)

        @pl.when(t + k <= n - 1)
        def _():
            work(t + k)

    norm_one(t)
    push(0, 1)
    push(1, 0)
    line.gather_step(AG1, 1, stream_at)
    for stage in range(2, cube.levels):
        push(0, stage)
    arrived_pair(1, norm_one)
    push(0, cube.levels)
    attn_save = pltpu.make_async_copy(attn_w, attn_out, out_sem.at[0])
    attn_save.start()
    project_one(t)
    push(1, 1)
    push(2, 0)
    line.gather_step(AG1, 2, stream_at)
    arrived_pair(1, project_one)

    def both(s):
        norm_one(s)
        project_one(s)

    for k in range(2, n):
        if k > 2:
            line.gather_step(AG1, k, stream_at)
        if k == n - 1:
            for c in range(chunks):
                line.gather_step(ph(COT, c), 0, cot_at(c))
        arrived_pair(k, both)
    one_save = pltpu.make_async_copy(flat_one.at[0:length, :], one_out, out_sem.at[1])
    one_save.start()
    qkv_save = pltpu.make_async_copy(qkv.at[0:length, 0 : 3 * inner], qkv_out, out_sem.at[2])
    qkv_save.start()
    for stage in range(2, cube.levels):
        push(1, stage)
    push(2, 1)
    push(3, 0)
    push(1, cube.levels)

    prefix, valid = bounds[0], bounds[1]
    score_scale = hd ** -0.5 * LOG2E

    def attend_rows(s):
        first = s * rows_dev
        reach = key_reach(first, rows_dev, length)
        limit = key_limit(first, rows_dev, prefix, valid)

        @pl.loop(0, heads)
        def _(h):
            def lanes(group):
                return pl.ds(pl.multiple_of(group * inner + h * hd, hd), hd)

            q = qkv[first : first + rows_dev, lanes(0)]
            scores = dot32(qkv[0:reach, lanes(1)], q, NT) * score_scale
            scores = jnp.where(lax.broadcasted_iota(jnp.int32, scores.shape, 0) <= limit, scores, NEG)
            top = jnp.max(scores, axis=0, keepdims=True)
            probs = jnp.exp2(scores - top)
            row_total = jnp.sum(probs, axis=0, keepdims=True)
            mixed = (dot32(qkv[0:reach, lanes(2)], probs.astype(bf16), TN) / row_total).T
            lse_ref[h, :, first : first + rows_dev] = top + jnp.log2(row_total)
            gate = jax.nn.sigmoid(gate_ref[h])
            qm = mapped(q.astype(f32))
            denominator = jnp.sum(qm * norm_ref[h], axis=-1, keepdims=True)
            retrieved = dot_three(qm, mem_ref[h], NN) / denominator
            mid[:, pl.ds(pl.multiple_of(s * inner + h * hd, hd), hd)] = mixed
            both_mix = (gate * retrieved + (1.0 - gate) * mixed).astype(bf16)
            for c in range(chunks):
                hid[s * c_rows : (s + 1) * c_rows, pl.ds(pl.multiple_of(c * inner + h * hd, hd), hd)] = both_mix[
                    c * c_rows : (c + 1) * c_rows
                ]

    def update_memory():
        @pl.loop(0, heads)
        def _(h):
            km = mapped(qkv[0:length, pl.ds(pl.multiple_of(inner + h * hd, hd), hd)].astype(f32))
            km = jnp.where(lax.broadcasted_iota(jnp.int32, km.shape, 0) < valid, km, 0.0)
            kh, kl = split_two(km)
            values = qkv[0:length, pl.ds(pl.multiple_of(2 * inner + h * hd, hd), hd)]
            memo_ref[h] = mem_ref[h] + dot32(kh, values, TN) + dot32(kl, values, TN)
            normo_ref[h] = norm_ref[h] + jnp.sum(km, axis=0, keepdims=True)

    for s in range(n):
        attend_rows(s)
    for stage in range(2, cube.levels):
        push(2, stage)
    comb_saves = []
    for s in range(n):
        comb_saves.append(
            pltpu.make_async_copy(mid.at[:, s * inner : (s + 1) * inner], mix_out.at[s * rows_dev : (s + 1) * rows_dev, :], out_sem.at[3 + s])
        )
        for c in range(chunks):
            comb_saves.append(
                pltpu.make_async_copy(
                    hid.at[s * c_rows : (s + 1) * c_rows, c * inner : (c + 1) * inner],
                    comb_out.at[s, c],
                    out_sem.at[3 + n + s * chunks + c],
                )
            )
    for item in comb_saves:
        item.start()

    def project(c):
        flat = part.at[c].reshape(n * c_rows, width)

        @pl.loop(0, width // tile)
        def _(j):
            cols = pl.ds(pl.multiple_of(j * tile, tile), tile)
            flat[:, cols] = dot32(
                hid[:, c * inner : (c + 1) * inner], attn_w[cols, 3 * inner : 4 * inner], NT
            ).astype(bf16)

    def norm_two(c):
        rows = slice(c * c_rows, (c + 1) * c_rows)
        branch = total[...]
        live = live_ref[rows, :]
        stat_ref[0:1, :] += jnp.sum(jnp.sum(branch * branch, axis=-1, keepdims=True) * live, axis=0, keepdims=True)
        m = stream[rows, :].astype(f32) + branch
        mid[rows, :] = m
        x[c, t] = (m * inverse_rms(m) * gain[1:2, :]).astype(bf16)

    def first_half(c, service):
        flat = x.at[c].reshape(n * c_rows, width)
        cot_flat = cot.reshape(n * c_rows, width)

        @pl.loop(0, units // tile)
        def _(j):
            cols = pl.ds(pl.multiple_of(j * tile, tile), tile)
            gate_pre = dot32(flat[...], w_three[0, :, cols], NN)
            up_pre = dot32(flat[...], w_three[1, :, cols], NN)
            grad_hidden = dot32(cot_flat[...], w_three[2, :, cols], NN)
            value, slope = gelu_pair(gate_pre)
            hid[:, cols] = (value * up_pre).astype(bf16)
            ul[:, cols] = (grad_hidden * value).astype(bf16)
            gl[:, cols] = (grad_hidden * up_pre * slope).astype(bf16)
            service(j)

    def second_half(c):
        flat = part.at[c].reshape(n * c_rows, width)

        @pl.loop(0, width // tile)
        def _(j):
            cols = pl.ds(pl.multiple_of(j * tile, tile), tile)
            terms = dot32(gl[...], w_three[0, cols, :], NT) + dot32(ul[...], w_three[1, cols, :], NT)
            flat[:, cols] = terms.astype(bf16)

    def branch_terms(c):
        @pl.loop(0, width // tile)
        def _(j):
            cols = pl.ds(pl.multiple_of(j * tile, tile), tile)
            ul[:, cols] = dot32(hid[...], w_three[2, cols, :], NT).astype(bf16)

    def norm_back(c):
        rows = slice(c * c_rows, (c + 1) * c_rows)
        m = mid[rows, :]
        inv = inverse_rms(m)
        u = m * inv
        gn = total[...]
        e = gn * gain[1:2, :]
        ggain_ref[...] += jnp.sum(gn * u, axis=0, keepdims=True)
        gm = stream[rows, :].astype(f32) + inv * (e - u * jnp.mean(e * u, axis=-1, keepdims=True))
        total[...] = gm
        x[c, t] = gm.astype(bf16)

    def scatter(kind, c, k):
        line.scatter_step(ph(kind, c), k, *lands(c))

    def gather(kind, c, k):
        line.gather_step(ph(kind, c), k, x_at(c) if kind != COT else cot_at(c))

    project(0)
    scatter(RS1, 0, 0)
    project(1)
    scatter(RS1, 1, 0)
    attn_save.wait()
    cube.sent(0, block_of(0))
    gate_load = pltpu.make_async_copy(mlp_hbm.at[0], w_three.at[0], load_sem.at[0])
    gate_load.start()
    gather(COT, 0, 1)
    gather(COT, 1, 1)
    update_memory()
    scatter(RS1, 0, 1)
    push(2, cube.levels)
    push(3, 1)
    one_save.wait()
    qkv_save.wait()
    up_load = pltpu.make_async_copy(mlp_hbm.at[1], w_three.at[1], load_sem.at[1])
    up_load.start()
    gather(COT, 0, 2)
    for k in range(2, n - 1):
        scatter(RS1, 0, k)
    for item in comb_saves:
        item.wait()
    line.scatter_end(ph(RS1, 0), *lands(0), total)
    norm_two(0)
    gather(AG2, 0, 0)
    scatter(RS1, 1, 1)
    gather(COT, 1, 2)
    for stage in range(2, cube.levels):
        push(3, stage)
    for k in range(1, n - 1):
        gather(AG2, 0, k)
        if k + 1 < n - 1:
            scatter(RS1, 1, k + 1)
    gather(COT, 0, 3)
    cot_loads = [pltpu.make_async_copy(cot_all.at[c], cot, load_sem.at[3 + c]) for c in range(chunks)]
    cot_loads[0].start()
    push(3, cube.levels)
    line.gather_sent(AG1, stream_at)
    down_load = pltpu.make_async_copy(mlp_hbm.at[2], w_three.at[2], load_sem.at[2])
    down_load.start()
    line.scatter_end(ph(RS1, 1), *lands(1), total)
    norm_two(1)
    cot_own = pltpu.make_async_copy(cot_hbm, stream, own_sem.at[5])
    cot_own.start()
    gather(AG2, 1, 0)
    gather(AG2, 0, n - 1)
    gather(COT, 1, 3)
    gate_load.wait()
    up_load.wait()
    down_load.wait()
    cot_own.wait()
    outs = {}

    def send_out(name, c, src, dst, sem):
        outs[name, c] = pltpu.make_async_copy(src, dst, out_sem.at[sem])
        outs[name, c].start()

    def save_terms(c):
        for s in range(n):
            outs[("terms", s), c] = pltpu.make_async_copy(
                ul.at[s * c_rows : (s + 1) * c_rows, :], terms_hbm.at[c, s], term_sem.at[c * n + s]
            )
            outs[("terms", s), c].start()

    def await_terms(c):
        for s in range(n):
            outs[("terms", s), c].wait()

    def rows_of(ref, c):
        return ref.at[pl.ds(c * c_rows, c_rows), :]

    def save_chunk(c):
        send_out("x", c, x.at[c], x_out.at[c], 0)
        send_out("hid", c, hid, hid_out.at[c], 1)
        send_out("gl", c, gl, gl_out.at[c], 2)
        send_out("ul", c, ul, ul_out.at[c], 3)

    def finish_back(c):
        line.scatter_end(ph(RS3, c), *lands(c), total)
        norm_back(c)
        send_out("gmid", c, total, rows_of(gmid_out, c), 5)
        gather(AG4, c, 0)
        outs["gmid", c].wait()

    def start_branch(c):
        line.scatter_sent(ph(RS3, c), *lands(c))
        load = pltpu.make_async_copy(terms_hbm.at[c], part.at[c], load_sem.at[5])
        load.start()
        load.wait()
        scatter(RS2, c, 0)

    def finish_branch(c):
        rows = slice(c * c_rows, (c + 1) * c_rows)
        line.scatter_end(ph(RS2, c), *lands(c), total)
        branch = total[...]
        result = mid[rows, :] + branch
        live = live_ref[rows, :]
        stat_ref[1:2, :] += jnp.sum(jnp.sum(result * result, axis=-1, keepdims=True) * live, axis=0, keepdims=True)
        stat_ref[2:3, :] += jnp.sum(jnp.sum(branch * branch, axis=-1, keepdims=True) * live, axis=0, keepdims=True)
        part[c, t] = result.astype(bf16)
        send_out("result", c, part.at[c, t], rows_of(result_out, c), 6)
        outs["result", c].wait()

    def during(*steps):
        def service(j):
            for at, step in enumerate(steps):
                @pl.when(j == at)
                def _():
                    step()

        return service

    half_rows = shard // 2
    flat_w = w_three.reshape(3 * width, units)
    cot_flat = cot.reshape(n * c_rows, width)
    trade_orders = [[1] + [1 << b for b in range(1, cube.levels)], [1] + [1 << b for b in range(cube.levels - 1, 0, -1)]]
    spare = width // 2
    sources = ((x_out, gl_out), (x_out, ul_out), (cot_all, hid_out))

    def grad_loads(g):
        left, right = sources[g]
        loads = [
            pltpu.make_async_copy(right.at[0], hid, grad_sem.at[0]),
            pltpu.make_async_copy(right.at[1], gl, grad_sem.at[1]),
            pltpu.make_async_copy(left.at[1], cot, grad_sem.at[2]),
        ]
        for s in range(n):
            loads.append(pltpu.make_async_copy(left.at[0, s], ul.at[s * c_rows : (s + 1) * c_rows, :], grad_sem.at[8 + s]))
        return loads

    def weight_grad(g, service=lambda j: None, wide=256):
        for item in grad_loads(g):
            item.start()
        for item in grad_loads(g):
            item.wait()
        if g > 0:
            first_trade(g - 1).wait_send()

        @pl.loop(0, width // wide)
        def _(j):
            cols = pl.ds(pl.multiple_of(j * wide, wide), wide)
            for first in range(0, units, units // 2):
                span = slice(first, first + units // 2)
                terms = dot32(ul[:, cols], hid[:, span], TN) + dot32(cot_flat[:, cols], gl[:, span], TN)
                for q in range(wide // shard):
                    mask = lax.bitwise_xor(j * (wide // shard) + q, f)
                    row = lax.rem(mask, 2) * spare + (1 - lax.rem(mask, 2)) * (g * width) + (mask // 2) * shard
                    flat_w[pl.ds(pl.multiple_of(row, shard), shard), span] = terms[q * shard : (q + 1) * shard].astype(bf16)
            service(j)

        first_trade(g).start()

    def first_trade(g):
        return pltpu.make_async_remote_copy(
            src_ref=flat_w.at[spare : 2 * spare, :],
            dst_ref=land.at[g, 0],
            send_sem=trade_send.at[g, 0, 0, 0],
            recv_sem=trade_recv.at[g, 0, 0, 0],
            device_id={"fsdp": cube.peer(1)},
            device_id_type=MESH,
        )

    def trades(g, i):
        for half in range(2):
            order = trade_orders[half]
            bit = order[i]
            for mask in range(fsdp_size):
                if all(mask & b == 0 for b in order[: i + 1]):
                    there = pl.ds((mask // 2) * shard + half * half_rows, half_rows)
                    here = pl.ds(g * width + ((mask ^ bit) // 2) * shard + half * half_rows, half_rows)
                    yield mask, half, pltpu.make_async_remote_copy(
                        src_ref=flat_w.at[here, :],
                        dst_ref=land.at[g, i, there, :],
                        send_sem=trade_send.at[g, i, half, mask // 2],
                        recv_sem=trade_recv.at[g, i, half, mask // 2],
                        device_id={"fsdp": cube.peer(bit)},
                        device_id_type=MESH,
                    )

    def trade_start(g, i):
        for _, _, item in trades(g, i):
            item.start()

    def add_first(g):
        first_trade(g).wait_recv()
        load = pltpu.make_async_copy(land.at[g, 0], flat_w.at[width + spare : width + 2 * spare, :], grad_sem.at[3])
        load.start()
        load.wait()

        @pl.loop(0, spare // half_rows)
        def _(r):
            mine = pl.ds(pl.multiple_of(g * width + r * half_rows, half_rows), half_rows)
            came = pl.ds(pl.multiple_of(width + spare + r * half_rows, half_rows), half_rows)
            flat_w[mine, :] = (flat_w[mine, :].astype(f32) + flat_w[came, :].astype(f32)).astype(bf16)

        trade_start(g, 1)

    def add_next(g, i):
        places = []
        for mask, half, item in trades(g, i):
            item.wait_recv()
            places.append((mask // 2) * shard + half * half_rows)
        loads = [
            pltpu.make_async_copy(
                land.at[g, i, place : place + half_rows, :],
                flat_w.at[2 * width + spare + place : 2 * width + spare + place + half_rows, :],
                grad_sem.at[4 + at % 4],
            )
            for at, place in enumerate(places)
        ]
        for base in range(0, len(loads), 4):
            for item in loads[base : base + 4]:
                item.start()
            for item in loads[base : base + 4]:
                item.wait()
        for place in places:
            mine = slice(g * width + place, g * width + place + half_rows)
            came = slice(2 * width + spare + place, 2 * width + spare + place + half_rows)
            flat_w[mine, :] = (flat_w[mine, :].astype(f32) + flat_w[came, :].astype(f32)).astype(bf16)
        trade_start(g, i + 1)
        if i + 1 == cube.levels - 1:
            send_out("kept", g, flat_w.at[g * width : g * width + shard, :], kept_out.at[g], 8 + g)

    def trade_end(g):
        for _, _, item in trades(g, cube.levels - 1):
            item.wait_recv()
        outs["kept", g].wait()

    def trade_sent(g):
        for i in range(1, cube.levels):
            for _, _, item in trades(g, i):
                item.wait_send()

    cot_loads[0].wait()
    first_half(0, during(*[functools.partial(gather, AG2, 1, k) for k in range(1, n)]))
    cot_loads[1].start()
    save_chunk(0)
    line.scatter_sent(ph(RS1, 0), *lands(0))
    second_half(0)
    line.gather_sent(ph(AG2, 0), x_at(0))
    outs["x", 0].wait()
    outs["ul", 0].wait()
    scatter(RS3, 0, 0)
    branch_terms(0)
    save_terms(0)
    outs["hid", 0].wait()
    outs["gl", 0].wait()
    await_terms(0)
    cot_loads[1].wait()
    first_half(1, during(lambda: None, *[functools.partial(scatter, RS3, 0, k) for k in range(1, n - 1)]))
    save_chunk(1)
    line.scatter_sent(ph(RS1, 1), *lands(1))
    second_half(1)
    line.gather_sent(ph(AG2, 1), x_at(1))
    outs["x", 1].wait()
    outs["ul", 1].wait()
    scatter(RS3, 1, 0)
    finish_back(0)
    branch_terms(1)
    save_terms(1)
    outs["hid", 1].wait()
    outs["gl", 1].wait()
    for item in range(1, 4):
        cube.sent(item, block_of(item))
    scatter(RS3, 1, 1)
    gather(AG4, 0, 1)
    start_branch(0)
    await_terms(1)

    def skip():
        pass

    def z_one():
        for k in range(2, n - 1):
            scatter(RS3, 1, k)
        gather(AG4, 0, 2)

    weight_grad(0, during(*[skip] * 6, z_one))
    scatter(RS2, 0, 1)
    weight_grad(1)
    finish_back(1)
    for k in range(3, n):
        gather(AG4, 0, k)
    send_out("branch", 0, x.at[0], branch_out.at[:, 0], 0)
    for k in range(2, n - 1):
        scatter(RS2, 0, k)
    add_first(0)
    gather(AG4, 1, 1)
    start_branch(1)
    weight_grad(2)
    finish_branch(0)
    gather(AG4, 1, 2)
    scatter(RS2, 1, 1)
    add_first(1)
    for i in range(1, cube.levels - 1):
        add_next(0, i)
    for k in range(3, n):
        gather(AG4, 1, k)
    send_out("branch", 1, x.at[1], branch_out.at[:, 1], 7)
    for k in range(2, n - 1):
        scatter(RS2, 1, k)
    add_first(2)
    finish_branch(1)
    for g in (1, 2):
        for i in range(1, cube.levels - 1):
            add_next(g, i)
    for g in range(3):
        trade_end(g)
        trade_sent(g)
    first_trade(2).wait_send()
    for c in range(chunks):
        outs["branch", c].wait()
    for c in range(chunks):
        line.gather_sent(ph(COT, c), cot_at(c))
        line.gather_sent(ph(AG4, c), x_at(c))
        line.scatter_sent(ph(RS2, c), *lands(c))


def whole_layer(bounds, gains, live, memory, norm, gate, stream, cot, attn_weights, mlp_weights, tp_size, fsdp_size, collective_id, tile=512):
    chunks = 2
    rows, width = stream.shape
    inner = attn_weights[0].shape[1]
    units = mlp_weights[0].shape[1]
    heads, hd = memory.shape[:2]
    length = rows * tp_size
    c_rows = rows // chunks
    bf, f32 = jnp.bfloat16, jnp.float32
    S = jax.ShapeDtypeStruct
    any_space = pl.BlockSpec(memory_space=pl.ANY)
    vmem = pl.BlockSpec(memory_space=pltpu.VMEM)
    smem = pl.BlockSpec(memory_space=pltpu.SMEM)
    grid_rows = (chunks, tp_size, c_rows)
    flat_rows = (chunks, tp_size * c_rows)
    levels = fsdp_size.bit_length() - 1
    V, DMA = pltpu.VMEM, pltpu.SemaphoreType.DMA
    return pl.pallas_call(
        functools.partial(layer_kernel, chunks=chunks, tp_size=tp_size, fsdp_size=fsdp_size, tile=tile),
        in_specs=[smem] + [vmem] * 5 + [any_space] * 9,
        out_specs=[any_space] * 17 + [vmem] * 6,
        out_shape=[
            S((3, width, units), bf),
            S((width, 4 * inner), bf),
            S((length, width), bf),
            S((length, 3 * inner), bf),
            S((tp_size, chunks, c_rows, inner), bf),
            S((length, inner), f32),
            S(grid_rows + (width,), bf),
            S(grid_rows + (width,), bf),
            S(flat_rows + (units,), bf), S(flat_rows + (units,), bf), S(flat_rows + (units,), bf),
            S(grid_rows + (width,), bf),
            S((rows, width), bf),
            S((rows, width), f32),
            S((tp_size, chunks, c_rows, width), bf),
            S((3, width // fsdp_size, units), bf),
            S((3, levels, width // 2, units), bf),
            S((1, width), f32), S((8, 128), f32), S((heads, 1, length), f32), S((heads, hd, hd), f32), S((heads, 1, hd), f32), S((8, width), f32),
        ],
        scratch_shapes=[
            V((3, width, units), bf),
            V(grid_rows + (width,), bf),
            V((tp_size, c_rows, width), bf),
            V(flat_rows[1:] + (units,), bf), V(flat_rows[1:] + (units,), bf), V(flat_rows[1:] + (units,), bf),
            V(grid_rows + (width,), bf),
            V((chunks, tp_size - 1, c_rows, width), bf), V((chunks, tp_size - 1, c_rows, width), bf),
            V((rows, width), bf),
            V((rows, width), f32), V((c_rows, width), f32),
            DMA((9 + chunks,)), DMA((6,)), DMA((3 + tp_size + tp_size * chunks,)),
            DMA((2 * tp_size,)), DMA((8 + tp_size,)),
            DMA((3, levels, 2, fsdp_size // 2)), DMA((3, levels, 2, fsdp_size // 2)),
            DMA((levels,)), DMA((levels,)),
            DMA((4, 2, fsdp_size)), DMA((4, 2, fsdp_size)),
            DMA((1 + 6 * chunks, 2, tp_size - 1)), DMA((1 + 6 * chunks, 2, tp_size - 1)),
        ],
        compiler_params=pltpu.CompilerParams(
            collective_id=collective_id, has_side_effects=True, vmem_limit_bytes=60 * 2**20
        ),
        name="layer_kernel",
    )(
        bounds, gains, live, memory, norm.reshape(heads, 1, hd), jnp.broadcast_to(gate[:, None, None], (heads, 1, hd)),
        stream, cot, *attn_weights, *mlp_weights,
    )


def contract_rows(first_mat, second_mat):
    return lax.dot_general(
        first_mat, second_mat, (((0,), (0,)), ((), ())), preferred_element_type=jnp.float32
    )


def times_transpose(first_mat, second_mat):
    return lax.dot_general(
        first_mat, second_mat, (((1,), (1,)), ((), ())), preferred_element_type=jnp.float32
    )


def halve(terms, axis, bits):
    size = lax.axis_size(axis)
    here = lax.axis_index(axis)
    left = [1 << b for b in range(size.bit_length() - 2, -1, -1)]
    for bit in bits:
        at = left.index(bit)
        mine = lax.rem(here // bit, 2)
        kept = lax.dynamic_index_in_dim(terms, mine, at, keepdims=False)
        sent = lax.dynamic_index_in_dim(terms, 1 - mine, at, keepdims=False)
        came = lax.ppermute(sent, axis, [(i, i ^ bit) for i in range(size)])
        total = kept.astype(jnp.float32) + came.astype(jnp.float32)
        left.pop(at)
        terms = total if not left else total.astype(jnp.bfloat16)
    return terms


def scatter_blocks(grad, axis):
    size = lax.axis_size(axis)
    levels = size.bit_length() - 1
    ups = [1 << b for b in range(1, levels)]
    rows = grad.shape[0] // size
    split = grad.reshape((2,) * levels + (2, rows // 2, grad.shape[1]))
    first = halve(lax.index_in_dim(split, 0, levels, keepdims=False), axis, [1] + ups)
    second = halve(lax.index_in_dim(split, 1, levels, keepdims=False), axis, [1] + ups[::-1])
    return jnp.concatenate([first, second], axis=0)


def on_device(
    stream,
    attn_gain,
    w_query,
    w_key,
    w_value,
    w_out,
    mem_gate,
    mlp_gain,
    w_gate,
    w_up,
    w_down,
    memory,
    normalizer,
    prefix,
    valid,
    cotangent,
):
    f32, bf16 = jnp.float32, jnp.bfloat16
    len_dev, width = (stream.shape[1], stream.shape[2])
    tp_size, fsdp_size = lax.axis_size("tp"), lax.axis_size("fsdp")
    tp_here, seq_here = lax.axis_index("tp"), lax.axis_index("fsdp")
    seq_len = len_dev * tp_size
    heads_here = mem_gate.shape[0]
    prefix_len = prefix[seq_here]
    valid_len = valid[seq_here]
    stream, cotangent = stream[0], cotangent[0]

    shard = width // fsdp_size
    gains = jnp.zeros((8, width), f32)
    gains = lax.dynamic_update_slice(
        gains, jnp.stack([attn_gain, mlp_gain]).astype(f32), (0, seq_here * shard)
    )
    bounds = jnp.stack([prefix_len, valid_len])
    local_position = tp_here * len_dev + jnp.arange(len_dev, dtype=jnp.int32)
    live_here = (local_position < valid_len).astype(f32)[:, None]
    (
        _, attn_full, flat_one, qkv_rows, combined, local_mix, _, _, _, _, _, _,
        stream_out, grad_middle, branch_low, kept, landed, gain_two_terms, stats, log_total, memory_next, normalizer_next, gains,
    ) = whole_layer(
        bounds, gains, live_here, memory[0], normalizer[0], mem_gate, stream, cotangent,
        (w_query, w_key, w_value, w_out), (w_gate, w_up, w_down), tp_size, fsdp_size, 1,
    )
    inner = w_query.shape[1]
    combined = combined.reshape(seq_len, inner)
    branch_low = branch_low.reshape(seq_len, width)
    query_full, key_full, value_full, out_full = (attn_full[:, p * inner : (p + 1) * inner] for p in range(4))

    gate_grad, up_grad, down_grad = (
        kept[g].astype(f32) + landed[g, -1, :shard].astype(f32) for g in range(3)
    )
    out_grad = scatter_blocks(contract_rows(branch_low, combined).astype(bf16), "fsdp")
    grad_combined = jnp.dot(branch_low, out_full, preferred_element_type=f32)
    query_low, key_low, value_low, grad_memory, grad_normalizer, gate_parts = attend_back(
        bounds, qkv_rows, grad_combined, local_mix, log_total,
        memory[0], normalizer[0], mem_gate,
    )
    one_terms = (
        times_transpose(query_low, query_full)
        + times_transpose(key_low, key_full)
        + times_transpose(value_low, value_full)
    )
    grad_normed_one = lax.psum_scatter(one_terms.astype(bf16), "tp", scatter_dimension=0, tiled=True).astype(f32)
    query_grad = scatter_blocks(contract_rows(flat_one, query_low).astype(bf16), "fsdp")
    key_grad = scatter_blocks(contract_rows(flat_one, key_low).astype(bf16), "fsdp")
    value_grad = scatter_blocks(contract_rows(flat_one, value_low).astype(bf16), "fsdp")

    stream_f = stream.astype(f32)
    inverse = lax.rsqrt(jnp.mean(stream_f * stream_f, axis=-1, keepdims=True) + norm_eps)
    unit = stream_f * inverse
    gain_one_terms = jnp.sum(grad_normed_one * unit, axis=0)
    scaled = grad_normed_one * gains[0]
    stream_grad = grad_middle + inverse * (scaled - unit * jnp.mean(scaled * unit, axis=-1, keepdims=True))

    gate_terms = jnp.zeros((tp_size, heads_here), f32).at[tp_here].set(jnp.sum(gate_parts, axis=(1, 2)))
    stat_terms = jnp.zeros((fsdp_size, 3), f32).at[seq_here].set(jnp.stack([stats[1, 0], stats[0, 0], stats[2, 0]]))
    joined = lax.psum(
        jnp.concatenate([gain_one_terms, gain_two_terms[0], gate_terms.reshape(-1), stat_terms.reshape(-1)]),
        ("fsdp", "tp"),
    )
    gain_one_grad = lax.dynamic_slice_in_dim(joined[:width], seq_here * shard, shard)
    gain_two_grad = lax.dynamic_slice_in_dim(joined[width : 2 * width], seq_here * shard, shard)
    gates = joined[2 * width : 2 * width + tp_size * heads_here].reshape(tp_size, heads_here)
    sums = joined[2 * width + tp_size * heads_here :].reshape(fsdp_size, 3)
    gate_grad_logit = lax.dynamic_index_in_dim(gates, tp_here, 0, keepdims=False)
    stat_sums = lax.dynamic_index_in_dim(sums, seq_here, 0)
    token_count = valid_len.astype(f32) * width
    rms_stats = jnp.sqrt(stat_sums / token_count + rms_eps)
    return (
        stream_out[None],
        stream_grad[None],
        gain_one_grad,
        query_grad,
        key_grad,
        value_grad,
        out_grad,
        gate_grad_logit,
        gain_two_grad,
        gate_grad,
        up_grad,
        down_grad,
        memory_next[None],
        normalizer_next[:, 0][None],
        grad_memory[None],
        grad_normalizer[:, 0][None],
        rms_stats,
    )


def solution(mesh):
    placed = (
        P("fsdp", "tp", None),
        P("fsdp"),
        P("fsdp", "tp"),
        P("fsdp", "tp"),
        P("fsdp", "tp"),
        P("fsdp", "tp"),
        P("tp"),
        P("fsdp"),
        P("fsdp", "tp"),
        P("fsdp", "tp"),
        P("fsdp", "tp"),
        P("fsdp", "tp", None, None),
        P("fsdp", "tp", None),
        P(),
        P(),
        P("fsdp", "tp", None),
    )
    return jax.shard_map(
        on_device,
        mesh=mesh,
        in_specs=placed,
        out_specs=(
            P("fsdp", "tp", None),
            P("fsdp", "tp", None),
            P("fsdp"),
            P("fsdp", "tp"),
            P("fsdp", "tp"),
            P("fsdp", "tp"),
            P("fsdp", "tp"),
            P("tp"),
            P("fsdp"),
            P("fsdp", "tp"),
            P("fsdp", "tp"),
            P("fsdp", "tp"),
            P("fsdp", "tp", None, None),
            P("fsdp", "tp", None),
            P("fsdp", "tp", None, None),
            P("fsdp", "tp", None),
            P("fsdp", None),
        ),
        check_vma=False,
    )
```

```python
import functools

import jax
import jax.numpy as jnp
from jax import lax
from jax.experimental import pallas as pl
from jax.experimental.pallas import tpu as pltpu
from jax.sharding import PartitionSpec as P

rms_eps = 1e-06
NEG = -1e30
LOG2E = 1.4426950408889634


def split_two(x):
    high = x.astype(jnp.bfloat16)
    return high, (x - high.astype(jnp.float32)).astype(jnp.bfloat16)


def dot32(a, b, dims):
    return lax.dot_general(a, b, (dims, ((), ())), preferred_element_type=jnp.float32)


def dot_three(a, b, dims):
    ah, al = split_two(a)
    bh, bl = split_two(b)
    return dot32(ah, bh, dims) + dot32(ah, bl, dims) + dot32(al, bh, dims)


NN, NT, TN = ((1,), (0,)), ((1,), (1,)), ((0,), (0,))


def mapped(v):
    return jnp.where(v > 0, v + 1.0, jnp.exp(jnp.minimum(v, 0.0)))


def key_reach(first, rows, keys):
    return min(keys, max(keys // 2, first + rows))


def key_limit(first, rows, prefix, valid):
    row = first + lax.broadcasted_iota(jnp.int32, (1, rows), 1)
    return jnp.minimum(valid - 1, jnp.maximum(row, prefix - 1))


norm_eps = 1e-06
MESH = pl.DeviceIdType.MESH
RIGHT, LEFT = 0, 1


class Line:
    def __init__(self, size, send_sem, recv_sem):
        self.size, self.send_sem, self.recv_sem = size, send_sem, recv_sem
        self.here = lax.axis_index("tp")

    def copy(self, phase, way, slot, src, dst):
        to = self.here + 1 if way == RIGHT else self.here - 1
        return pltpu.make_async_remote_copy(
            src_ref=src,
            dst_ref=dst,
            send_sem=self.send_sem.at[phase, way, slot],
            recv_sem=self.recv_sem.at[phase, way, slot],
            device_id={"tp": to},
            device_id_type=MESH,
        )

    def arrived(self, phase, way, slot, dst):
        self.copy(phase, way, slot, dst, dst).wait_recv()

    def scatter_step(self, phase, k, part, land_right, land_left):
        n, t = self.size, self.here
        far, near = n - 1 - k, k

        def pass_on(way, shard, land, first):
            @pl.when(jnp.logical_not(first))
            def _():
                self.arrived(phase, way, k, land)
                part[shard] = (part[shard].astype(jnp.float32) + land[...].astype(jnp.float32)).astype(part.dtype)

            self.copy(phase, way, k, part.at[shard], land).start()

        @pl.when(t < far)
        def _():
            pass_on(RIGHT, far, land_right.at[far - 1], t == 0)

        @pl.when(t > near)
        def _():
            pass_on(LEFT, near, land_left.at[near], t == n - 1)

    def scatter_end(self, phase, part, land_right, land_left, total):
        n, t = self.size, self.here
        total[...] = part[t].astype(jnp.float32)

        @pl.when(t > 0)
        def _():
            self.arrived(phase, RIGHT, n - 1 - t, land_right.at[t - 1])
            total[...] += land_right[t - 1].astype(jnp.float32)

        @pl.when(t < n - 1)
        def _():
            self.arrived(phase, LEFT, t, land_left.at[t])
            total[...] += land_left[t].astype(jnp.float32)

    def scatter_sent(self, phase, part, land_right, land_left):
        n, t = self.size, self.here
        for k in range(n - 1):
            far, near = n - 1 - k, k

            @pl.when(t < far)
            def _():
                self.copy(phase, RIGHT, k, part.at[far], land_right.at[far - 1]).wait_send()

            @pl.when(t > near)
            def _():
                self.copy(phase, LEFT, k, part.at[near], land_left.at[near]).wait_send()

    def gather_step(self, phase, k, shard_at):
        n, t = self.size, self.here

        @pl.when(t >= k)
        def _():
            shard = shard_at(t - k)
            if k > 0:
                self.arrived(phase, RIGHT, k - 1, shard)
            if k < n - 1:
                @pl.when(t < n - 1)
                def _():
                    self.copy(phase, RIGHT, k, shard, shard).start()

        @pl.when(t + k <= n - 1)
        def _():
            shard = shard_at(t + k)
            if k > 0:
                self.arrived(phase, LEFT, k - 1, shard)
            if k < n - 1:
                @pl.when(t > 0)
                def _():
                    self.copy(phase, LEFT, k, shard, shard).start()

    def gather_sent(self, phase, shard_at):
        n, t = self.size, self.here
        for k in range(n - 1):
            @pl.when((t >= k) & (t < n - 1))
            def _():
                self.copy(phase, RIGHT, k, shard_at(t - k), shard_at(t - k)).wait_send()

            @pl.when((t + k <= n - 1) & (t > 0))
            def _():
                self.copy(phase, LEFT, k, shard_at(t + k), shard_at(t + k)).wait_send()


class Cube:
    def __init__(self, size, send_sem, recv_sem):
        self.size, self.send_sem, self.recv_sem = size, send_sem, recv_sem
        self.here = lax.axis_index("fsdp")
        self.levels = size.bit_length() - 1
        ups = [1 << b for b in range(1, self.levels)]
        self.orders = [ups[::-1] + [1], ups + [1]]

    def peer(self, bit):
        return lax.bitwise_xor(self.here, bit)

    def held(self, half, stage):
        masks = [0]
        for bit in self.orders[half][:stage]:
            masks += [mask ^ bit for mask in masks]
        return masks

    def copy(self, item, half, mask, bit, block_at):
        owner = self.peer(mask) if mask else self.here
        block = block_at(owner, half)
        return pltpu.make_async_remote_copy(
            src_ref=block,
            dst_ref=block,
            send_sem=self.send_sem.at[item, half, mask ^ bit],
            recv_sem=self.recv_sem.at[item, half, mask ^ bit],
            device_id={"fsdp": self.peer(bit)},
            device_id_type=MESH,
        )

    def await_stage(self, item, stage, block_at):
        for half in range(2):
            bit = self.orders[half][stage]
            for mask in self.held(half, stage):
                block = block_at(self.peer(mask ^ bit), half)
                pltpu.make_async_remote_copy(
                    src_ref=block,
                    dst_ref=block,
                    send_sem=self.send_sem.at[item, half, mask ^ bit],
                    recv_sem=self.recv_sem.at[item, half, mask ^ bit],
                    device_id={"fsdp": self.peer(bit)},
                    device_id_type=MESH,
                ).wait_recv()

    def stage(self, item, stage, block_at):
        if stage > 0:
            self.await_stage(item, stage - 1, block_at)
        if stage == self.levels:
            return
        for half in range(2):
            bit = self.orders[half][stage]
            for mask in self.held(half, stage):
                self.copy(item, half, mask, bit, block_at).start()

    def sent(self, item, block_at):
        for stage in range(self.levels):
            for half in range(2):
                bit = self.orders[half][stage]
                for mask in self.held(half, stage):
                    self.copy(item, half, mask, bit, block_at).wait_send()


GELU_A, GELU_B = 0.7978845608028654, 0.044715


def gelu_pair(v):
    square = v * v
    curve = jnp.tanh(v * (GELU_A + GELU_A * GELU_B * square))
    half = 0.5 + 0.5 * curve
    slope = half + (0.5 * v) * (1.0 - curve * curve) * (GELU_A + 3.0 * GELU_A * GELU_B * square)
    return v * half, slope


def inverse_rms(v):
    return lax.rsqrt(jnp.mean(v * v, axis=-1, keepdims=True) + norm_eps)


def layer_kernel(
    bounds, gain_in, live_ref, mem_ref, norm_ref, gate_ref,
    stream_hbm, cot_hbm, wq_hbm, wk_hbm, wv_hbm, wo_hbm, wg_hbm, wu_hbm, wd_hbm,
    mlp_hbm, attn_out, one_out, qkv_out, comb_out, mix_out, cot_all, x_out, hid_out, gl_out, ul_out, terms_hbm,
    result_out, gmid_out, branch_out, kept_out, land, all_out, mid_out, to_send,
    ggain_ref, stat_ref, lse_ref, memo_ref, normo_ref, gain,
    w_three, x, cot, hid, gl, ul, part, land_r, land_l, stream, mid, total,
    own_sem, load_sem, out_sem, term_sem, grad_sem, trade_send, trade_recv, gain_send, gain_recv, cube_send, cube_recv, line_send, line_recv,
    *, chunks, tp_size, fsdp_size, tile,
):
    n = tp_size
    bf16, f32 = jnp.bfloat16, jnp.float32
    t, f = lax.axis_index("tp"), lax.axis_index("fsdp")
    c_rows, width = x.shape[2], x.shape[3]
    units = hid.shape[1]
    rows_dev = stream.shape[0]
    length = rows_dev * n
    heads, hd = mem_ref.shape[0], mem_ref.shape[2]
    inner = heads * hd
    shard = width // fsdp_size
    line = Line(n, line_send, line_recv)
    cube = Cube(fsdp_size, cube_send, cube_recv)
    bits = [1 << b for b in range(cube.levels)]
    AG1 = 0

    def ph(kind, c):
        return 1 + kind * chunks + c

    COT, RS1, AG2, RS3, AG4, RS2 = range(6)

    attn_w = w_three.at[0]
    qkv = w_three.at[1]
    flat_one = w_three.at[2]

    def stream_at(s):
        return w_three.at[2, pl.ds(pl.multiple_of(length + s * rows_dev, rows_dev), rows_dev), :]

    def x_at(c):
        return lambda s: x.at[c, s]

    def cot_at(c):
        return lambda s: cot_all.at[c, s]

    def lands(c):
        return part.at[c], land_r.at[c], land_l.at[c]

    def block_of(item):
        whole = attn_w if item == 0 else mlp_hbm.at[item - 1]

        def at(owner, half):
            rows = shard // 2
            return whole.at[pl.ds(pl.multiple_of(owner * shard + half * rows, rows), rows), :]

        return at

    def push(item, stage):
        cube.stage(item, stage, block_of(item))

    own_rows = pl.ds(pl.multiple_of(f * shard, shard), shard)
    own = [
        pltpu.make_async_copy(w, w_three.at[0, own_rows, p * inner : (p + 1) * inner], own_sem.at[p])
        for p, w in enumerate((wq_hbm, wk_hbm, wv_hbm, wo_hbm))
    ]
    own += [pltpu.make_async_copy(stream_hbm, stream_at(t), own_sem.at[4]), pltpu.make_async_copy(stream_hbm, stream, own_sem.at[5])]
    homes = [hid.at[0:shard, :], hid.at[shard : 2 * shard, :], gl.at[0:shard, :]]
    own += [pltpu.make_async_copy(w, homes[m], own_sem.at[6 + m]) for m, w in enumerate((wg_hbm, wu_hbm, wd_hbm))]
    own.append(pltpu.make_async_copy(cot_hbm, ul.at[0:rows_dev, :], own_sem.at[9]))
    placed = [pltpu.make_async_copy(homes[m], mlp_hbm.at[m, own_rows, :], own_sem.at[6 + m]) for m in range(3)]
    placed += [
        pltpu.make_async_copy(ul.at[c * c_rows : (c + 1) * c_rows, :], cot_all.at[c, t], own_sem.at[9 + c])
        for c in range(chunks)
    ]
    for item in own:
        item.start()
    gain[...] = gain_in[...]
    ggain_ref[...] = jnp.zeros_like(ggain_ref)
    stat_ref[...] = jnp.zeros_like(stat_ref)

    barrier = pltpu.get_barrier_semaphore()

    @pl.when(t > 0)
    def _():
        pl.semaphore_signal(barrier, inc=1, device_id={"tp": t - 1}, device_id_type=MESH)

    @pl.when(t < n - 1)
    def _():
        pl.semaphore_signal(barrier, inc=1, device_id={"tp": t + 1}, device_id_type=MESH)

    for bit in bits:
        pl.semaphore_signal(barrier, inc=1, device_id={"fsdp": cube.peer(bit)}, device_id_type=MESH)
    peers = (t > 0).astype(jnp.int32) + (t < n - 1).astype(jnp.int32) + len(bits)
    pl.semaphore_wait(barrier, peers)

    for item in own[:6]:
        item.wait()
    push(0, 0)
    line.gather_step(AG1, 0, stream_at)
    for item in own[6:]:
        item.wait()
    for item in placed:
        item.start()
    for level, bit in enumerate(bits):
        trade = pltpu.make_async_remote_copy(
            src_ref=gain,
            dst_ref=total.at[8 * level : 8 * level + 8, :],
            send_sem=gain_send.at[level],
            recv_sem=gain_recv.at[level],
            device_id={"fsdp": cube.peer(bit)},
            device_id_type=MESH,
        )
        trade.start()
        trade.wait()
        gain[...] += total[8 * level : 8 * level + 8, :]
    for item in placed:
        item.wait()

    def norm_one(s):
        v = stream_at(s)[...].astype(f32)
        flat_one[pl.ds(pl.multiple_of(s * rows_dev, rows_dev), rows_dev), :] = (
            v * inverse_rms(v) * gain[0:1, :]
        ).astype(bf16)

    def project_one(s):
        rows = pl.ds(pl.multiple_of(s * rows_dev, rows_dev), rows_dev)

        @pl.loop(0, 3)
        def _(p):
            cols = pl.ds(pl.multiple_of(p * inner, inner), inner)
            qkv[rows, cols] = dot32(flat_one[rows, :], attn_w[:, cols], NN).astype(bf16)

    def arrived_pair(k, work):
        @pl.when(t >= k)
        def _():
            work(t - k)

        @pl.when(t + k <= n - 1)
        def _():
            work(t + k)

    norm_one(t)
    push(0, 1)
    push(1, 0)
    line.gather_step(AG1, 1, stream_at)
    for stage in range(2, cube.levels):
        push(0, stage)
    arrived_pair(1, norm_one)
    push(0, cube.levels)
    attn_save = pltpu.make_async_copy(attn_w, attn_out, out_sem.at[0])
    attn_save.start()
    project_one(t)
    push(1, 1)
    push(2, 0)
    line.gather_step(AG1, 2, stream_at)
    arrived_pair(1, project_one)

    def both(s):
        norm_one(s)
        project_one(s)

    for k in range(2, n):
        if k > 2:
            line.gather_step(AG1, k, stream_at)
        if k == n - 1:
            for c in range(chunks):
                line.gather_step(ph(COT, c), 0, cot_at(c))
        arrived_pair(k, both)
    one_save = pltpu.make_async_copy(flat_one.at[0:length, :], one_out, out_sem.at[1])
    one_save.start()
    all_save = pltpu.make_async_copy(flat_one.at[length : 2 * length, :], all_out, own_sem.at[4])
    all_save.start()
    qkv_save = pltpu.make_async_copy(qkv.at[0:length, 0 : 3 * inner], qkv_out, out_sem.at[2])
    qkv_save.start()
    for stage in range(2, cube.levels):
        push(1, stage)
    push(2, 1)
    push(3, 0)
    push(1, cube.levels)

    prefix, valid = bounds[0], bounds[1]
    score_scale = hd ** -0.5 * LOG2E

    def attend_rows(s):
        first = s * rows_dev
        reach = key_reach(first, rows_dev, length)
        limit = key_limit(first, rows_dev, prefix, valid)

        @pl.loop(0, heads)
        def _(h):
            def lanes(group):
                return pl.ds(pl.multiple_of(group * inner + h * hd, hd), hd)

            q = qkv[first : first + rows_dev, lanes(0)]
            scores = dot32(qkv[0:reach, lanes(1)], q, NT) * score_scale
            scores = jnp.where(lax.broadcasted_iota(jnp.int32, scores.shape, 0) <= limit, scores, NEG)
            top = jnp.max(scores, axis=0, keepdims=True)
            probs = jnp.exp2(scores - top)
            row_total = jnp.sum(probs, axis=0, keepdims=True)
            mixed = (dot32(qkv[0:reach, lanes(2)], probs.astype(bf16), TN) / row_total).T
            lse_ref[h, :, first : first + rows_dev] = top + jnp.log2(row_total)
            gate = jax.nn.sigmoid(gate_ref[h])
            qm = mapped(q.astype(f32))
            denominator = jnp.sum(qm * norm_ref[h], axis=-1, keepdims=True)
            retrieved = dot_three(qm, mem_ref[h], NN) / denominator
            mid[:, pl.ds(pl.multiple_of(s * inner + h * hd, hd), hd)] = mixed
            both_mix = (gate * retrieved + (1.0 - gate) * mixed).astype(bf16)
            for c in range(chunks):
                hid[s * c_rows : (s + 1) * c_rows, pl.ds(pl.multiple_of(c * inner + h * hd, hd), hd)] = both_mix[
                    c * c_rows : (c + 1) * c_rows
                ]

    def update_memory():
        @pl.loop(0, heads)
        def _(h):
            km = mapped(qkv[0:length, pl.ds(pl.multiple_of(inner + h * hd, hd), hd)].astype(f32))
            km = jnp.where(lax.broadcasted_iota(jnp.int32, km.shape, 0) < valid, km, 0.0)
            kh, kl = split_two(km)
            values = qkv[0:length, pl.ds(pl.multiple_of(2 * inner + h * hd, hd), hd)]
            memo_ref[h] = mem_ref[h] + dot32(kh, values, TN) + dot32(kl, values, TN)
            normo_ref[h] = norm_ref[h] + jnp.sum(km, axis=0, keepdims=True)

    for s in range(n):
        attend_rows(s)
    for stage in range(2, cube.levels):
        push(2, stage)
    comb_saves = []
    for s in range(n):
        comb_saves.append(
            pltpu.make_async_copy(mid.at[:, s * inner : (s + 1) * inner], mix_out.at[s * rows_dev : (s + 1) * rows_dev, :], out_sem.at[3 + s])
        )
        for c in range(chunks):
            comb_saves.append(
                pltpu.make_async_copy(
                    hid.at[s * c_rows : (s + 1) * c_rows, c * inner : (c + 1) * inner],
                    comb_out.at[s, c],
                    out_sem.at[3 + n + s * chunks + c],
                )
            )
    for item in comb_saves:
        item.start()

    def project(c):
        flat = part.at[c].reshape(n * c_rows, width)

        @pl.loop(0, width // tile)
        def _(j):
            cols = pl.ds(pl.multiple_of(j * tile, tile), tile)
            flat[:, cols] = dot32(
                hid[:, c * inner : (c + 1) * inner], attn_w[cols, 3 * inner : 4 * inner], NT
            ).astype(bf16)

    def norm_two(c):
        rows = slice(c * c_rows, (c + 1) * c_rows)
        branch = total[...]
        live = live_ref[rows, :]
        stat_ref[0:1, :] += jnp.sum(jnp.sum(branch * branch, axis=-1, keepdims=True) * live, axis=0, keepdims=True)
        m = stream[rows, :].astype(f32) + branch
        mid[rows, :] = m
        x[c, t] = (m * inverse_rms(m) * gain[1:2, :]).astype(bf16)

    def first_half(c, service):
        flat = x.at[c].reshape(n * c_rows, width)
        cot_flat = cot.reshape(n * c_rows, width)

        @pl.loop(0, units // tile)
        def _(j):
            cols = pl.ds(pl.multiple_of(j * tile, tile), tile)
            gate_pre = dot32(flat[...], w_three[0, :, cols], NN)
            up_pre = dot32(flat[...], w_three[1, :, cols], NN)
            grad_hidden = dot32(cot_flat[...], w_three[2, :, cols], NN)
            value, slope = gelu_pair(gate_pre)
            hid[:, cols] = (value * up_pre).astype(bf16)
            ul[:, cols] = (grad_hidden * value).astype(bf16)
            gl[:, cols] = (grad_hidden * up_pre * slope).astype(bf16)
            service(j)

    def second_half(c):
        flat = part.at[c].reshape(n * c_rows, width)

        @pl.loop(0, width // tile)
        def _(j):
            cols = pl.ds(pl.multiple_of(j * tile, tile), tile)
            terms = dot32(gl[...], w_three[0, cols, :], NT) + dot32(ul[...], w_three[1, cols, :], NT)
            flat[:, cols] = terms.astype(bf16)

    def branch_terms(c):
        @pl.loop(0, width // tile)
        def _(j):
            cols = pl.ds(pl.multiple_of(j * tile, tile), tile)
            ul[:, cols] = dot32(hid[...], w_three[2, cols, :], NT).astype(bf16)

    def norm_back(c):
        rows = slice(c * c_rows, (c + 1) * c_rows)
        m = mid[rows, :]
        inv = inverse_rms(m)
        u = m * inv
        gn = total[...]
        e = gn * gain[1:2, :]
        ggain_ref[...] += jnp.sum(gn * u, axis=0, keepdims=True)
        gm = stream[rows, :].astype(f32) + inv * (e - u * jnp.mean(e * u, axis=-1, keepdims=True))
        total[...] = gm
        x[c, t] = gm.astype(bf16)

    def scatter(kind, c, k):
        line.scatter_step(ph(kind, c), k, *lands(c))

    def gather(kind, c, k):
        line.gather_step(ph(kind, c), k, x_at(c) if kind != COT else cot_at(c))

    project(0)
    scatter(RS1, 0, 0)
    project(1)
    scatter(RS1, 1, 0)
    attn_save.wait()
    cube.sent(0, block_of(0))
    gate_load = pltpu.make_async_copy(mlp_hbm.at[0], w_three.at[0], load_sem.at[0])
    gate_load.start()
    gather(COT, 0, 1)
    gather(COT, 1, 1)
    update_memory()
    scatter(RS1, 0, 1)
    push(2, cube.levels)
    push(3, 1)
    one_save.wait()
    all_save.wait()
    qkv_save.wait()
    up_load = pltpu.make_async_copy(mlp_hbm.at[1], w_three.at[1], load_sem.at[1])
    up_load.start()
    gather(COT, 0, 2)
    for k in range(2, n - 1):
        scatter(RS1, 0, k)
    for item in comb_saves:
        item.wait()
    line.scatter_end(ph(RS1, 0), *lands(0), total)
    norm_two(0)
    gather(AG2, 0, 0)
    scatter(RS1, 1, 1)
    gather(COT, 1, 2)
    for stage in range(2, cube.levels):
        push(3, stage)
    for k in range(1, n - 1):
        gather(AG2, 0, k)
        if k + 1 < n - 1:
            scatter(RS1, 1, k + 1)
    gather(COT, 0, 3)
    cot_loads = [pltpu.make_async_copy(cot_all.at[c], cot, load_sem.at[3 + c]) for c in range(chunks)]
    cot_loads[0].start()
    push(3, cube.levels)
    line.gather_sent(AG1, stream_at)
    down_load = pltpu.make_async_copy(mlp_hbm.at[2], w_three.at[2], load_sem.at[2])
    down_load.start()
    line.scatter_end(ph(RS1, 1), *lands(1), total)
    norm_two(1)
    cot_own = pltpu.make_async_copy(cot_hbm, stream, own_sem.at[5])
    cot_own.start()
    gather(AG2, 1, 0)
    gather(AG2, 0, n - 1)
    gather(COT, 1, 3)
    gate_load.wait()
    up_load.wait()
    down_load.wait()
    cot_own.wait()
    outs = {}

    def send_out(name, c, src, dst, sem):
        outs[name, c] = pltpu.make_async_copy(src, dst, out_sem.at[sem])
        outs[name, c].start()

    def save_terms(c):
        for s in range(n):
            outs[("terms", s), c] = pltpu.make_async_copy(
                ul.at[s * c_rows : (s + 1) * c_rows, :], terms_hbm.at[c, s], term_sem.at[c * n + s]
            )
            outs[("terms", s), c].start()

    def await_terms(c):
        for s in range(n):
            outs[("terms", s), c].wait()

    def rows_of(ref, c):
        return ref.at[pl.ds(c * c_rows, c_rows), :]

    def save_chunk(c):
        send_out("x", c, x.at[c], x_out.at[c], 0)
        send_out("hid", c, hid, hid_out.at[c], 1)
        send_out("gl", c, gl, gl_out.at[c], 2)
        send_out("ul", c, ul, ul_out.at[c], 3)

    def finish_back(c):
        line.scatter_end(ph(RS3, c), *lands(c), total)
        norm_back(c)
        send_out("gmid", c, total, rows_of(gmid_out, c), 5)
        gather(AG4, c, 0)
        outs["gmid", c].wait()

    def start_branch(c):
        line.scatter_sent(ph(RS3, c), *lands(c))
        load = pltpu.make_async_copy(terms_hbm.at[c], part.at[c], load_sem.at[5])
        load.start()
        load.wait()
        scatter(RS2, c, 0)

    def finish_branch(c):
        rows = slice(c * c_rows, (c + 1) * c_rows)
        line.scatter_end(ph(RS2, c), *lands(c), total)
        branch = total[...]
        result = mid[rows, :] + branch
        live = live_ref[rows, :]
        stat_ref[1:2, :] += jnp.sum(jnp.sum(result * result, axis=-1, keepdims=True) * live, axis=0, keepdims=True)
        stat_ref[2:3, :] += jnp.sum(jnp.sum(branch * branch, axis=-1, keepdims=True) * live, axis=0, keepdims=True)
        part[c, t] = result.astype(bf16)
        send_out("result", c, part.at[c, t], result_out, 6)
        outs["result", c].wait()

    def during(*steps):
        def service(j):
            for at, step in enumerate(steps):
                @pl.when(j == at)
                def _():
                    step()

        return service

    half_rows = shard // 2
    flat_w = w_three.reshape(3 * width, units)
    cot_flat = cot.reshape(n * c_rows, width)
    trade_orders = [[1] + [1 << b for b in range(1, cube.levels)], [1] + [1 << b for b in range(cube.levels - 1, 0, -1)]]
    spare = width // 2
    sources = ((x_out, gl_out), (x_out, ul_out), (cot_all, hid_out))

    def grad_loads(g):
        left, right = sources[g]
        loads = [
            pltpu.make_async_copy(right.at[0], hid, grad_sem.at[0]),
            pltpu.make_async_copy(right.at[1], gl, grad_sem.at[1]),
            pltpu.make_async_copy(left.at[1], cot, grad_sem.at[2]),
        ]
        for s in range(n):
            loads.append(pltpu.make_async_copy(left.at[0, s], ul.at[s * c_rows : (s + 1) * c_rows, :], grad_sem.at[8 + s]))
        return loads

    def weight_grad(g, service=lambda j: None, wide=256):
        for item in grad_loads(g):
            item.start()
        for item in grad_loads(g):
            item.wait()
        if g > 0:
            first_trade(g - 1).wait_send()

        @pl.loop(0, width // wide)
        def _(j):
            cols = pl.ds(pl.multiple_of(j * wide, wide), wide)
            for first in range(0, units, units // 2):
                span = slice(first, first + units // 2)
                terms = dot32(ul[:, cols], hid[:, span], TN) + dot32(cot_flat[:, cols], gl[:, span], TN)
                for q in range(wide // shard):
                    mask = lax.bitwise_xor(j * (wide // shard) + q, f)
                    row = lax.rem(mask, 2) * spare + (1 - lax.rem(mask, 2)) * (g * width) + (mask // 2) * shard
                    flat_w[pl.ds(pl.multiple_of(row, shard), shard), span] = terms[q * shard : (q + 1) * shard].astype(bf16)
            service(j)

        first_trade(g).start()

    def first_trade(g):
        return pltpu.make_async_remote_copy(
            src_ref=flat_w.at[spare : 2 * spare, :],
            dst_ref=land.at[g, 0],
            send_sem=trade_send.at[g, 0, 0, 0],
            recv_sem=trade_recv.at[g, 0, 0, 0],
            device_id={"fsdp": cube.peer(1)},
            device_id_type=MESH,
        )

    def trades(g, i):
        for half in range(2):
            order = trade_orders[half]
            bit = order[i]
            for mask in range(fsdp_size):
                if all(mask & b == 0 for b in order[: i + 1]):
                    there = pl.ds((mask // 2) * shard + half * half_rows, half_rows)
                    here = pl.ds(g * width + ((mask ^ bit) // 2) * shard + half * half_rows, half_rows)
                    yield mask, half, pltpu.make_async_remote_copy(
                        src_ref=flat_w.at[here, :],
                        dst_ref=land.at[g, i, there, :],
                        send_sem=trade_send.at[g, i, half, mask // 2],
                        recv_sem=trade_recv.at[g, i, half, mask // 2],
                        device_id={"fsdp": cube.peer(bit)},
                        device_id_type=MESH,
                    )

    def trade_start(g, i):
        for _, _, item in trades(g, i):
            item.start()

    def add_first(g):
        first_trade(g).wait_recv()
        load = pltpu.make_async_copy(land.at[g, 0], flat_w.at[width + spare : width + 2 * spare, :], grad_sem.at[3])
        load.start()
        load.wait()

        @pl.loop(0, spare // half_rows)
        def _(r):
            mine = pl.ds(pl.multiple_of(g * width + r * half_rows, half_rows), half_rows)
            came = pl.ds(pl.multiple_of(width + spare + r * half_rows, half_rows), half_rows)
            flat_w[mine, :] = (flat_w[mine, :].astype(f32) + flat_w[came, :].astype(f32)).astype(bf16)

        trade_start(g, 1)

    def save_last(g):
        send_out("kept", g, flat_w.at[g * width : g * width + shard, :], kept_out.at[g], 8 + 3 * g)
        for half in range(2):
            row = g * width + (trade_orders[half][-1] // 2) * shard + half * half_rows
            send_out(("last", half), g, flat_w.at[row : row + half_rows, :], to_send.at[g, half], 9 + 3 * g + half)

    def add_next(g, i):
        places = []
        for mask, half, item in trades(g, i):
            item.wait_recv()
            places.append((mask // 2) * shard + half * half_rows)
        loads = [
            pltpu.make_async_copy(
                land.at[g, i, place : place + half_rows, :],
                flat_w.at[2 * width + spare + place : 2 * width + spare + place + half_rows, :],
                grad_sem.at[4 + at % 4],
            )
            for at, place in enumerate(places)
        ]
        for base in range(0, len(loads), 4):
            for item in loads[base : base + 4]:
                item.start()
            for item in loads[base : base + 4]:
                item.wait()
        for place in places:
            mine = slice(g * width + place, g * width + place + half_rows)
            came = slice(2 * width + spare + place, 2 * width + spare + place + half_rows)
            flat_w[mine, :] = (flat_w[mine, :].astype(f32) + flat_w[came, :].astype(f32)).astype(bf16)
        if i + 1 < cube.levels - 1:
            trade_start(g, i + 1)
        else:
            save_last(g)

    def trade_end(g):
        outs["kept", g].wait()
        for half in range(2):
            outs[("last", half), g].wait()

    def trade_sent(g):
        for i in range(1, cube.levels - 1):
            for _, _, item in trades(g, i):
                item.wait_send()

    cot_loads[0].wait()
    first_half(0, during(*[functools.partial(gather, AG2, 1, k) for k in range(1, n)]))
    cot_loads[1].start()
    save_chunk(0)
    line.scatter_sent(ph(RS1, 0), *lands(0))
    second_half(0)
    line.gather_sent(ph(AG2, 0), x_at(0))
    outs["x", 0].wait()
    outs["ul", 0].wait()
    scatter(RS3, 0, 0)
    branch_terms(0)
    save_terms(0)
    outs["hid", 0].wait()
    outs["gl", 0].wait()
    await_terms(0)
    cot_loads[1].wait()
    first_half(1, during(lambda: None, *[functools.partial(scatter, RS3, 0, k) for k in range(1, n - 1)]))
    save_chunk(1)
    line.scatter_sent(ph(RS1, 1), *lands(1))
    second_half(1)
    line.gather_sent(ph(AG2, 1), x_at(1))
    outs["x", 1].wait()
    outs["ul", 1].wait()
    scatter(RS3, 1, 0)
    finish_back(0)
    branch_terms(1)
    save_terms(1)
    outs["hid", 1].wait()
    outs["gl", 1].wait()
    for item in range(1, 4):
        cube.sent(item, block_of(item))
    scatter(RS3, 1, 1)
    gather(AG4, 0, 1)
    start_branch(0)
    await_terms(1)

    def skip():
        pass

    def z_one():
        for k in range(2, n - 1):
            scatter(RS3, 1, k)
        gather(AG4, 0, 2)

    weight_grad(0, during(*[skip] * 6, z_one))
    scatter(RS2, 0, 1)
    weight_grad(1)
    finish_back(1)
    mid_save = pltpu.make_async_copy(mid, mid_out, own_sem.at[5])
    mid_save.start()
    for k in range(3, n):
        gather(AG4, 0, k)
    send_out("branch", 0, x.at[0], branch_out.at[:, 0], 0)
    for k in range(2, n - 1):
        scatter(RS2, 0, k)
    add_first(0)
    gather(AG4, 1, 1)
    weight_grad(2)
    finish_branch(0)
    add_first(1)
    gather(AG4, 1, 2)
    add_first(2)
    for i in range(1, cube.levels - 1):
        add_next(0, i)
    for k in range(3, n):
        gather(AG4, 1, k)
    send_out("branch", 1, x.at[1], branch_out.at[:, 1], 7)
    for g in (1, 2):
        for i in range(1, cube.levels - 1):
            add_next(g, i)
    for g in range(3):
        trade_end(g)
        trade_sent(g)
    first_trade(2).wait_send()
    mid_save.wait()
    line.scatter_sent(ph(RS3, 1), *lands(1))
    for c in range(chunks):
        outs["branch", c].wait()
    for c in range(chunks):
        line.gather_sent(ph(COT, c), cot_at(c))
        line.gather_sent(ph(AG4, c), x_at(c))
        if c == 0:
            line.scatter_sent(ph(RS2, c), *lands(c))


def whole_layer(bounds, gains, live, memory, norm, gate, stream, cot, attn_weights, mlp_weights, tp_size, fsdp_size, collective_id, tile=512):
    chunks = 2
    rows, width = stream.shape
    inner = attn_weights[0].shape[1]
    units = mlp_weights[0].shape[1]
    heads, hd = memory.shape[:2]
    length = rows * tp_size
    c_rows = rows // chunks
    bf, f32 = jnp.bfloat16, jnp.float32
    S = jax.ShapeDtypeStruct
    any_space = pl.BlockSpec(memory_space=pl.ANY)
    vmem = pl.BlockSpec(memory_space=pltpu.VMEM)
    smem = pl.BlockSpec(memory_space=pltpu.SMEM)
    grid_rows = (chunks, tp_size, c_rows)
    flat_rows = (chunks, tp_size * c_rows)
    levels = fsdp_size.bit_length() - 1
    V, DMA = pltpu.VMEM, pltpu.SemaphoreType.DMA
    return pl.pallas_call(
        functools.partial(layer_kernel, chunks=chunks, tp_size=tp_size, fsdp_size=fsdp_size, tile=tile),
        in_specs=[smem] + [vmem] * 5 + [any_space] * 9,
        out_specs=[any_space] * 20 + [vmem] * 6,
        out_shape=[
            S((3, width, units), bf),
            S((width, 4 * inner), bf),
            S((length, width), bf),
            S((length, 3 * inner), bf),
            S((tp_size, chunks, c_rows, inner), bf),
            S((length, inner), f32),
            S(grid_rows + (width,), bf),
            S(grid_rows + (width,), bf),
            S(flat_rows + (units,), bf), S(flat_rows + (units,), bf), S(flat_rows + (units,), bf),
            S(grid_rows + (width,), bf),
            S((rows // chunks, width), bf),
            S((rows, width), f32),
            S((tp_size, chunks, c_rows, width), bf),
            S((3, width // fsdp_size, units), bf),
            S((3, levels - 1, width // 2, units), bf),
            S((length, width), bf),
            S((rows, width), f32),
            S((3, 2, width // fsdp_size // 2, units), bf),
            S((1, width), f32), S((8, 128), f32), S((heads, 1, length), f32), S((heads, hd, hd), f32), S((heads, 1, hd), f32), S((8, width), f32),
        ],
        scratch_shapes=[
            V((3, width, units), bf),
            V(grid_rows + (width,), bf),
            V((tp_size, c_rows, width), bf),
            V(flat_rows[1:] + (units,), bf), V(flat_rows[1:] + (units,), bf), V(flat_rows[1:] + (units,), bf),
            V(grid_rows + (width,), bf),
            V((chunks, tp_size - 1, c_rows, width), bf), V((chunks, tp_size - 1, c_rows, width), bf),
            V((rows, width), bf),
            V((rows, width), f32), V((c_rows, width), f32),
            DMA((9 + chunks,)), DMA((6,)), DMA((max(17, 3 + tp_size + tp_size * chunks),)),
            DMA((2 * tp_size,)), DMA((8 + tp_size,)),
            DMA((3, levels - 1, 2, fsdp_size // 2)), DMA((3, levels - 1, 2, fsdp_size // 2)),
            DMA((levels,)), DMA((levels,)),
            DMA((4, 2, fsdp_size)), DMA((4, 2, fsdp_size)),
            DMA((1 + 6 * chunks, 2, tp_size - 1)), DMA((1 + 6 * chunks, 2, tp_size - 1)),
        ],
        compiler_params=pltpu.CompilerParams(
            collective_id=collective_id, has_side_effects=True, vmem_limit_bytes=60 * 2**20
        ),
        name="layer_kernel",
    )(
        bounds, gains, live, memory, norm.reshape(heads, 1, hd), jnp.broadcast_to(gate[:, None, None], (heads, 1, hd)),
        stream, cot, *attn_weights, *mlp_weights,
    )


def tail_kernel(
    bounds, gains, live_ref, mem_ref, norm_ref, gate_ref, lse_ref, gain_two_ref, stat_ref,
    branch_hbm, attn_hbm, qkv_hbm, mix_hbm, one_hbm, comb_hbm, stream_hbm, all_hbm, gmid_hbm, mid_hbm, terms_hbm, send_hbm,
    grad_out, result_out, land_mlp, land, kept_out,
    dmem_ref, dnorm_ref, sums,
    attn_w, g_ref, spare_ref, rows_ref, one_ref, qkv, dqkv, mixed_ref, gc_ref, part, land_r, land_l, dk_acc, dv_acc,
    sums_land,
    load_sem, out_sem, mlp_send, mlp_recv, sums_send, sums_recv, trade_send, trade_recv, line_send, line_recv,
    *, chunks, tp_size, fsdp_size, tile,
):
    n = tp_size
    bf16, f32 = jnp.bfloat16, jnp.float32
    t, f = lax.axis_index("tp"), lax.axis_index("fsdp")
    c_rows, width = part.shape[2], part.shape[3]
    rows_dev = c_rows * chunks
    length = n * rows_dev
    heads, hd = mem_ref.shape[0], mem_ref.shape[2]
    inner = heads * hd
    shard = width // fsdp_size
    half_rows = shard // 2
    spare = width // 2
    levels, tp_levels = fsdp_size.bit_length() - 1, n.bit_length() - 1
    orders = [[1] + [1 << b for b in range(1, levels)], [1] + [1 << b for b in range(levels - 1, 0, -1)]]
    line = Line(n, line_send, line_recv)
    total, extra = gc_ref.at[0:c_rows, :], gc_ref.at[c_rows : 2 * c_rows, :]
    count = [0]

    def load(src, dst):
        item = pltpu.make_async_copy(src, dst, load_sem.at[count[0]])
        count[0] += 1
        item.start()
        return item

    def peer(bit):
        return lax.bitwise_xor(f, bit)

    def place(s, c):
        return slice(c * n * c_rows + s * c_rows, c * n * c_rows + (s + 1) * c_rows)

    def origin(s, c):
        return slice(s * rows_dev + c * c_rows, s * rows_dev + (c + 1) * c_rows)

    weight_load = load(attn_hbm, attn_w)
    branch_load = load(branch_hbm, rows_ref)
    terms_load = load(terms_hbm, part.at[chunks])
    comb_load = load(comb_hbm, spare_ref.at[:, 0:inner])
    qkv_load = load(qkv_hbm, qkv)
    mix_load = load(mix_hbm, mixed_ref)
    one_loads = [load(one_hbm.at[origin(s, c), :], one_ref.at[place(s, c), :]) for c in range(chunks) for s in range(n)]

    barrier = pltpu.get_barrier_semaphore()
    for k in range(1, n):
        pl.semaphore_signal(barrier, inc=1, device_id={"tp": lax.rem(t + k, n)}, device_id_type=MESH)
    for b in range(levels):
        pl.semaphore_signal(barrier, inc=1, device_id={"fsdp": peer(1 << b)}, device_id_type=MESH)
    pl.semaphore_wait(barrier, n - 1 + levels)

    mlp_trades = [
        pltpu.make_async_remote_copy(
            src_ref=send_hbm.at[g, half],
            dst_ref=land_mlp.at[g, half],
            send_sem=mlp_send.at[g, half],
            recv_sem=mlp_recv.at[g, half],
            device_id={"fsdp": peer(orders[half][-1])},
            device_id_type=MESH,
        )
        for g in range(3)
        for half in range(2)
    ]
    for item in mlp_trades:
        item.start()

    def lands(c):
        return part.at[c], land_r.at[c], land_l.at[c]

    def scatter(c, k):
        line.scatter_step(c, k, *lands(c))

    terms_load.wait()
    scatter(chunks, 0)

    for item in (weight_load, branch_load, comb_load):
        item.wait()

    def store_grad(j, wide, cols, terms):
        for q in range(wide // shard):
            mask = lax.bitwise_xor(j * (wide // shard) + q, f)
            row = lax.rem(mask, 2) * spare + (mask // 2) * shard
            g_ref[pl.ds(pl.multiple_of(row, shard), shard), cols] = terms[q * shard : (q + 1) * shard].astype(bf16)

    wide = 256

    @pl.loop(0, n)
    def _(s):
        rows = pl.ds(pl.multiple_of(s * rows_dev, rows_dev), rows_dev)
        gc_ref[:, pl.ds(pl.multiple_of(s * inner, inner), inner)] = dot32(
            rows_ref[rows, :], attn_w[:, 3 * inner : 4 * inner], NN
        )

    sums[...] = jnp.zeros_like(sums)
    sums[1:2, :] = gain_two_ref[...]
    lane = lax.broadcasted_iota(jnp.int32, (1, width), 1)
    qkv_load.wait()
    mix_load.wait()

    prefix, valid = bounds[0], bounds[1]
    scale = hd ** -0.5

    @pl.loop(0, heads)
    def _(h):
        def lanes(group):
            return pl.ds(pl.multiple_of(group * inner + h * hd, hd), hd)

        gate = jax.nn.sigmoid(gate_ref[h])
        memory, norm = mem_ref[h], norm_ref[h]
        dmem_ref[h] = jnp.zeros((hd, hd), f32)
        dnorm_ref[h] = jnp.zeros((1, hd), f32)
        dgate = jnp.zeros((1, hd), f32)
        for s in range(n - 1, -1, -1):
            first = s * rows_dev
            reach = key_reach(first, rows_dev, length)
            rows = slice(first, first + rows_dev)
            q = qkv[rows, lanes(0)]
            gc = gc_ref[:, pl.ds(pl.multiple_of(s * inner + h * hd, hd), hd)]
            mixed = mixed_ref[rows, lanes(0)]
            qm = mapped(q.astype(f32))
            inverse = 1.0 / jnp.sum(qm * norm, axis=-1, keepdims=True)
            retrieved = dot_three(qm, memory, NN) * inverse
            dgate = dgate + jnp.sum(gc * (retrieved - mixed), axis=0, keepdims=True)
            gnum = gate * gc * inverse
            gden = -jnp.sum(gnum * retrieved, axis=-1, keepdims=True)
            dmem_ref[h] += dot_three(qm, gnum, TN)
            dnorm_ref[h] += jnp.sum(gden * qm, axis=0, keepdims=True)
            dq_mem = (dot_three(gnum, memory, NT) + gden * norm) * jnp.minimum(qm, 1.0)
            low = ((1.0 - gate) * gc).astype(bf16)
            delta = jnp.sum((low.astype(f32) * mixed).T, axis=0, keepdims=True)
            keys = qkv[0:reach, lanes(1)]
            scores = dot32(keys, q, NT) * (scale * LOG2E)
            limit = key_limit(first, rows_dev, prefix, valid)
            scores = jnp.where(
                lax.broadcasted_iota(jnp.int32, scores.shape, 0) <= limit, scores - lse_ref[h, :, rows], NEG
            )
            probs = jnp.exp2(scores)
            gp = dot32(qkv[0:reach, lanes(2)], low, NT)
            gs = (probs * (gp - delta)).astype(bf16)
            dv = dot32(probs.astype(bf16), low, NN)
            dk = dot32(gs, q, NN)
            if s == n - 1:
                dv_acc[...] = dv
                dk_acc[...] = dk
            else:
                dv_acc[0:reach, :] += dv
                dk_acc[0:reach, :] += dk
            dq = (dot32(keys, gs, TN).T * scale + dq_mem).astype(bf16)
            for c in range(chunks):
                dqkv[place(s, c), lanes(0)] = dq[c * c_rows : (c + 1) * c_rows]
        for s in range(n):
            for c in range(chunks):
                dqkv[place(s, c), lanes(1)] = (dk_acc[origin(s, c), :] * scale).astype(bf16)
                dqkv[place(s, c), lanes(2)] = dv_acc[origin(s, c), :].astype(bf16)
        dgate_sum = jnp.sum(dgate * (gate * (1.0 - gate)), axis=-1, keepdims=True)
        sums[2:3, :] += jnp.where(lane == t * heads + h, dgate_sum, 0.0)
        for k in range(1, n - 1):
            @pl.when(h == k)
            def _():
                scatter(chunks, k)

    @pl.loop(0, width // wide)
    def _(j):
        cols = pl.ds(pl.multiple_of(j * wide, wide), wide)
        store_grad(j, wide, slice(3 * inner, 4 * inner), dot32(rows_ref[:, cols], spare_ref[:, 0:inner], TN))

    all_loads = [load(all_hbm.at[origin(s, c), :], rows_ref.at[place(s, c), :]) for c in range(chunks) for s in range(n)]
    for item in all_loads:
        item.wait()

    for c in range(chunks):
        here = slice(c * n * c_rows, (c + 1) * n * c_rows)
        inverse_all = inverse_rms(rows_ref[here, :].astype(f32))
        flat = part.at[c].reshape(n * c_rows, width)

        @pl.loop(0, width // tile)
        def _(j):
            cols = pl.ds(pl.multiple_of(j * tile, tile), tile)
            terms = dot32(dqkv[here, :], attn_w[cols, 0 : 3 * inner], NT)
            flat[:, cols] = terms.astype(bf16)
            unit = rows_ref[here, cols].astype(f32) * inverse_all
            sums[0:1, cols] += jnp.sum(terms * unit, axis=0, keepdims=True)

        scatter(c, 0)

    own_rows = slice(rows_dev - c_rows, rows_dev)
    mid_load = load(mid_hbm.at[own_rows, :], extra)
    line.scatter_end(chunks, *lands(chunks), total)
    mid_load.wait()
    branch = total[...]
    result = extra[...] + branch
    live = live_ref[own_rows, :]
    part[chunks, t] = result.astype(bf16)
    result_save = pltpu.make_async_copy(part.at[chunks, t], result_out, out_sem.at[0])
    result_save.start()

    def square_sum(v):
        return jnp.sum(jnp.sum(v * v, axis=-1, keepdims=True) * live, axis=0, keepdims=True)

    stats = (stat_ref[1:2, 0:1] + square_sum(result), stat_ref[0:1, 0:1], stat_ref[2:3, 0:1] + square_sum(branch))
    for at, value in enumerate(stats):
        sums[3:4, :] += jnp.where(lane == 3 * f + at, value, 0.0)

    def sums_step(at):
        target = {"fsdp": peer(1 << at)} if at < levels else {"tp": lax.bitwise_xor(t, 1 << (at - levels))}
        return pltpu.make_async_remote_copy(
            src_ref=sums,
            dst_ref=sums_land.at[at],
            send_sem=sums_send.at[at],
            recv_sem=sums_recv.at[at],
            device_id=target,
            device_id_type=MESH,
        )

    def sums_add(at):
        sums_step(at).wait()
        sums[...] += sums_land[at]

    sums_step(0).start()

    for item in one_loads:
        item.wait()

    @pl.loop(0, width // wide)
    def _(j):
        cols = pl.ds(pl.multiple_of(j * wide, wide), wide)
        store_grad(j, wide, slice(0, 3 * inner), dot32(one_ref[:, cols], dqkv[...], TN))

    first_trade = pltpu.make_async_remote_copy(
        src_ref=g_ref.at[spare : 2 * spare, :],
        dst_ref=land.at[0],
        send_sem=trade_send.at[0, 0, 0],
        recv_sem=trade_recv.at[0, 0, 0],
        device_id={"fsdp": peer(1)},
        device_id_type=MESH,
    )
    first_trade.start()

    def trades(i):
        for half in range(2):
            order = orders[half]
            bit = order[i]
            for mask in range(fsdp_size):
                if all(mask & b == 0 for b in order[: i + 1]):
                    there = (mask // 2) * shard + half * half_rows
                    here = ((mask ^ bit) // 2) * shard + half * half_rows
                    yield there, pltpu.make_async_remote_copy(
                        src_ref=g_ref.at[here : here + half_rows, :],
                        dst_ref=land.at[i, there : there + half_rows, :],
                        send_sem=trade_send.at[i, half, mask // 2],
                        recv_sem=trade_recv.at[i, half, mask // 2],
                        device_id={"fsdp": peer(bit)},
                        device_id_type=MESH,
                    )

    def add_rows(mine, came):
        g_ref[mine, :] = (g_ref[mine, :].astype(f32) + spare_ref[came, :].astype(f32)).astype(bf16)

    scatter(0, 1)
    sums_add(0)
    sums_step(1).start()
    scatter(1, 1)
    first_trade.wait_recv()
    first_load = load(land.at[0], spare_ref)
    first_load.wait()

    @pl.loop(0, spare // half_rows)
    def _(r):
        rows = pl.ds(pl.multiple_of(r * half_rows, half_rows), half_rows)
        add_rows(rows, rows)

    for _, item in trades(1):
        item.start()
    for k in range(2, n - 1):
        scatter(0, k)
    sums_add(1)
    sums_step(2).start()

    one_gain = gains[0:1, :]

    def finish(c):
        rows = slice(c * c_rows, (c + 1) * c_rows)
        gmid_load = load(gmid_hbm.at[rows, :], extra)
        stream_load = load(stream_hbm.at[rows, :], part.at[chunks, 0])
        line.scatter_end(c, *lands(c), total)
        gmid_load.wait()
        stream_load.wait()
        v = part[chunks, 0].astype(f32)
        inv = inverse_rms(v)
        u = v * inv
        e = total[...] * one_gain
        total[...] = extra[...] + inv * (e - u * jnp.mean(e * u, axis=-1, keepdims=True))
        save = pltpu.make_async_copy(total, grad_out.at[rows, :], out_sem.at[1])
        save.start()
        save.wait()

    result_save.wait()
    line.scatter_sent(chunks, *lands(chunks))
    for at in range(2, levels):
        sums_add(at)
        sums_step(at + 1).start()
    for k in range(2, n - 1):
        scatter(1, k)
    for i in range(1, levels - 1):
        arrived = list(trades(i))
        loads = []
        for there, item in arrived:
            item.wait_recv()
            loads.append(load(land.at[i, there : there + half_rows, :], spare_ref.at[there : there + half_rows, :]))
        for item in loads:
            item.wait()
        for there, _ in arrived:
            rows = slice(there, there + half_rows)
            add_rows(rows, rows)
        for _, item in trades(i + 1):
            item.start()
    kept_save = pltpu.make_async_copy(g_ref.at[0:shard, :], kept_out, out_sem.at[2])
    kept_save.start()
    finish(0)
    for at in range(levels, levels + tp_levels):
        sums_add(at)
        if at + 1 < levels + tp_levels:
            sums_step(at + 1).start()
    finish(1)
    for _, item in trades(levels - 1):
        item.wait_recv()
    kept_save.wait()
    for item in mlp_trades:
        item.wait()
    first_trade.wait_send()
    for i in range(1, levels):
        for _, item in trades(i):
            item.wait_send()
    for c in range(chunks):
        line.scatter_sent(c, *lands(c))


def whole_tail(
    bounds, gains, live, memory, norm, gate, lse, gain_two, stat,
    branch, attn_full, qkv, mix, flat_one, comb, stream, stream_all, gmid, mid, terms, to_send, tp_size, fsdp_size, collective_id, tile=512,
):
    chunks = 2
    rows, width = stream.shape
    length = rows * tp_size
    c_rows = rows // chunks
    heads, hd = memory.shape[:2]
    inner = heads * hd
    units = to_send.shape[-1]
    shard = width // fsdp_size
    levels, tp_levels = fsdp_size.bit_length() - 1, tp_size.bit_length() - 1
    bf, f32 = jnp.bfloat16, jnp.float32
    S, V, DMA = jax.ShapeDtypeStruct, pltpu.VMEM, pltpu.SemaphoreType.DMA
    any_space = pl.BlockSpec(memory_space=pl.ANY)
    vmem = pl.BlockSpec(memory_space=pltpu.VMEM)
    smem = pl.BlockSpec(memory_space=pltpu.SMEM)
    adds = sum(2 * (fsdp_size >> (i + 1)) for i in range(1, levels - 1))
    loads = 6 + 2 * length // c_rows + 2 + 4 + adds
    return pl.pallas_call(
        functools.partial(tail_kernel, chunks=chunks, tp_size=tp_size, fsdp_size=fsdp_size, tile=tile),
        in_specs=[smem] + [vmem] * 8 + [any_space] * 12,
        out_specs=[any_space] * 5 + [vmem] * 3,
        out_shape=[
            S((rows, width), f32),
            S((c_rows, width), bf),
            S(to_send.shape, bf),
            S((levels, width // 2, 4 * inner), bf),
            S((shard, 4 * inner), bf),
            S((heads, hd, hd), f32), S((heads, 1, hd), f32), S((8, width), f32),
        ],
        scratch_shapes=[
            V((width, 4 * inner), bf),
            V((width, 4 * inner), bf),
            V((width // 2, 4 * inner), bf),
            V((length, width), bf),
            V((length, width), bf),
            V((length, 3 * inner), bf), V((length, 3 * inner), bf),
            V((length, inner), f32), V((rows, tp_size * inner), f32),
            V((chunks + 1, tp_size, c_rows, width), bf),
            V((chunks + 1, tp_size - 1, c_rows, width), bf), V((chunks + 1, tp_size - 1, c_rows, width), bf),
            V((length, hd), f32), V((length, hd), f32),
            V((levels + tp_levels, 8, width), f32),
            DMA((loads,)), DMA((3,)),
            DMA((3, 2)), DMA((3, 2)),
            DMA((levels + tp_levels,)), DMA((levels + tp_levels,)),
            DMA((levels, 2, fsdp_size // 2)), DMA((levels, 2, fsdp_size // 2)),
            DMA((chunks + 1, 2, tp_size - 1)), DMA((chunks + 1, 2, tp_size - 1)),
        ],
        compiler_params=pltpu.CompilerParams(
            collective_id=collective_id, has_side_effects=True, vmem_limit_bytes=60 * 2**20
        ),
        name="tail_kernel",
    )(
        bounds, gains, live, memory, norm.reshape(heads, 1, hd), jnp.broadcast_to(gate[:, None, None], (heads, 1, hd)),
        lse, gain_two, stat, branch, attn_full, qkv, mix, flat_one, comb, stream, stream_all, gmid, mid, terms, to_send,
    )


def on_device(
    stream,
    attn_gain,
    w_query,
    w_key,
    w_value,
    w_out,
    mem_gate,
    mlp_gain,
    w_gate,
    w_up,
    w_down,
    memory,
    normalizer,
    prefix,
    valid,
    cotangent,
):
    f32, bf16 = jnp.float32, jnp.bfloat16
    len_dev, width = (stream.shape[1], stream.shape[2])
    tp_size, fsdp_size = lax.axis_size("tp"), lax.axis_size("fsdp")
    tp_here, seq_here = lax.axis_index("tp"), lax.axis_index("fsdp")
    seq_len = len_dev * tp_size
    heads_here = mem_gate.shape[0]
    prefix_len = prefix[seq_here]
    valid_len = valid[seq_here]
    stream, cotangent = stream[0], cotangent[0]

    shard = width // fsdp_size
    gains = jnp.zeros((8, width), f32)
    gains = lax.dynamic_update_slice(
        gains, jnp.stack([attn_gain, mlp_gain]).astype(f32), (0, seq_here * shard)
    )
    bounds = jnp.stack([prefix_len, valid_len])
    local_position = tp_here * len_dev + jnp.arange(len_dev, dtype=jnp.int32)
    live_here = (local_position < valid_len).astype(f32)[:, None]
    (
        _, attn_full, flat_one, qkv_rows, combined, local_mix, _, _, _, _, _, mlp_terms,
        first_out, grad_middle, branch_low, kept, _, stream_all, middle_rows, to_send,
        gain_two_terms, stats, log_total, memory_next, normalizer_next, gains,
    ) = whole_layer(
        bounds, gains, live_here, memory[0], normalizer[0], mem_gate, stream, cotangent,
        (w_query, w_key, w_value, w_out), (w_gate, w_up, w_down), tp_size, fsdp_size, 1,
    )
    inner = w_query.shape[1]
    stream_grad, second_out, landed, attn_landed, attn_kept, grad_memory, grad_normalizer, joined = whole_tail(
        bounds, gains, live_here, memory[0], normalizer[0], mem_gate, log_total, gain_two_terms, stats,
        branch_low.reshape(seq_len, width), attn_full, qkv_rows, local_mix, flat_one, combined.reshape(seq_len, inner),
        stream, stream_all, grad_middle, middle_rows, mlp_terms[1], to_send, tp_size, fsdp_size, 2,
    )
    stream_out = jnp.concatenate([first_out, second_out], axis=0)
    gate_grad, up_grad, down_grad = (
        kept[g].astype(f32) + landed[g].reshape(shard, -1).astype(f32) for g in range(3)
    )
    query_grad, key_grad, value_grad, out_grad = (
        attn_kept[:, p * inner : (p + 1) * inner].astype(f32)
        + attn_landed[-1, :shard, p * inner : (p + 1) * inner].astype(f32)
        for p in range(4)
    )
    gain_one_grad = lax.dynamic_slice(joined, (0, seq_here * shard), (1, shard))[0]
    gain_two_grad = lax.dynamic_slice(joined, (1, seq_here * shard), (1, shard))[0]
    gate_grad_logit = lax.dynamic_slice(joined, (2, tp_here * heads_here), (1, heads_here))[0]
    stat_sums = lax.dynamic_slice(joined, (3, seq_here * 3), (1, 3))
    token_count = valid_len.astype(f32) * width
    rms_stats = jnp.sqrt(stat_sums / token_count + rms_eps)
    return (
        stream_out[None],
        stream_grad[None],
        gain_one_grad,
        query_grad,
        key_grad,
        value_grad,
        out_grad,
        gate_grad_logit,
        gain_two_grad,
        gate_grad,
        up_grad,
        down_grad,
        memory_next[None],
        normalizer_next[:, 0][None],
        grad_memory[None],
        grad_normalizer[:, 0][None],
        rms_stats,
    )


def solution(mesh):
    placed = (
        P("fsdp", "tp", None),
        P("fsdp"),
        P("fsdp", "tp"),
        P("fsdp", "tp"),
        P("fsdp", "tp"),
        P("fsdp", "tp"),
        P("tp"),
        P("fsdp"),
        P("fsdp", "tp"),
        P("fsdp", "tp"),
        P("fsdp", "tp"),
        P("fsdp", "tp", None, None),
        P("fsdp", "tp", None),
        P(),
        P(),
        P("fsdp", "tp", None),
    )
    return jax.shard_map(
        on_device,
        mesh=mesh,
        in_specs=placed,
        out_specs=(
            P("fsdp", "tp", None),
            P("fsdp", "tp", None),
            P("fsdp"),
            P("fsdp", "tp"),
            P("fsdp", "tp"),
            P("fsdp", "tp"),
            P("fsdp", "tp"),
            P("tp"),
            P("fsdp"),
            P("fsdp", "tp"),
            P("fsdp", "tp"),
            P("fsdp", "tp"),
            P("fsdp", "tp", None, None),
            P("fsdp", "tp", None),
            P("fsdp", "tp", None, None),
            P("fsdp", "tp", None),
            P("fsdp", None),
        ),
        check_vma=False,
    )
```

```python
import functools

import jax
import jax.numpy as jnp
from jax import lax
from jax.experimental import pallas as pl
from jax.experimental.pallas import tpu as pltpu
from jax.sharding import PartitionSpec as P

rms_eps = 1e-06
NEG = -1e30
LOG2E = 1.4426950408889634


def split_two(x):
    high = x.astype(jnp.bfloat16)
    return high, (x - high.astype(jnp.float32)).astype(jnp.bfloat16)


def dot32(a, b, dims):
    return lax.dot_general(a, b, (dims, ((), ())), preferred_element_type=jnp.float32)


def dot_three(a, b, dims):
    ah, al = split_two(a)
    bh, bl = split_two(b)
    return dot32(ah, bh, dims) + dot32(ah, bl, dims) + dot32(al, bh, dims)


NN, NT, TN = ((1,), (0,)), ((1,), (1,)), ((0,), (0,))


def mapped(v):
    return jnp.where(v > 0, v + 1.0, jnp.exp(jnp.minimum(v, 0.0)))


def key_reach(first, rows, keys):
    return min(keys, max(keys // 2, first + rows))


def key_limit(first, rows, prefix, valid):
    row = first + lax.broadcasted_iota(jnp.int32, (1, rows), 1)
    return jnp.minimum(valid - 1, jnp.maximum(row, prefix - 1))


norm_eps = 1e-06
MESH = pl.DeviceIdType.MESH
RIGHT, LEFT = 0, 1
PIECE = 32


class Line:
    def __init__(self, size, send_sem, recv_sem):
        self.size, self.send_sem, self.recv_sem = size, send_sem, recv_sem
        self.here = lax.axis_index("tp")

    def copy(self, phase, way, slot, src, dst):
        to = self.here + 1 if way == RIGHT else self.here - 1
        return pltpu.make_async_remote_copy(
            src_ref=src,
            dst_ref=dst,
            send_sem=self.send_sem.at[phase, way, slot],
            recv_sem=self.recv_sem.at[phase, way, slot],
            device_id={"tp": to},
            device_id_type=MESH,
        )

    def arrived(self, phase, way, slot, dst):
        self.copy(phase, way, slot, dst, dst).wait_recv()

    def scatter_step(self, phase, step, part, land_right, land_left):
        n, t = self.size, self.here

        def pass_on(way, slot, shard, land, first):
            @pl.when(jnp.logical_not(first))
            def _():
                self.arrived(phase, way, slot, land)

                @pl.loop(0, part.shape[1] // PIECE)
                def _(r):
                    rows = pl.ds(pl.multiple_of(r * PIECE, PIECE), PIECE)
                    came = land[rows, :].astype(jnp.float32)
                    part[shard, rows, :] = (part[shard, rows, :].astype(jnp.float32) + came).astype(part.dtype)

            self.copy(phase, way, slot, part.at[shard], land).start()

        right, left = step - t, step - (n - 1 - t)
        far, near = n - 1 - right, left

        @pl.when((right >= 0) & (far > t))
        def _():
            pass_on(RIGHT, right, far, land_right.at[far - 1], t == 0)

        @pl.when((left >= 0) & (near < t))
        def _():
            pass_on(LEFT, left, near, land_left.at[near], t == n - 1)

    def scatter_end(self, phase, part, land_right, land_left, total):
        n, t = self.size, self.here

        def over(work):
            @pl.loop(0, part.shape[1] // PIECE)
            def _(r):
                work(pl.ds(pl.multiple_of(r * PIECE, PIECE), PIECE))

        def own(rows):
            total[rows, :] = part[t, rows, :].astype(jnp.float32)

        def from_left(rows):
            total[rows, :] += land_right[t - 1, rows, :].astype(jnp.float32)

        def from_right(rows):
            total[rows, :] += land_left[t, rows, :].astype(jnp.float32)

        over(own)

        @pl.when(t > 0)
        def _():
            self.arrived(phase, RIGHT, n - 1 - t, land_right.at[t - 1])
            over(from_left)

        @pl.when(t < n - 1)
        def _():
            self.arrived(phase, LEFT, t, land_left.at[t])
            over(from_right)

    def scatter_sent(self, phase, part, land_right, land_left):
        n, t = self.size, self.here
        for k in range(n - 1):
            far, near = n - 1 - k, k

            @pl.when(t < far)
            def _():
                self.copy(phase, RIGHT, k, part.at[far], land_right.at[far - 1]).wait_send()

            @pl.when(t > near)
            def _():
                self.copy(phase, LEFT, k, part.at[near], land_left.at[near]).wait_send()

    def gather_step(self, phase, k, shard_at):
        n, t = self.size, self.here

        @pl.when(t >= k)
        def _():
            shard = shard_at(t - k)
            if k > 0:
                self.arrived(phase, RIGHT, k - 1, shard)
            if k < n - 1:
                @pl.when(t < n - 1)
                def _():
                    self.copy(phase, RIGHT, k, shard, shard).start()

        @pl.when(t + k <= n - 1)
        def _():
            shard = shard_at(t + k)
            if k > 0:
                self.arrived(phase, LEFT, k - 1, shard)
            if k < n - 1:
                @pl.when(t > 0)
                def _():
                    self.copy(phase, LEFT, k, shard, shard).start()

    def gather_sent(self, phase, shard_at):
        n, t = self.size, self.here
        for k in range(n - 1):
            @pl.when((t >= k) & (t < n - 1))
            def _():
                self.copy(phase, RIGHT, k, shard_at(t - k), shard_at(t - k)).wait_send()

            @pl.when((t + k <= n - 1) & (t > 0))
            def _():
                self.copy(phase, LEFT, k, shard_at(t + k), shard_at(t + k)).wait_send()


class Cube:
    def __init__(self, size, send_sem, recv_sem):
        self.size, self.send_sem, self.recv_sem = size, send_sem, recv_sem
        self.here = lax.axis_index("fsdp")
        self.levels = size.bit_length() - 1
        ups = [1 << b for b in range(1, self.levels)]
        self.orders = [ups[::-1] + [1], ups + [1]]

    def peer(self, bit):
        return lax.bitwise_xor(self.here, bit)

    def held(self, half, stage):
        masks = [0]
        for bit in self.orders[half][:stage]:
            masks += [mask ^ bit for mask in masks]
        return masks

    def copy(self, item, half, mask, bit, block_at):
        owner = self.peer(mask) if mask else self.here
        block = block_at(owner, half)
        return pltpu.make_async_remote_copy(
            src_ref=block,
            dst_ref=block,
            send_sem=self.send_sem.at[item, half, mask ^ bit],
            recv_sem=self.recv_sem.at[item, half, mask ^ bit],
            device_id={"fsdp": self.peer(bit)},
            device_id_type=MESH,
        )

    def await_stage(self, item, stage, block_at):
        for half in range(2):
            bit = self.orders[half][stage]
            for mask in self.held(half, stage):
                block = block_at(self.peer(mask ^ bit), half)
                pltpu.make_async_remote_copy(
                    src_ref=block,
                    dst_ref=block,
                    send_sem=self.send_sem.at[item, half, mask ^ bit],
                    recv_sem=self.recv_sem.at[item, half, mask ^ bit],
                    device_id={"fsdp": self.peer(bit)},
                    device_id_type=MESH,
                ).wait_recv()

    def stage(self, item, stage, block_at):
        if stage > 0:
            self.await_stage(item, stage - 1, block_at)
        if stage == self.levels:
            return
        for half in range(2):
            bit = self.orders[half][stage]
            for mask in self.held(half, stage):
                self.copy(item, half, mask, bit, block_at).start()

    def sent(self, item, block_at):
        for stage in range(self.levels):
            for half in range(2):
                bit = self.orders[half][stage]
                for mask in self.held(half, stage):
                    self.copy(item, half, mask, bit, block_at).wait_send()


GELU_A, GELU_B = 0.7978845608028654, 0.044715


def gelu_pair(v):
    square = v * v
    curve = jnp.tanh(v * (GELU_A + GELU_A * GELU_B * square))
    half = 0.5 + 0.5 * curve
    slope = half + (0.5 * v) * (1.0 - curve * curve) * (GELU_A + 3.0 * GELU_A * GELU_B * square)
    return v * half, slope


def inverse_rms(v):
    return lax.rsqrt(jnp.mean(v * v, axis=-1, keepdims=True) + norm_eps)


def layer_kernel(
    bounds, gain_in, live_ref, mem_ref, norm_ref, gate_ref,
    stream_hbm, cot_hbm, wq_hbm, wk_hbm, wv_hbm, wo_hbm, wg_hbm, wu_hbm, wd_hbm,
    mlp_hbm, attn_out, one_out, qkv_out, comb_out, mix_out, cot_all, x_out, hid_out, gl_out, ul_out, terms_hbm,
    result_out, gmid_out, branch_out, kept_out, land, all_out, mid_out, to_send,
    ggain_ref, stat_ref, lse_ref, memo_ref, normo_ref, gain,
    w_three, x, cot, hid, gl, ul, part, land_r, land_l, stream, mid, total,
    own_sem, load_sem, out_sem, term_sem, grad_sem, trade_send, trade_recv, gain_send, gain_recv, cube_send, cube_recv, line_send, line_recv,
    *, chunks, tp_size, fsdp_size, tile,
):
    n = tp_size
    bf16, f32 = jnp.bfloat16, jnp.float32
    t, f = lax.axis_index("tp"), lax.axis_index("fsdp")
    c_rows, width = x.shape[2], x.shape[3]
    units = hid.shape[1]
    rows_dev = stream.shape[0]
    length = rows_dev * n
    heads, hd = mem_ref.shape[0], mem_ref.shape[2]
    inner = heads * hd
    shard = width // fsdp_size
    line = Line(n, line_send, line_recv)
    cube = Cube(fsdp_size, cube_send, cube_recv)
    bits = [1 << b for b in range(cube.levels)]
    AG1 = 0

    def ph(kind, c):
        return 1 + kind * chunks + c

    COT, RS1, AG2, RS3, AG4, RS2 = range(6)

    attn_w = w_three.at[0]
    qkv = w_three.at[1]
    flat_one = w_three.at[2]

    def stream_at(s):
        return w_three.at[2, pl.ds(pl.multiple_of(length + s * rows_dev, rows_dev), rows_dev), :]

    def x_at(c):
        return lambda s: x.at[c, s]

    def cot_at(c):
        return lambda s: cot_all.at[c, s]

    def lands(c):
        return part.at[c], land_r.at[c], land_l.at[c]

    def block_of(item):
        whole = attn_w if item == 0 else mlp_hbm.at[item - 1]

        def at(owner, half):
            rows = shard // 2
            return whole.at[pl.ds(pl.multiple_of(owner * shard + half * rows, rows), rows), :]

        return at

    def push(item, stage):
        cube.stage(item, stage, block_of(item))

    own_rows = pl.ds(pl.multiple_of(f * shard, shard), shard)
    own = [
        pltpu.make_async_copy(w, w_three.at[0, own_rows, p * inner : (p + 1) * inner], own_sem.at[p])
        for p, w in enumerate((wq_hbm, wk_hbm, wv_hbm, wo_hbm))
    ]
    own += [pltpu.make_async_copy(stream_hbm, stream_at(t), own_sem.at[4]), pltpu.make_async_copy(stream_hbm, stream, own_sem.at[5])]
    homes = [hid.at[0:shard, :], hid.at[shard : 2 * shard, :], gl.at[0:shard, :]]
    own += [pltpu.make_async_copy(w, homes[m], own_sem.at[6 + m]) for m, w in enumerate((wg_hbm, wu_hbm, wd_hbm))]
    own.append(pltpu.make_async_copy(cot_hbm, ul.at[0:rows_dev, :], own_sem.at[9]))
    placed = [pltpu.make_async_copy(homes[m], mlp_hbm.at[m, own_rows, :], own_sem.at[6 + m]) for m in range(3)]
    placed += [
        pltpu.make_async_copy(ul.at[c * c_rows : (c + 1) * c_rows, :], cot_all.at[c, t], own_sem.at[9 + c])
        for c in range(chunks)
    ]
    for item in own:
        item.start()
    gain[...] = gain_in[...]
    ggain_ref[...] = jnp.zeros_like(ggain_ref)
    stat_ref[...] = jnp.zeros_like(stat_ref)

    barrier = pltpu.get_barrier_semaphore()

    @pl.when(t > 0)
    def _():
        pl.semaphore_signal(barrier, inc=1, device_id={"tp": t - 1}, device_id_type=MESH)

    @pl.when(t < n - 1)
    def _():
        pl.semaphore_signal(barrier, inc=1, device_id={"tp": t + 1}, device_id_type=MESH)

    for bit in bits:
        pl.semaphore_signal(barrier, inc=1, device_id={"fsdp": cube.peer(bit)}, device_id_type=MESH)
    peers = (t > 0).astype(jnp.int32) + (t < n - 1).astype(jnp.int32) + len(bits)
    pl.semaphore_wait(barrier, peers)

    for item in own[:6]:
        item.wait()
    push(0, 0)
    line.gather_step(AG1, 0, stream_at)
    for item in own[6:]:
        item.wait()
    for item in placed:
        item.start()
    for level, bit in enumerate(bits):
        trade = pltpu.make_async_remote_copy(
            src_ref=gain,
            dst_ref=total.at[8 * level : 8 * level + 8, :],
            send_sem=gain_send.at[level],
            recv_sem=gain_recv.at[level],
            device_id={"fsdp": cube.peer(bit)},
            device_id_type=MESH,
        )
        trade.start()
        trade.wait()
        gain[...] += total[8 * level : 8 * level + 8, :]
    for item in placed:
        item.wait()

    def norm_one(s):
        raw = stream_at(s)

        @pl.loop(0, rows_dev // PIECE)
        def _(r):
            v = raw[pl.ds(pl.multiple_of(r * PIECE, PIECE), PIECE), :].astype(f32)
            flat_one[pl.ds(pl.multiple_of(s * rows_dev + r * PIECE, PIECE), PIECE), :] = (
                v * inverse_rms(v) * gain[0:1, :]
            ).astype(bf16)

    def project_one(s):
        rows = pl.ds(pl.multiple_of(s * rows_dev, rows_dev), rows_dev)

        @pl.loop(0, 3)
        def _(p):
            cols = pl.ds(pl.multiple_of(p * inner, inner), inner)
            qkv[rows, cols] = dot32(flat_one[rows, :], attn_w[:, cols], NN).astype(bf16)

    def arrived_pair(k, work):
        @pl.when(t >= k)
        def _():
            work(t - k)

        @pl.when(t + k <= n - 1)
        def _():
            work(t + k)

    norm_one(t)
    push(0, 1)
    push(1, 0)
    line.gather_step(AG1, 1, stream_at)
    for stage in range(2, cube.levels):
        push(0, stage)
    arrived_pair(1, norm_one)
    push(0, cube.levels)
    attn_save = pltpu.make_async_copy(attn_w, attn_out, out_sem.at[0])
    attn_save.start()
    project_one(t)
    push(1, 1)
    push(2, 0)
    line.gather_step(AG1, 2, stream_at)
    arrived_pair(1, project_one)

    def both(s):
        norm_one(s)
        project_one(s)

    for k in range(2, n):
        if k > 2:
            line.gather_step(AG1, k, stream_at)
        if k == n - 1:
            for c in range(chunks):
                line.gather_step(ph(COT, c), 0, cot_at(c))
        arrived_pair(k, both)
    one_save = pltpu.make_async_copy(flat_one.at[0:length, :], one_out, out_sem.at[1])
    one_save.start()
    all_save = pltpu.make_async_copy(flat_one.at[length : 2 * length, :], all_out, own_sem.at[4])
    all_save.start()
    qkv_save = pltpu.make_async_copy(qkv.at[0:length, 0 : 3 * inner], qkv_out, out_sem.at[2])
    qkv_save.start()
    for stage in range(2, cube.levels):
        push(1, stage)
    push(2, 1)
    push(3, 0)
    push(1, cube.levels)

    prefix, valid = bounds[0], bounds[1]
    score_scale = hd ** -0.5 * LOG2E

    def attend_rows(s):
        first = s * rows_dev
        reach = key_reach(first, rows_dev, length)
        limit = key_limit(first, rows_dev, prefix, valid)

        @pl.loop(0, heads)
        def _(h):
            def lanes(group):
                return pl.ds(pl.multiple_of(group * inner + h * hd, hd), hd)

            q = qkv[first : first + rows_dev, lanes(0)]
            scores = dot32(qkv[0:reach, lanes(1)], q, NT) * score_scale
            scores = jnp.where(lax.broadcasted_iota(jnp.int32, scores.shape, 0) <= limit, scores, NEG)
            top = jnp.max(scores, axis=0, keepdims=True)
            probs = jnp.exp2(scores - top)
            row_total = jnp.sum(probs, axis=0, keepdims=True)
            mixed = (dot32(qkv[0:reach, lanes(2)], probs.astype(bf16), TN) / row_total).T
            lse_ref[h, :, first : first + rows_dev] = top + jnp.log2(row_total)
            gate = jax.nn.sigmoid(gate_ref[h])
            qm = mapped(q.astype(f32))
            denominator = jnp.sum(qm * norm_ref[h], axis=-1, keepdims=True)
            retrieved = dot_three(qm, mem_ref[h], NN) / denominator
            mid[:, pl.ds(pl.multiple_of(s * inner + h * hd, hd), hd)] = mixed
            both_mix = (gate * retrieved + (1.0 - gate) * mixed).astype(bf16)
            for c in range(chunks):
                hid[s * c_rows : (s + 1) * c_rows, pl.ds(pl.multiple_of(c * inner + h * hd, hd), hd)] = both_mix[
                    c * c_rows : (c + 1) * c_rows
                ]

    def update_memory():
        @pl.loop(0, heads)
        def _(h):
            km = mapped(qkv[0:length, pl.ds(pl.multiple_of(inner + h * hd, hd), hd)].astype(f32))
            km = jnp.where(lax.broadcasted_iota(jnp.int32, km.shape, 0) < valid, km, 0.0)
            kh, kl = split_two(km)
            values = qkv[0:length, pl.ds(pl.multiple_of(2 * inner + h * hd, hd), hd)]
            memo_ref[h] = mem_ref[h] + dot32(kh, values, TN) + dot32(kl, values, TN)
            normo_ref[h] = norm_ref[h] + jnp.sum(km, axis=0, keepdims=True)

    for s in range(n):
        attend_rows(s)
    for stage in range(2, cube.levels):
        push(2, stage)
    comb_saves = []
    for s in range(n):
        comb_saves.append(
            pltpu.make_async_copy(mid.at[:, s * inner : (s + 1) * inner], mix_out.at[s * rows_dev : (s + 1) * rows_dev, :], out_sem.at[3 + s])
        )
        for c in range(chunks):
            comb_saves.append(
                pltpu.make_async_copy(
                    hid.at[s * c_rows : (s + 1) * c_rows, c * inner : (c + 1) * inner],
                    comb_out.at[s, c],
                    out_sem.at[3 + n + s * chunks + c],
                )
            )
    for item in comb_saves:
        item.start()

    def project(c):
        flat = part.at[c].reshape(n * c_rows, width)

        @pl.loop(0, width // tile)
        def _(j):
            cols = pl.ds(pl.multiple_of(j * tile, tile), tile)
            flat[:, cols] = dot32(
                hid[:, c * inner : (c + 1) * inner], attn_w[cols, 3 * inner : 4 * inner], NT
            ).astype(bf16)

    def by_piece(c, work):
        @pl.loop(0, c_rows // PIECE)
        def _(r):
            piece = pl.ds(pl.multiple_of(r * PIECE, PIECE), PIECE)
            work(piece, pl.ds(pl.multiple_of(c * c_rows + r * PIECE, PIECE), PIECE))

    def square_sum(v, live):
        return jnp.sum(jnp.sum(v * v, axis=-1, keepdims=True) * live, axis=0, keepdims=True)

    def norm_two(c):
        def work(piece, rows):
            branch = total[piece, :]
            stat_ref[0:1, :] += square_sum(branch, live_ref[rows, :])
            m = stream[rows, :].astype(f32) + branch
            mid[rows, :] = m
            x[c, t, piece, :] = (m * inverse_rms(m) * gain[1:2, :]).astype(bf16)

        by_piece(c, work)

    def first_half(c, service):
        flat = x.at[c].reshape(n * c_rows, width)
        cot_flat = cot.reshape(n * c_rows, width)

        @pl.loop(0, units // tile)
        def _(j):
            cols = pl.ds(pl.multiple_of(j * tile, tile), tile)
            gate_pre = dot32(flat[...], w_three[0, :, cols], NN)
            up_pre = dot32(flat[...], w_three[1, :, cols], NN)
            grad_hidden = dot32(cot_flat[...], w_three[2, :, cols], NN)
            value, slope = gelu_pair(gate_pre)
            hid[:, cols] = (value * up_pre).astype(bf16)
            ul[:, cols] = (grad_hidden * value).astype(bf16)
            gl[:, cols] = (grad_hidden * up_pre * slope).astype(bf16)
            service(j)

    def second_half(c):
        flat = part.at[c].reshape(n * c_rows, width)

        @pl.loop(0, width // tile)
        def _(j):
            cols = pl.ds(pl.multiple_of(j * tile, tile), tile)
            terms = dot32(gl[...], w_three[0, cols, :], NT) + dot32(ul[...], w_three[1, cols, :], NT)
            flat[:, cols] = terms.astype(bf16)

    def branch_terms(c):
        @pl.loop(0, width // tile)
        def _(j):
            cols = pl.ds(pl.multiple_of(j * tile, tile), tile)
            ul[:, cols] = dot32(hid[...], w_three[2, cols, :], NT).astype(bf16)

    def norm_back(c):
        def work(piece, rows):
            m = mid[rows, :]
            inv = inverse_rms(m)
            u = m * inv
            gn = total[piece, :]
            e = gn * gain[1:2, :]
            ggain_ref[...] += jnp.sum(gn * u, axis=0, keepdims=True)
            gm = stream[rows, :].astype(f32) + inv * (e - u * jnp.mean(e * u, axis=-1, keepdims=True))
            total[piece, :] = gm
            x[c, t, piece, :] = gm.astype(bf16)

        by_piece(c, work)

    def scatter(kind, c, k):
        line.scatter_step(ph(kind, c), k, *lands(c))

    def gather(kind, c, k):
        line.gather_step(ph(kind, c), k, x_at(c) if kind != COT else cot_at(c))

    project(0)
    scatter(RS1, 0, 0)
    project(1)
    scatter(RS1, 1, 0)
    attn_save.wait()
    cube.sent(0, block_of(0))
    gate_load = pltpu.make_async_copy(mlp_hbm.at[0], w_three.at[0], load_sem.at[0])
    gate_load.start()
    gather(COT, 0, 1)
    gather(COT, 1, 1)
    update_memory()
    scatter(RS1, 0, 1)
    push(2, cube.levels)
    push(3, 1)
    one_save.wait()
    all_save.wait()
    qkv_save.wait()
    up_load = pltpu.make_async_copy(mlp_hbm.at[1], w_three.at[1], load_sem.at[1])
    up_load.start()
    gather(COT, 0, 2)
    for k in range(2, n - 1):
        scatter(RS1, 0, k)
    for item in comb_saves:
        item.wait()
    line.scatter_end(ph(RS1, 0), *lands(0), total)
    norm_two(0)
    gather(AG2, 0, 0)
    scatter(RS1, 1, 1)
    gather(COT, 1, 2)
    for stage in range(2, cube.levels):
        push(3, stage)
    for k in range(1, n - 1):
        gather(AG2, 0, k)
        if k + 1 < n - 1:
            scatter(RS1, 1, k + 1)
    gather(COT, 0, 3)
    cot_loads = [pltpu.make_async_copy(cot_all.at[c], cot, load_sem.at[3 + c]) for c in range(chunks)]
    cot_loads[0].start()
    push(3, cube.levels)
    line.gather_sent(AG1, stream_at)
    down_load = pltpu.make_async_copy(mlp_hbm.at[2], w_three.at[2], load_sem.at[2])
    down_load.start()
    line.scatter_end(ph(RS1, 1), *lands(1), total)
    norm_two(1)
    cot_own = pltpu.make_async_copy(cot_hbm, stream, own_sem.at[5])
    cot_own.start()
    gather(AG2, 1, 0)
    gather(AG2, 0, n - 1)
    gather(COT, 1, 3)
    gate_load.wait()
    up_load.wait()
    down_load.wait()
    cot_own.wait()
    outs = {}

    def send_out(name, c, src, dst, sem):
        outs[name, c] = pltpu.make_async_copy(src, dst, out_sem.at[sem])
        outs[name, c].start()

    def save_terms(c):
        for s in range(n):
            outs[("terms", s), c] = pltpu.make_async_copy(
                ul.at[s * c_rows : (s + 1) * c_rows, :], terms_hbm.at[c, s], term_sem.at[c * n + s]
            )
            outs[("terms", s), c].start()

    def await_terms(c):
        for s in range(n):
            outs[("terms", s), c].wait()

    def rows_of(ref, c):
        return ref.at[pl.ds(c * c_rows, c_rows), :]

    def save_chunk(c):
        send_out("x", c, x.at[c], x_out.at[c], 0)
        send_out("hid", c, hid, hid_out.at[c], 1)
        send_out("gl", c, gl, gl_out.at[c], 2)
        send_out("ul", c, ul, ul_out.at[c], 3)

    def finish_back(c):
        line.scatter_end(ph(RS3, c), *lands(c), total)
        norm_back(c)
        send_out("gmid", c, total, rows_of(gmid_out, c), 5)
        gather(AG4, c, 0)
        outs["gmid", c].wait()

    def start_branch(c):
        line.scatter_sent(ph(RS3, c), *lands(c))
        load = pltpu.make_async_copy(terms_hbm.at[c], part.at[c], load_sem.at[5])
        load.start()
        load.wait()
        scatter(RS2, c, 0)

    def finish_branch(c):
        line.scatter_end(ph(RS2, c), *lands(c), total)

        def work(piece, rows):
            branch = total[piece, :]
            result = mid[rows, :] + branch
            live = live_ref[rows, :]
            stat_ref[1:2, :] += square_sum(result, live)
            stat_ref[2:3, :] += square_sum(branch, live)
            part[c, t, piece, :] = result.astype(bf16)

        by_piece(c, work)
        send_out("result", c, part.at[c, t], result_out, 6)
        outs["result", c].wait()

    def during(*steps):
        def service(j):
            for at, step in enumerate(steps):
                @pl.when(j == at)
                def _():
                    step()

        return service

    half_rows = shard // 2
    flat_w = w_three.reshape(3 * width, units)
    cot_flat = cot.reshape(n * c_rows, width)
    trade_orders = [[1] + [1 << b for b in range(1, cube.levels)], [1] + [1 << b for b in range(cube.levels - 1, 0, -1)]]
    spare = width // 2
    sources = ((x_out, gl_out), (x_out, ul_out), (cot_all, hid_out))

    def grad_loads(g):
        left, right = sources[g]
        loads = [
            pltpu.make_async_copy(right.at[0], hid, grad_sem.at[0]),
            pltpu.make_async_copy(right.at[1], gl, grad_sem.at[1]),
            pltpu.make_async_copy(left.at[1], cot, grad_sem.at[2]),
        ]
        for s in range(n):
            loads.append(pltpu.make_async_copy(left.at[0, s], ul.at[s * c_rows : (s + 1) * c_rows, :], grad_sem.at[8 + s]))
        return loads

    def weight_grad(g, service=lambda j: None, wide=256):
        for item in grad_loads(g):
            item.start()
        for item in grad_loads(g):
            item.wait()
        if g > 0:
            first_trade(g - 1).wait_send()

        @pl.loop(0, width // wide)
        def _(j):
            cols = pl.ds(pl.multiple_of(j * wide, wide), wide)
            for first in range(0, units, units // 2):
                span = slice(first, first + units // 2)
                terms = dot32(ul[:, cols], hid[:, span], TN) + dot32(cot_flat[:, cols], gl[:, span], TN)
                for q in range(wide // shard):
                    mask = lax.bitwise_xor(j * (wide // shard) + q, f)
                    row = lax.rem(mask, 2) * spare + (1 - lax.rem(mask, 2)) * (g * width) + (mask // 2) * shard
                    flat_w[pl.ds(pl.multiple_of(row, shard), shard), span] = terms[q * shard : (q + 1) * shard].astype(bf16)
            service(j)

        first_trade(g).start()

    def first_trade(g):
        return pltpu.make_async_remote_copy(
            src_ref=flat_w.at[spare : 2 * spare, :],
            dst_ref=land.at[g, 0],
            send_sem=trade_send.at[g, 0, 0, 0],
            recv_sem=trade_recv.at[g, 0, 0, 0],
            device_id={"fsdp": cube.peer(1)},
            device_id_type=MESH,
        )

    def trades(g, i):
        for half in range(2):
            order = trade_orders[half]
            bit = order[i]
            for mask in range(fsdp_size):
                if all(mask & b == 0 for b in order[: i + 1]):
                    there = pl.ds((mask // 2) * shard + half * half_rows, half_rows)
                    here = pl.ds(g * width + ((mask ^ bit) // 2) * shard + half * half_rows, half_rows)
                    yield mask, half, pltpu.make_async_remote_copy(
                        src_ref=flat_w.at[here, :],
                        dst_ref=land.at[g, i, there, :],
                        send_sem=trade_send.at[g, i, half, mask // 2],
                        recv_sem=trade_recv.at[g, i, half, mask // 2],
                        device_id={"fsdp": cube.peer(bit)},
                        device_id_type=MESH,
                    )

    def trade_start(g, i):
        for _, _, item in trades(g, i):
            item.start()

    def add_first(g):
        first_trade(g).wait_recv()
        load = pltpu.make_async_copy(land.at[g, 0], flat_w.at[width + spare : width + 2 * spare, :], grad_sem.at[3])
        load.start()
        load.wait()

        @pl.loop(0, spare // half_rows)
        def _(r):
            mine = pl.ds(pl.multiple_of(g * width + r * half_rows, half_rows), half_rows)
            came = pl.ds(pl.multiple_of(width + spare + r * half_rows, half_rows), half_rows)
            flat_w[mine, :] = (flat_w[mine, :].astype(f32) + flat_w[came, :].astype(f32)).astype(bf16)

        trade_start(g, 1)

    def save_last(g):
        send_out("kept", g, flat_w.at[g * width : g * width + shard, :], kept_out.at[g], 8 + 3 * g)
        for half in range(2):
            row = g * width + (trade_orders[half][-1] // 2) * shard + half * half_rows
            send_out(("last", half), g, flat_w.at[row : row + half_rows, :], to_send.at[g, half], 9 + 3 * g + half)

    def add_next(g, i):
        places = []
        for mask, half, item in trades(g, i):
            item.wait_recv()
            places.append((mask // 2) * shard + half * half_rows)
        loads = [
            pltpu.make_async_copy(
                land.at[g, i, place : place + half_rows, :],
                flat_w.at[2 * width + spare + place : 2 * width + spare + place + half_rows, :],
                grad_sem.at[4 + at % 4],
            )
            for at, place in enumerate(places)
        ]
        for base in range(0, len(loads), 4):
            for item in loads[base : base + 4]:
                item.start()
            for item in loads[base : base + 4]:
                item.wait()
        for place in places:
            mine = slice(g * width + place, g * width + place + half_rows)
            came = slice(2 * width + spare + place, 2 * width + spare + place + half_rows)
            flat_w[mine, :] = (flat_w[mine, :].astype(f32) + flat_w[came, :].astype(f32)).astype(bf16)
        if i + 1 < cube.levels - 1:
            trade_start(g, i + 1)
        else:
            save_last(g)

    def trade_end(g):
        outs["kept", g].wait()
        for half in range(2):
            outs[("last", half), g].wait()

    def trade_sent(g):
        for i in range(1, cube.levels - 1):
            for _, _, item in trades(g, i):
                item.wait_send()

    cot_loads[0].wait()
    first_half(0, during(*[functools.partial(gather, AG2, 1, k) for k in range(1, n)]))
    cot_loads[1].start()
    save_chunk(0)
    line.scatter_sent(ph(RS1, 0), *lands(0))
    second_half(0)
    line.gather_sent(ph(AG2, 0), x_at(0))
    outs["x", 0].wait()
    outs["ul", 0].wait()
    scatter(RS3, 0, 0)
    branch_terms(0)
    save_terms(0)
    outs["hid", 0].wait()
    outs["gl", 0].wait()
    await_terms(0)
    cot_loads[1].wait()
    first_half(1, during(lambda: None, *[functools.partial(scatter, RS3, 0, k) for k in range(1, n - 1)]))
    save_chunk(1)
    line.scatter_sent(ph(RS1, 1), *lands(1))
    second_half(1)
    line.gather_sent(ph(AG2, 1), x_at(1))
    outs["x", 1].wait()
    outs["ul", 1].wait()
    scatter(RS3, 1, 0)
    finish_back(0)
    branch_terms(1)
    save_terms(1)
    outs["hid", 1].wait()
    outs["gl", 1].wait()
    for item in range(1, 4):
        cube.sent(item, block_of(item))
    scatter(RS3, 1, 1)
    gather(AG4, 0, 1)
    start_branch(0)
    await_terms(1)

    def skip():
        pass

    def z_one():
        for k in range(2, n - 1):
            scatter(RS3, 1, k)
        gather(AG4, 0, 2)

    weight_grad(0, during(*[skip] * 6, z_one))
    scatter(RS2, 0, 1)
    weight_grad(1)
    finish_back(1)
    mid_save = pltpu.make_async_copy(mid, mid_out, own_sem.at[5])
    mid_save.start()
    for k in range(3, n):
        gather(AG4, 0, k)
    send_out("branch", 0, x.at[0], branch_out.at[:, 0], 0)
    for k in range(2, n - 1):
        scatter(RS2, 0, k)
    add_first(0)
    gather(AG4, 1, 1)
    weight_grad(2)
    finish_branch(0)
    add_first(1)
    gather(AG4, 1, 2)
    add_first(2)
    for i in range(1, cube.levels - 1):
        add_next(0, i)
    for k in range(3, n):
        gather(AG4, 1, k)
    send_out("branch", 1, x.at[1], branch_out.at[:, 1], 7)
    for g in (1, 2):
        for i in range(1, cube.levels - 1):
            add_next(g, i)
    for g in range(3):
        trade_end(g)
        trade_sent(g)
    first_trade(2).wait_send()
    mid_save.wait()
    line.scatter_sent(ph(RS3, 1), *lands(1))
    for c in range(chunks):
        outs["branch", c].wait()
    for c in range(chunks):
        line.gather_sent(ph(COT, c), cot_at(c))
        line.gather_sent(ph(AG4, c), x_at(c))
        if c == 0:
            line.scatter_sent(ph(RS2, c), *lands(c))


def whole_layer(bounds, gains, live, memory, norm, gate, stream, cot, attn_weights, mlp_weights, tp_size, fsdp_size, collective_id, tile=512):
    chunks = 2
    rows, width = stream.shape
    inner = attn_weights[0].shape[1]
    units = mlp_weights[0].shape[1]
    heads, hd = memory.shape[:2]
    length = rows * tp_size
    c_rows = rows // chunks
    bf, f32 = jnp.bfloat16, jnp.float32
    S = jax.ShapeDtypeStruct
    any_space = pl.BlockSpec(memory_space=pl.ANY)
    vmem = pl.BlockSpec(memory_space=pltpu.VMEM)
    smem = pl.BlockSpec(memory_space=pltpu.SMEM)
    grid_rows = (chunks, tp_size, c_rows)
    flat_rows = (chunks, tp_size * c_rows)
    levels = fsdp_size.bit_length() - 1
    V, DMA = pltpu.VMEM, pltpu.SemaphoreType.DMA
    return pl.pallas_call(
        functools.partial(layer_kernel, chunks=chunks, tp_size=tp_size, fsdp_size=fsdp_size, tile=tile),
        in_specs=[smem] + [vmem] * 5 + [any_space] * 9,
        out_specs=[any_space] * 20 + [vmem] * 6,
        out_shape=[
            S((3, width, units), bf),
            S((width, 4 * inner), bf),
            S((length, width), bf),
            S((length, 3 * inner), bf),
            S((tp_size, chunks, c_rows, inner), bf),
            S((length, inner), f32),
            S(grid_rows + (width,), bf),
            S(grid_rows + (width,), bf),
            S(flat_rows + (units,), bf), S(flat_rows + (units,), bf), S(flat_rows + (units,), bf),
            S(grid_rows + (width,), bf),
            S((rows // chunks, width), bf),
            S((rows, width), f32),
            S((tp_size, chunks, c_rows, width), bf),
            S((3, width // fsdp_size, units), bf),
            S((3, levels - 1, width // 2, units), bf),
            S((length, width), bf),
            S((rows, width), f32),
            S((3, 2, width // fsdp_size // 2, units), bf),
            S((1, width), f32), S((8, 128), f32), S((heads, 1, length), f32), S((heads, hd, hd), f32), S((heads, 1, hd), f32), S((8, width), f32),
        ],
        scratch_shapes=[
            V((3, width, units), bf),
            V(grid_rows + (width,), bf),
            V((tp_size, c_rows, width), bf),
            V(flat_rows[1:] + (units,), bf), V(flat_rows[1:] + (units,), bf), V(flat_rows[1:] + (units,), bf),
            V(grid_rows + (width,), bf),
            V((chunks, tp_size - 1, c_rows, width), bf), V((chunks, tp_size - 1, c_rows, width), bf),
            V((rows, width), bf),
            V((rows, width), f32), V((c_rows, width), f32),
            DMA((9 + chunks,)), DMA((6,)), DMA((max(17, 3 + tp_size + tp_size * chunks),)),
            DMA((2 * tp_size,)), DMA((8 + tp_size,)),
            DMA((3, levels - 1, 2, fsdp_size // 2)), DMA((3, levels - 1, 2, fsdp_size // 2)),
            DMA((levels,)), DMA((levels,)),
            DMA((4, 2, fsdp_size)), DMA((4, 2, fsdp_size)),
            DMA((1 + 6 * chunks, 2, tp_size - 1)), DMA((1 + 6 * chunks, 2, tp_size - 1)),
        ],
        compiler_params=pltpu.CompilerParams(
            collective_id=collective_id, has_side_effects=True, vmem_limit_bytes=60 * 2**20
        ),
        name="layer_kernel",
    )(
        bounds, gains, live, memory, norm.reshape(heads, 1, hd), jnp.broadcast_to(gate[:, None, None], (heads, 1, hd)),
        stream, cot, *attn_weights, *mlp_weights,
    )


def tail_kernel(
    bounds, gains, live_ref, mem_ref, norm_ref, gate_ref, lse_ref, gain_two_ref, stat_ref,
    branch_hbm, attn_hbm, qkv_hbm, mix_hbm, one_hbm, comb_hbm, stream_hbm, all_hbm, gmid_hbm, mid_hbm, terms_hbm, send_hbm,
    grad_out, result_out, land_mlp, land, kept_out,
    dmem_ref, dnorm_ref, sums,
    attn_w, g_ref, spare_ref, rows_ref, one_ref, qkv, dqkv, mixed_ref, gc_ref, part, land_r, land_l, dk_acc, dv_acc,
    sums_land,
    load_sem, out_sem, mlp_send, mlp_recv, sums_send, sums_recv, trade_send, trade_recv, line_send, line_recv,
    *, chunks, tp_size, fsdp_size, tile,
):
    n = tp_size
    bf16, f32 = jnp.bfloat16, jnp.float32
    t, f = lax.axis_index("tp"), lax.axis_index("fsdp")
    c_rows, width = part.shape[2], part.shape[3]
    rows_dev = c_rows * chunks
    length = n * rows_dev
    heads, hd = mem_ref.shape[0], mem_ref.shape[2]
    inner = heads * hd
    shard = width // fsdp_size
    half_rows = shard // 2
    spare = width // 2
    levels, tp_levels = fsdp_size.bit_length() - 1, n.bit_length() - 1
    orders = [[1] + [1 << b for b in range(1, levels)], [1] + [1 << b for b in range(levels - 1, 0, -1)]]
    line = Line(n, line_send, line_recv)
    total, extra = gc_ref.at[0:c_rows, :], gc_ref.at[c_rows : 2 * c_rows, :]
    count = [0]

    def load(src, dst):
        item = pltpu.make_async_copy(src, dst, load_sem.at[count[0]])
        count[0] += 1
        item.start()
        return item

    def peer(bit):
        return lax.bitwise_xor(f, bit)

    def place(s, c):
        return slice(c * n * c_rows + s * c_rows, c * n * c_rows + (s + 1) * c_rows)

    def origin(s, c):
        return slice(s * rows_dev + c * c_rows, s * rows_dev + (c + 1) * c_rows)

    weight_load = load(attn_hbm, attn_w)
    branch_load = load(branch_hbm, rows_ref)
    terms_load = load(terms_hbm.at[chunks - 1], part.at[chunks])
    comb_load = load(comb_hbm, spare_ref.at[:, 0:inner])
    qkv_load = load(qkv_hbm, qkv)
    mix_load = load(mix_hbm, mixed_ref)
    one_loads = [load(one_hbm.at[origin(s, c), :], one_ref.at[place(s, c), :]) for c in range(chunks) for s in range(n)]

    barrier = pltpu.get_barrier_semaphore()
    for k in range(1, n):
        pl.semaphore_signal(barrier, inc=1, device_id={"tp": lax.rem(t + k, n)}, device_id_type=MESH)
    for b in range(levels):
        pl.semaphore_signal(barrier, inc=1, device_id={"fsdp": peer(1 << b)}, device_id_type=MESH)
    pl.semaphore_wait(barrier, n - 1 + levels)

    mlp_trades = [
        pltpu.make_async_remote_copy(
            src_ref=send_hbm.at[g, half],
            dst_ref=land_mlp.at[g, half],
            send_sem=mlp_send.at[g, half],
            recv_sem=mlp_recv.at[g, half],
            device_id={"fsdp": peer(orders[half][-1])},
            device_id_type=MESH,
        )
        for g in range(3)
        for half in range(2)
    ]
    for item in mlp_trades:
        item.start()

    def lands(c):
        return part.at[c], land_r.at[c], land_l.at[c]

    def scatter(c, k):
        line.scatter_step(c, k, *lands(c))

    terms_load.wait()
    scatter(chunks, 0)

    for item in (weight_load, branch_load, comb_load):
        item.wait()

    def store_grad(j, wide, cols, terms):
        for q in range(wide // shard):
            mask = lax.bitwise_xor(j * (wide // shard) + q, f)
            row = lax.rem(mask, 2) * spare + (mask // 2) * shard
            g_ref[pl.ds(pl.multiple_of(row, shard), shard), cols] = terms[q * shard : (q + 1) * shard].astype(bf16)

    wide = 256

    @pl.loop(0, n)
    def _(s):
        rows = pl.ds(pl.multiple_of(s * rows_dev, rows_dev), rows_dev)
        gc_ref[:, pl.ds(pl.multiple_of(s * inner, inner), inner)] = dot32(
            rows_ref[rows, :], attn_w[:, 3 * inner : 4 * inner], NN
        )

    sums[...] = jnp.zeros_like(sums)
    sums[1:2, :] = gain_two_ref[...]
    lane = lax.broadcasted_iota(jnp.int32, (1, width), 1)
    qkv_load.wait()
    mix_load.wait()

    prefix, valid = bounds[0], bounds[1]
    scale = hd ** -0.5

    @pl.loop(0, heads)
    def _(h):
        def lanes(group):
            return pl.ds(pl.multiple_of(group * inner + h * hd, hd), hd)

        gate = jax.nn.sigmoid(gate_ref[h])
        memory, norm = mem_ref[h], norm_ref[h]
        dmem_ref[h] = jnp.zeros((hd, hd), f32)
        dnorm_ref[h] = jnp.zeros((1, hd), f32)
        dgate = jnp.zeros((1, hd), f32)
        for s in range(n - 1, -1, -1):
            first = s * rows_dev
            reach = key_reach(first, rows_dev, length)
            rows = slice(first, first + rows_dev)
            q = qkv[rows, lanes(0)]
            gc = gc_ref[:, pl.ds(pl.multiple_of(s * inner + h * hd, hd), hd)]
            mixed = mixed_ref[rows, lanes(0)]
            qm = mapped(q.astype(f32))
            inverse = 1.0 / jnp.sum(qm * norm, axis=-1, keepdims=True)
            retrieved = dot_three(qm, memory, NN) * inverse
            dgate = dgate + jnp.sum(gc * (retrieved - mixed), axis=0, keepdims=True)
            gnum = gate * gc * inverse
            gden = -jnp.sum(gnum * retrieved, axis=-1, keepdims=True)
            dmem_ref[h] += dot_three(qm, gnum, TN)
            dnorm_ref[h] += jnp.sum(gden * qm, axis=0, keepdims=True)
            dq_mem = (dot_three(gnum, memory, NT) + gden * norm) * jnp.minimum(qm, 1.0)
            low = ((1.0 - gate) * gc).astype(bf16)
            delta = jnp.sum((low.astype(f32) * mixed).T, axis=0, keepdims=True)
            keys = qkv[0:reach, lanes(1)]
            scores = dot32(keys, q, NT) * (scale * LOG2E)
            limit = key_limit(first, rows_dev, prefix, valid)
            scores = jnp.where(
                lax.broadcasted_iota(jnp.int32, scores.shape, 0) <= limit, scores - lse_ref[h, :, rows], NEG
            )
            probs = jnp.exp2(scores)
            gp = dot32(qkv[0:reach, lanes(2)], low, NT)
            gs = (probs * (gp - delta)).astype(bf16)
            dv = dot32(probs.astype(bf16), low, NN)
            dk = dot32(gs, q, NN)
            if s == n - 1:
                dv_acc[...] = dv
                dk_acc[...] = dk
            else:
                dv_acc[0:reach, :] += dv
                dk_acc[0:reach, :] += dk
            dq = (dot32(keys, gs, TN).T * scale + dq_mem).astype(bf16)
            for c in range(chunks):
                dqkv[place(s, c), lanes(0)] = dq[c * c_rows : (c + 1) * c_rows]
        for s in range(n):
            for c in range(chunks):
                dqkv[place(s, c), lanes(1)] = (dk_acc[origin(s, c), :] * scale).astype(bf16)
                dqkv[place(s, c), lanes(2)] = dv_acc[origin(s, c), :].astype(bf16)
        dgate_sum = jnp.sum(dgate * (gate * (1.0 - gate)), axis=-1, keepdims=True)
        sums[2:3, :] += jnp.where(lane == t * heads + h, dgate_sum, 0.0)
        for k in range(1, n - 1):
            @pl.when(h == k)
            def _():
                scatter(chunks, k)

    @pl.loop(0, width // wide)
    def _(j):
        cols = pl.ds(pl.multiple_of(j * wide, wide), wide)
        store_grad(j, wide, slice(3 * inner, 4 * inner), dot32(rows_ref[:, cols], spare_ref[:, 0:inner], TN))

    all_loads = [load(all_hbm.at[origin(s, c), :], rows_ref.at[place(s, c), :]) for c in range(chunks) for s in range(n)]
    for item in all_loads:
        item.wait()

    for c in range(chunks):
        here = slice(c * n * c_rows, (c + 1) * n * c_rows)
        inverse_all = inverse_rms(rows_ref[here, :].astype(f32))
        flat = part.at[c].reshape(n * c_rows, width)

        @pl.loop(0, width // tile)
        def _(j):
            cols = pl.ds(pl.multiple_of(j * tile, tile), tile)
            terms = dot32(dqkv[here, :], attn_w[cols, 0 : 3 * inner], NT)
            flat[:, cols] = terms.astype(bf16)
            unit = rows_ref[here, cols].astype(f32) * inverse_all
            sums[0:1, cols] += jnp.sum(terms * unit, axis=0, keepdims=True)

        scatter(c, 0)

    own_rows = slice(rows_dev - c_rows, rows_dev)
    mid_load = load(mid_hbm.at[own_rows, :], extra)
    line.scatter_end(chunks, *lands(chunks), total)
    mid_load.wait()

    def by_piece(work):
        @pl.loop(0, c_rows // PIECE)
        def _(r):
            work(pl.ds(pl.multiple_of(r * PIECE, PIECE), PIECE), r * PIECE)

    def close_branch(piece, first):
        branch = total[piece, :]
        result = extra[piece, :] + branch
        live = live_ref[pl.ds(pl.multiple_of(rows_dev - c_rows + first, PIECE), PIECE), :]
        part[chunks, t, piece, :] = result.astype(bf16)
        values = (result, branch)
        for at, value in zip((0, 2), values):
            squares = jnp.sum(jnp.sum(value * value, axis=-1, keepdims=True) * live, axis=0, keepdims=True)
            sums[3:4, :] += jnp.where(lane == 3 * f + at, squares, 0.0)

    by_piece(close_branch)
    result_save = pltpu.make_async_copy(part.at[chunks, t], result_out, out_sem.at[0])
    result_save.start()
    for at, row in enumerate((1, 0, 2)):
        sums[3:4, :] += jnp.where(lane == 3 * f + at, stat_ref[row : row + 1, 0:1], 0.0)

    def sums_step(at):
        target = {"fsdp": peer(1 << at)} if at < levels else {"tp": lax.bitwise_xor(t, 1 << (at - levels))}
        return pltpu.make_async_remote_copy(
            src_ref=sums,
            dst_ref=sums_land.at[at],
            send_sem=sums_send.at[at],
            recv_sem=sums_recv.at[at],
            device_id=target,
            device_id_type=MESH,
        )

    def sums_add(at):
        sums_step(at).wait()
        sums[...] += sums_land[at]

    sums_step(0).start()

    for item in one_loads:
        item.wait()

    @pl.loop(0, width // wide)
    def _(j):
        cols = pl.ds(pl.multiple_of(j * wide, wide), wide)
        store_grad(j, wide, slice(0, 3 * inner), dot32(one_ref[:, cols], dqkv[...], TN))

    first_trade = pltpu.make_async_remote_copy(
        src_ref=g_ref.at[spare : 2 * spare, :],
        dst_ref=land.at[0],
        send_sem=trade_send.at[0, 0, 0],
        recv_sem=trade_recv.at[0, 0, 0],
        device_id={"fsdp": peer(1)},
        device_id_type=MESH,
    )
    first_trade.start()

    def trades(i):
        for half in range(2):
            order = orders[half]
            bit = order[i]
            for mask in range(fsdp_size):
                if all(mask & b == 0 for b in order[: i + 1]):
                    there = (mask // 2) * shard + half * half_rows
                    here = ((mask ^ bit) // 2) * shard + half * half_rows
                    yield there, pltpu.make_async_remote_copy(
                        src_ref=g_ref.at[here : here + half_rows, :],
                        dst_ref=land.at[i, there : there + half_rows, :],
                        send_sem=trade_send.at[i, half, mask // 2],
                        recv_sem=trade_recv.at[i, half, mask // 2],
                        device_id={"fsdp": peer(bit)},
                        device_id_type=MESH,
                    )

    def add_rows(mine, came):
        g_ref[mine, :] = (g_ref[mine, :].astype(f32) + spare_ref[came, :].astype(f32)).astype(bf16)

    scatter(0, 1)
    sums_add(0)
    sums_step(1).start()
    scatter(1, 1)
    first_trade.wait_recv()
    first_load = load(land.at[0], spare_ref)
    first_load.wait()

    @pl.loop(0, spare // half_rows)
    def _(r):
        rows = pl.ds(pl.multiple_of(r * half_rows, half_rows), half_rows)
        add_rows(rows, rows)

    for _, item in trades(1):
        item.start()
    for k in range(2, n - 1):
        scatter(0, k)
    sums_add(1)
    sums_step(2).start()

    one_gain = gains[0:1, :]

    def finish(c):
        rows = slice(c * c_rows, (c + 1) * c_rows)
        gmid_load = load(gmid_hbm.at[rows, :], extra)
        stream_load = load(stream_hbm.at[rows, :], part.at[chunks, 0])
        line.scatter_end(c, *lands(c), total)
        gmid_load.wait()
        stream_load.wait()

        def close(piece, first):
            v = part[chunks, 0, piece, :].astype(f32)
            inv = inverse_rms(v)
            u = v * inv
            e = total[piece, :] * one_gain
            total[piece, :] = extra[piece, :] + inv * (e - u * jnp.mean(e * u, axis=-1, keepdims=True))

        by_piece(close)
        save = pltpu.make_async_copy(total, grad_out.at[rows, :], out_sem.at[1])
        save.start()
        save.wait()

    result_save.wait()
    line.scatter_sent(chunks, *lands(chunks))
    for at in range(2, levels):
        sums_add(at)
        sums_step(at + 1).start()
    for k in range(2, n - 1):
        scatter(1, k)
    for i in range(1, levels - 1):
        arrived = list(trades(i))
        loads = []
        for there, item in arrived:
            item.wait_recv()
            loads.append(load(land.at[i, there : there + half_rows, :], spare_ref.at[there : there + half_rows, :]))
        for item in loads:
            item.wait()
        for there, _ in arrived:
            rows = slice(there, there + half_rows)
            add_rows(rows, rows)
        for _, item in trades(i + 1):
            item.start()
    kept_save = pltpu.make_async_copy(g_ref.at[0:shard, :], kept_out, out_sem.at[2])
    kept_save.start()
    finish(0)
    for at in range(levels, levels + tp_levels):
        sums_add(at)
        if at + 1 < levels + tp_levels:
            sums_step(at + 1).start()
    finish(1)
    for _, item in trades(levels - 1):
        item.wait_recv()
    kept_save.wait()
    for item in mlp_trades:
        item.wait()
    first_trade.wait_send()
    for i in range(1, levels):
        for _, item in trades(i):
            item.wait_send()
    for c in range(chunks):
        line.scatter_sent(c, *lands(c))


def whole_tail(
    bounds, gains, live, memory, norm, gate, lse, gain_two, stat,
    branch, attn_full, qkv, mix, flat_one, comb, stream, stream_all, gmid, mid, terms, to_send, tp_size, fsdp_size, collective_id, tile=512,
):
    chunks = 2
    rows, width = stream.shape
    length = rows * tp_size
    c_rows = rows // chunks
    heads, hd = memory.shape[:2]
    inner = heads * hd
    units = to_send.shape[-1]
    shard = width // fsdp_size
    levels, tp_levels = fsdp_size.bit_length() - 1, tp_size.bit_length() - 1
    bf, f32 = jnp.bfloat16, jnp.float32
    S, V, DMA = jax.ShapeDtypeStruct, pltpu.VMEM, pltpu.SemaphoreType.DMA
    any_space = pl.BlockSpec(memory_space=pl.ANY)
    vmem = pl.BlockSpec(memory_space=pltpu.VMEM)
    smem = pl.BlockSpec(memory_space=pltpu.SMEM)
    adds = sum(2 * (fsdp_size >> (i + 1)) for i in range(1, levels - 1))
    loads = 6 + 2 * length // c_rows + 2 + 4 + adds
    return pl.pallas_call(
        functools.partial(tail_kernel, chunks=chunks, tp_size=tp_size, fsdp_size=fsdp_size, tile=tile),
        in_specs=[smem] + [vmem] * 8 + [any_space] * 12,
        out_specs=[any_space] * 5 + [vmem] * 3,
        out_shape=[
            S((rows, width), f32),
            S((c_rows, width), bf),
            S(to_send.shape, bf),
            S((levels, width // 2, 4 * inner), bf),
            S((shard, 4 * inner), bf),
            S((heads, hd, hd), f32), S((heads, 1, hd), f32), S((8, width), f32),
        ],
        scratch_shapes=[
            V((width, 4 * inner), bf),
            V((width, 4 * inner), bf),
            V((width // 2, 4 * inner), bf),
            V((length, width), bf),
            V((length, width), bf),
            V((length, 3 * inner), bf), V((length, 3 * inner), bf),
            V((length, inner), f32), V((rows, tp_size * inner), f32),
            V((chunks + 1, tp_size, c_rows, width), bf),
            V((chunks + 1, tp_size - 1, c_rows, width), bf), V((chunks + 1, tp_size - 1, c_rows, width), bf),
            V((length, hd), f32), V((length, hd), f32),
            V((levels + tp_levels, 8, width), f32),
            DMA((loads,)), DMA((3,)),
            DMA((3, 2)), DMA((3, 2)),
            DMA((levels + tp_levels,)), DMA((levels + tp_levels,)),
            DMA((levels, 2, fsdp_size // 2)), DMA((levels, 2, fsdp_size // 2)),
            DMA((chunks + 1, 2, tp_size - 1)), DMA((chunks + 1, 2, tp_size - 1)),
        ],
        compiler_params=pltpu.CompilerParams(
            collective_id=collective_id, has_side_effects=True, vmem_limit_bytes=60 * 2**20
        ),
        name="tail_kernel",
    )(
        bounds, gains, live, memory, norm.reshape(heads, 1, hd), jnp.broadcast_to(gate[:, None, None], (heads, 1, hd)),
        lse, gain_two, stat, branch, attn_full, qkv, mix, flat_one, comb, stream, stream_all, gmid, mid, terms, to_send,
    )


def on_device(
    stream,
    attn_gain,
    w_query,
    w_key,
    w_value,
    w_out,
    mem_gate,
    mlp_gain,
    w_gate,
    w_up,
    w_down,
    memory,
    normalizer,
    prefix,
    valid,
    cotangent,
):
    f32, bf16 = jnp.float32, jnp.bfloat16
    len_dev, width = (stream.shape[1], stream.shape[2])
    tp_size, fsdp_size = lax.axis_size("tp"), lax.axis_size("fsdp")
    tp_here, seq_here = lax.axis_index("tp"), lax.axis_index("fsdp")
    seq_len = len_dev * tp_size
    heads_here = mem_gate.shape[0]
    prefix_len = prefix[seq_here]
    valid_len = valid[seq_here]
    stream, cotangent = stream[0], cotangent[0]

    shard = width // fsdp_size
    gains = jnp.zeros((8, width), f32)
    gains = lax.dynamic_update_slice(
        gains, jnp.stack([attn_gain, mlp_gain]).astype(f32), (0, seq_here * shard)
    )
    bounds = jnp.stack([prefix_len, valid_len])
    local_position = tp_here * len_dev + jnp.arange(len_dev, dtype=jnp.int32)
    live_here = (local_position < valid_len).astype(f32)[:, None]
    (
        _, attn_full, flat_one, qkv_rows, combined, local_mix, _, _, _, _, _, mlp_terms,
        first_out, grad_middle, branch_low, kept, _, stream_all, middle_rows, to_send,
        gain_two_terms, stats, log_total, memory_next, normalizer_next, gains,
    ) = whole_layer(
        bounds, gains, live_here, memory[0], normalizer[0], mem_gate, stream, cotangent,
        (w_query, w_key, w_value, w_out), (w_gate, w_up, w_down), tp_size, fsdp_size, 1,
    )
    inner = w_query.shape[1]
    stream_grad, second_out, landed, attn_landed, attn_kept, grad_memory, grad_normalizer, joined = whole_tail(
        bounds, gains, live_here, memory[0], normalizer[0], mem_gate, log_total, gain_two_terms, stats,
        branch_low.reshape(seq_len, width), attn_full, qkv_rows, local_mix, flat_one, combined.reshape(seq_len, inner),
        stream, stream_all, grad_middle, middle_rows, mlp_terms, to_send, tp_size, fsdp_size, 2,
    )
    stream_out = jnp.concatenate([first_out, second_out], axis=0)
    gate_grad, up_grad, down_grad = (
        kept[g].astype(f32) + landed[g].reshape(shard, -1).astype(f32) for g in range(3)
    )
    query_grad, key_grad, value_grad, out_grad = (
        attn_kept[:, p * inner : (p + 1) * inner].astype(f32)
        + attn_landed[-1, :shard, p * inner : (p + 1) * inner].astype(f32)
        for p in range(4)
    )
    gain_one_grad = lax.dynamic_slice(joined, (0, seq_here * shard), (1, shard))[0]
    gain_two_grad = lax.dynamic_slice(joined, (1, seq_here * shard), (1, shard))[0]
    gate_grad_logit = lax.dynamic_slice(joined, (2, tp_here * heads_here), (1, heads_here))[0]
    stat_sums = lax.dynamic_slice(joined, (3, seq_here * 3), (1, 3))
    token_count = valid_len.astype(f32) * width
    rms_stats = jnp.sqrt(stat_sums / token_count + rms_eps)
    return (
        stream_out[None],
        stream_grad[None],
        gain_one_grad,
        query_grad,
        key_grad,
        value_grad,
        out_grad,
        gate_grad_logit,
        gain_two_grad,
        gate_grad,
        up_grad,
        down_grad,
        memory_next[None],
        normalizer_next[:, 0][None],
        grad_memory[None],
        grad_normalizer[:, 0][None],
        rms_stats,
    )


def solution(mesh):
    placed = (
        P("fsdp", "tp", None),
        P("fsdp"),
        P("fsdp", "tp"),
        P("fsdp", "tp"),
        P("fsdp", "tp"),
        P("fsdp", "tp"),
        P("tp"),
        P("fsdp"),
        P("fsdp", "tp"),
        P("fsdp", "tp"),
        P("fsdp", "tp"),
        P("fsdp", "tp", None, None),
        P("fsdp", "tp", None),
        P(),
        P(),
        P("fsdp", "tp", None),
    )
    return jax.shard_map(
        on_device,
        mesh=mesh,
        in_specs=placed,
        out_specs=(
            P("fsdp", "tp", None),
            P("fsdp", "tp", None),
            P("fsdp"),
            P("fsdp", "tp"),
            P("fsdp", "tp"),
            P("fsdp", "tp"),
            P("fsdp", "tp"),
            P("tp"),
            P("fsdp"),
            P("fsdp", "tp"),
            P("fsdp", "tp"),
            P("fsdp", "tp"),
            P("fsdp", "tp", None, None),
            P("fsdp", "tp", None),
            P("fsdp", "tp", None, None),
            P("fsdp", "tp", None),
            P("fsdp", None),
        ),
        check_vma=False,
    )
```

```python
import functools

import jax
import jax.numpy as jnp
from jax import lax
from jax.experimental import pallas as pl
from jax.experimental.pallas import tpu as pltpu
from jax.sharding import PartitionSpec as P

rms_eps = 1e-06
NEG = -1e30
LOG2E = 1.4426950408889634


def split_two(x):
    high = x.astype(jnp.bfloat16)
    return high, (x - high.astype(jnp.float32)).astype(jnp.bfloat16)


def dot32(a, b, dims):
    return lax.dot_general(a, b, (dims, ((), ())), preferred_element_type=jnp.float32)


def dot_three(a, b, dims):
    ah, al = split_two(a)
    bh, bl = split_two(b)
    return dot32(ah, bh, dims) + dot32(ah, bl, dims) + dot32(al, bh, dims)


NN, NT, TN = ((1,), (0,)), ((1,), (1,)), ((0,), (0,))


def mapped(v):
    return jnp.where(v > 0, v + 1.0, jnp.exp(jnp.minimum(v, 0.0)))


def key_reach(first, rows, keys):
    return min(keys, max(keys // 2, first + rows))


def key_limit(first, rows, prefix, valid):
    row = first + lax.broadcasted_iota(jnp.int32, (1, rows), 1)
    return jnp.minimum(valid - 1, jnp.maximum(row, prefix - 1))


norm_eps = 1e-06
MESH = pl.DeviceIdType.MESH
RIGHT, LEFT = 0, 1
PIECE = 32


class Line:
    def __init__(self, size, send_sem, recv_sem):
        self.size, self.send_sem, self.recv_sem = size, send_sem, recv_sem
        self.here = lax.axis_index("tp")

    def copy(self, phase, way, slot, src, dst):
        to = self.here + 1 if way == RIGHT else self.here - 1
        return pltpu.make_async_remote_copy(
            src_ref=src,
            dst_ref=dst,
            send_sem=self.send_sem.at[phase, way, slot],
            recv_sem=self.recv_sem.at[phase, way, slot],
            device_id={"tp": to},
            device_id_type=MESH,
        )

    def arrived(self, phase, way, slot, dst):
        self.copy(phase, way, slot, dst, dst).wait_recv()

    def scatter_step(self, phase, step, part, land_right, land_left):
        n, t = self.size, self.here

        def pass_on(way, slot, shard, land, first):
            @pl.when(jnp.logical_not(first))
            def _():
                self.arrived(phase, way, slot, land)

                @pl.loop(0, part.shape[1] // PIECE)
                def _(r):
                    rows = pl.ds(pl.multiple_of(r * PIECE, PIECE), PIECE)
                    came = land[rows, :].astype(jnp.float32)
                    part[shard, rows, :] = (part[shard, rows, :].astype(jnp.float32) + came).astype(part.dtype)

            self.copy(phase, way, slot, part.at[shard], land).start()

        right, left = step - t, step - (n - 1 - t)
        far, near = n - 1 - right, left

        @pl.when((right >= 0) & (far > t))
        def _():
            pass_on(RIGHT, right, far, land_right.at[far - 1], t == 0)

        @pl.when((left >= 0) & (near < t))
        def _():
            pass_on(LEFT, left, near, land_left.at[near], t == n - 1)

    def scatter_end(self, phase, part, land_right, land_left, total):
        n, t = self.size, self.here

        def over(work):
            @pl.loop(0, part.shape[1] // PIECE)
            def _(r):
                work(pl.ds(pl.multiple_of(r * PIECE, PIECE), PIECE))

        def own(rows):
            total[rows, :] = part[t, rows, :].astype(jnp.float32)

        def from_left(rows):
            total[rows, :] += land_right[t - 1, rows, :].astype(jnp.float32)

        def from_right(rows):
            total[rows, :] += land_left[t, rows, :].astype(jnp.float32)

        over(own)

        @pl.when(t > 0)
        def _():
            self.arrived(phase, RIGHT, n - 1 - t, land_right.at[t - 1])
            over(from_left)

        @pl.when(t < n - 1)
        def _():
            self.arrived(phase, LEFT, t, land_left.at[t])
            over(from_right)

    def scatter_sent(self, phase, part, land_right, land_left):
        n, t = self.size, self.here
        for k in range(n - 1):
            far, near = n - 1 - k, k

            @pl.when(t < far)
            def _():
                self.copy(phase, RIGHT, k, part.at[far], land_right.at[far - 1]).wait_send()

            @pl.when(t > near)
            def _():
                self.copy(phase, LEFT, k, part.at[near], land_left.at[near]).wait_send()

    def gather_step(self, phase, k, shard_at):
        n, t = self.size, self.here

        @pl.when(t >= k)
        def _():
            shard = shard_at(t - k)
            if k > 0:
                self.arrived(phase, RIGHT, k - 1, shard)
            if k < n - 1:
                @pl.when(t < n - 1)
                def _():
                    self.copy(phase, RIGHT, k, shard, shard).start()

        @pl.when(t + k <= n - 1)
        def _():
            shard = shard_at(t + k)
            if k > 0:
                self.arrived(phase, LEFT, k - 1, shard)
            if k < n - 1:
                @pl.when(t > 0)
                def _():
                    self.copy(phase, LEFT, k, shard, shard).start()

    def gather_sent(self, phase, shard_at):
        n, t = self.size, self.here
        for k in range(n - 1):
            @pl.when((t >= k) & (t < n - 1))
            def _():
                self.copy(phase, RIGHT, k, shard_at(t - k), shard_at(t - k)).wait_send()

            @pl.when((t + k <= n - 1) & (t > 0))
            def _():
                self.copy(phase, LEFT, k, shard_at(t + k), shard_at(t + k)).wait_send()


class Cube:
    def __init__(self, size, send_sem, recv_sem):
        self.size, self.send_sem, self.recv_sem = size, send_sem, recv_sem
        self.here = lax.axis_index("fsdp")
        self.levels = size.bit_length() - 1
        ups = [1 << b for b in range(1, self.levels)]
        self.orders = [ups[::-1] + [1], ups + [1]]

    def peer(self, bit):
        return lax.bitwise_xor(self.here, bit)

    def held(self, half, stage):
        masks = [0]
        for bit in self.orders[half][:stage]:
            masks += [mask ^ bit for mask in masks]
        return masks

    def copy(self, item, half, mask, bit, block_at):
        owner = self.peer(mask) if mask else self.here
        block = block_at(owner, half)
        return pltpu.make_async_remote_copy(
            src_ref=block,
            dst_ref=block,
            send_sem=self.send_sem.at[item, half, mask ^ bit],
            recv_sem=self.recv_sem.at[item, half, mask ^ bit],
            device_id={"fsdp": self.peer(bit)},
            device_id_type=MESH,
        )

    def await_stage(self, item, stage, block_at):
        for half in range(2):
            bit = self.orders[half][stage]
            for mask in self.held(half, stage):
                block = block_at(self.peer(mask ^ bit), half)
                pltpu.make_async_remote_copy(
                    src_ref=block,
                    dst_ref=block,
                    send_sem=self.send_sem.at[item, half, mask ^ bit],
                    recv_sem=self.recv_sem.at[item, half, mask ^ bit],
                    device_id={"fsdp": self.peer(bit)},
                    device_id_type=MESH,
                ).wait_recv()

    def stage(self, item, stage, block_at):
        if stage > 0:
            self.await_stage(item, stage - 1, block_at)
        if stage == self.levels:
            return
        for half in range(2):
            bit = self.orders[half][stage]
            for mask in self.held(half, stage):
                self.copy(item, half, mask, bit, block_at).start()

    def sent(self, item, block_at):
        for stage in range(self.levels):
            for half in range(2):
                bit = self.orders[half][stage]
                for mask in self.held(half, stage):
                    self.copy(item, half, mask, bit, block_at).wait_send()


GELU_A, GELU_B = 0.7978845608028654, 0.044715


def gelu_pair(v):
    square = v * v
    curve = jnp.tanh(v * (GELU_A + GELU_A * GELU_B * square))
    half = 0.5 + 0.5 * curve
    slope = half + (0.5 * v) * (1.0 - curve * curve) * (GELU_A + 3.0 * GELU_A * GELU_B * square)
    return v * half, slope


def inverse_rms(v):
    return lax.rsqrt(jnp.mean(v * v, axis=-1, keepdims=True) + norm_eps)


def layer_kernel(
    bounds, gain_in, live_ref, mem_ref, norm_ref, gate_ref,
    stream_hbm, cot_hbm, wq_hbm, wk_hbm, wv_hbm, wo_hbm, wg_hbm, wu_hbm, wd_hbm,
    mlp_hbm, attn_out, one_out, qkv_out, comb_out, mix_out, cot_all, x_out, hid_out, gl_out, ul_out, terms_hbm,
    result_out, gmid_out, branch_out, kept_out, land, all_out, mid_out, to_send,
    ggain_ref, stat_ref, lse_ref, memo_ref, normo_ref, gain,
    w_three, x, cot, hid, gl, ul, part, land_r, land_l, stream, mid, total,
    own_sem, load_sem, out_sem, term_sem, grad_sem, trade_send, trade_recv, gain_send, gain_recv, cube_send, cube_recv, line_send, line_recv,
    *, chunks, tp_size, fsdp_size, tile,
):
    n = tp_size
    bf16, f32 = jnp.bfloat16, jnp.float32
    t, f = lax.axis_index("tp"), lax.axis_index("fsdp")
    c_rows, width = x.shape[2], x.shape[3]
    units = hid.shape[1]
    rows_dev = stream.shape[0]
    length = rows_dev * n
    heads, hd = mem_ref.shape[0], mem_ref.shape[2]
    inner = heads * hd
    shard = width // fsdp_size
    line = Line(n, line_send, line_recv)
    cube = Cube(fsdp_size, cube_send, cube_recv)
    bits = [1 << b for b in range(cube.levels)]
    AG1 = 0

    def ph(kind, c):
        return 1 + kind * chunks + c

    COT, RS1, AG2, RS3, AG4, RS2 = range(6)

    attn_w = w_three.at[0]
    qkv = w_three.at[1]
    flat_one = w_three.at[2]

    def stream_at(s):
        return w_three.at[2, pl.ds(pl.multiple_of(length + s * rows_dev, rows_dev), rows_dev), :]

    def x_at(c):
        return lambda s: x.at[c, s]

    def cot_at(c):
        return lambda s: cot_all.at[c, s]

    def lands(c):
        return part.at[c], land_r.at[c], land_l.at[c]

    def block_of(item):
        whole = attn_w if item == 0 else mlp_hbm.at[item - 1]

        def at(owner, half):
            rows = shard // 2
            return whole.at[pl.ds(pl.multiple_of(owner * shard + half * rows, rows), rows), :]

        return at

    def push(item, stage):
        cube.stage(item, stage, block_of(item))

    own_rows = pl.ds(pl.multiple_of(f * shard, shard), shard)
    own = [
        pltpu.make_async_copy(w, w_three.at[0, own_rows, p * inner : (p + 1) * inner], own_sem.at[p])
        for p, w in enumerate((wq_hbm, wk_hbm, wv_hbm, wo_hbm))
    ]
    own += [pltpu.make_async_copy(stream_hbm, stream_at(t), own_sem.at[4]), pltpu.make_async_copy(stream_hbm, stream, own_sem.at[5])]
    homes = [hid.at[0:shard, :], hid.at[shard : 2 * shard, :], gl.at[0:shard, :]]
    own += [pltpu.make_async_copy(w, homes[m], own_sem.at[6 + m]) for m, w in enumerate((wg_hbm, wu_hbm, wd_hbm))]
    own.append(pltpu.make_async_copy(cot_hbm, ul.at[0:rows_dev, :], own_sem.at[9]))
    placed = [pltpu.make_async_copy(homes[m], mlp_hbm.at[m, own_rows, :], own_sem.at[6 + m]) for m in range(3)]
    placed += [
        pltpu.make_async_copy(ul.at[c * c_rows : (c + 1) * c_rows, :], cot_all.at[c, t], own_sem.at[9 + c])
        for c in range(chunks)
    ]
    for item in own:
        item.start()
    gain[...] = gain_in[...]
    ggain_ref[...] = jnp.zeros_like(ggain_ref)
    stat_ref[...] = jnp.zeros_like(stat_ref)

    barrier = pltpu.get_barrier_semaphore()

    @pl.when(t > 0)
    def _():
        pl.semaphore_signal(barrier, inc=1, device_id={"tp": t - 1}, device_id_type=MESH)

    @pl.when(t < n - 1)
    def _():
        pl.semaphore_signal(barrier, inc=1, device_id={"tp": t + 1}, device_id_type=MESH)

    for bit in bits:
        pl.semaphore_signal(barrier, inc=1, device_id={"fsdp": cube.peer(bit)}, device_id_type=MESH)
    peers = (t > 0).astype(jnp.int32) + (t < n - 1).astype(jnp.int32) + len(bits)
    pl.semaphore_wait(barrier, peers)

    for item in own[:6]:
        item.wait()
    push(0, 0)
    line.gather_step(AG1, 0, stream_at)
    for item in own[6:]:
        item.wait()
    for item in placed:
        item.start()
    for level, bit in enumerate(bits):
        trade = pltpu.make_async_remote_copy(
            src_ref=gain,
            dst_ref=total.at[8 * level : 8 * level + 8, :],
            send_sem=gain_send.at[level],
            recv_sem=gain_recv.at[level],
            device_id={"fsdp": cube.peer(bit)},
            device_id_type=MESH,
        )
        trade.start()
        trade.wait()
        gain[...] += total[8 * level : 8 * level + 8, :]
    for item in placed:
        item.wait()

    def norm_one(s):
        raw = stream_at(s)

        @pl.loop(0, rows_dev // PIECE)
        def _(r):
            v = raw[pl.ds(pl.multiple_of(r * PIECE, PIECE), PIECE), :].astype(f32)
            flat_one[pl.ds(pl.multiple_of(s * rows_dev + r * PIECE, PIECE), PIECE), :] = (
                v * inverse_rms(v) * gain[0:1, :]
            ).astype(bf16)

    def project_one(s):
        rows = pl.ds(pl.multiple_of(s * rows_dev, rows_dev), rows_dev)

        @pl.loop(0, 3)
        def _(p):
            cols = pl.ds(pl.multiple_of(p * inner, inner), inner)
            qkv[rows, cols] = dot32(flat_one[rows, :], attn_w[:, cols], NN).astype(bf16)

    def arrived_pair(k, work):
        @pl.when(t >= k)
        def _():
            work(t - k)

        @pl.when(t + k <= n - 1)
        def _():
            work(t + k)

    norm_one(t)
    push(0, 1)
    push(1, 0)
    line.gather_step(AG1, 1, stream_at)
    for stage in range(2, cube.levels):
        push(0, stage)
    arrived_pair(1, norm_one)
    push(0, cube.levels)
    attn_save = pltpu.make_async_copy(attn_w, attn_out, out_sem.at[0])
    attn_save.start()
    project_one(t)
    push(1, 1)
    push(2, 0)
    line.gather_step(AG1, 2, stream_at)
    arrived_pair(1, project_one)

    def both(s):
        norm_one(s)
        project_one(s)

    for k in range(2, n):
        if k > 2:
            line.gather_step(AG1, k, stream_at)
        if k == n - 1:
            for c in range(chunks):
                line.gather_step(ph(COT, c), 0, cot_at(c))
        arrived_pair(k, both)
    one_save = pltpu.make_async_copy(flat_one.at[0:length, :], one_out, out_sem.at[1])
    one_save.start()
    all_save = pltpu.make_async_copy(flat_one.at[length : 2 * length, :], all_out, own_sem.at[4])
    all_save.start()
    qkv_save = pltpu.make_async_copy(qkv.at[0:length, 0 : 3 * inner], qkv_out, out_sem.at[2])
    qkv_save.start()
    for stage in range(2, cube.levels):
        push(1, stage)
    push(2, 1)
    push(3, 0)
    push(1, cube.levels)

    prefix, valid = bounds[0], bounds[1]
    score_scale = hd ** -0.5 * LOG2E

    def attend_rows(s):
        first = s * rows_dev
        reach = key_reach(first, rows_dev, length)
        limit = key_limit(first, rows_dev, prefix, valid)

        @pl.loop(0, heads)
        def _(h):
            def lanes(group):
                return pl.ds(pl.multiple_of(group * inner + h * hd, hd), hd)

            q = qkv[first : first + rows_dev, lanes(0)]
            scores = dot32(qkv[0:reach, lanes(1)], q, NT) * score_scale
            scores = jnp.where(lax.broadcasted_iota(jnp.int32, scores.shape, 0) <= limit, scores, NEG)
            top = jnp.max(scores, axis=0, keepdims=True)
            probs = jnp.exp2(scores - top)
            row_total = jnp.sum(probs, axis=0, keepdims=True)
            mixed = (dot32(qkv[0:reach, lanes(2)], probs.astype(bf16), TN) / row_total).T
            lse_ref[h, :, first : first + rows_dev] = top + jnp.log2(row_total)
            gate = jax.nn.sigmoid(gate_ref[h])
            qm = mapped(q.astype(f32))
            denominator = jnp.sum(qm * norm_ref[h], axis=-1, keepdims=True)
            retrieved = dot_three(qm, mem_ref[h], NN) / denominator
            mid[:, pl.ds(pl.multiple_of(s * inner + h * hd, hd), hd)] = mixed
            both_mix = (gate * retrieved + (1.0 - gate) * mixed).astype(bf16)
            for c in range(chunks):
                hid[s * c_rows : (s + 1) * c_rows, pl.ds(pl.multiple_of(c * inner + h * hd, hd), hd)] = both_mix[
                    c * c_rows : (c + 1) * c_rows
                ]

    def update_memory():
        @pl.loop(0, heads)
        def _(h):
            km = mapped(qkv[0:length, pl.ds(pl.multiple_of(inner + h * hd, hd), hd)].astype(f32))
            km = jnp.where(lax.broadcasted_iota(jnp.int32, km.shape, 0) < valid, km, 0.0)
            kh, kl = split_two(km)
            values = qkv[0:length, pl.ds(pl.multiple_of(2 * inner + h * hd, hd), hd)]
            memo_ref[h] = mem_ref[h] + dot32(kh, values, TN) + dot32(kl, values, TN)
            normo_ref[h] = norm_ref[h] + jnp.sum(km, axis=0, keepdims=True)

    for s in range(n):
        attend_rows(s)
        if s == n - 2:
            line.gather_step(ph(COT, 0), 1, cot_at(0))
    for stage in range(2, cube.levels):
        push(2, stage)
    comb_saves = []
    for s in range(n):
        comb_saves.append(
            pltpu.make_async_copy(mid.at[:, s * inner : (s + 1) * inner], mix_out.at[s * rows_dev : (s + 1) * rows_dev, :], out_sem.at[3 + s])
        )
        for c in range(chunks):
            comb_saves.append(
                pltpu.make_async_copy(
                    hid.at[s * c_rows : (s + 1) * c_rows, c * inner : (c + 1) * inner],
                    comb_out.at[s, c],
                    out_sem.at[3 + n + s * chunks + c],
                )
            )
    for item in comb_saves:
        item.start()

    def project(c):
        flat = part.at[c].reshape(n * c_rows, width)

        @pl.loop(0, width // tile)
        def _(j):
            cols = pl.ds(pl.multiple_of(j * tile, tile), tile)
            flat[:, cols] = dot32(
                hid[:, c * inner : (c + 1) * inner], attn_w[cols, 3 * inner : 4 * inner], NT
            ).astype(bf16)

    def by_piece(c, work):
        @pl.loop(0, c_rows // PIECE)
        def _(r):
            piece = pl.ds(pl.multiple_of(r * PIECE, PIECE), PIECE)
            work(piece, pl.ds(pl.multiple_of(c * c_rows + r * PIECE, PIECE), PIECE))

    def square_sum(v, live):
        return jnp.sum(jnp.sum(v * v, axis=-1, keepdims=True) * live, axis=0, keepdims=True)

    def norm_two(c):
        def work(piece, rows):
            branch = total[piece, :]
            stat_ref[0:1, :] += square_sum(branch, live_ref[rows, :])
            m = stream[rows, :].astype(f32) + branch
            mid[rows, :] = m
            x[c, t, piece, :] = (m * inverse_rms(m) * gain[1:2, :]).astype(bf16)

        by_piece(c, work)

    def first_half(c, service):
        flat = x.at[c].reshape(n * c_rows, width)
        cot_flat = cot.reshape(n * c_rows, width)

        @pl.loop(0, units // tile)
        def _(j):
            cols = pl.ds(pl.multiple_of(j * tile, tile), tile)
            gate_pre = dot32(flat[...], w_three[0, :, cols], NN)
            up_pre = dot32(flat[...], w_three[1, :, cols], NN)
            grad_hidden = dot32(cot_flat[...], w_three[2, :, cols], NN)
            value, slope = gelu_pair(gate_pre)
            hid[:, cols] = (value * up_pre).astype(bf16)
            ul[:, cols] = (grad_hidden * value).astype(bf16)
            gl[:, cols] = (grad_hidden * up_pre * slope).astype(bf16)
            service(j)

    def second_half(c):
        flat = part.at[c].reshape(n * c_rows, width)

        @pl.loop(0, width // tile)
        def _(j):
            cols = pl.ds(pl.multiple_of(j * tile, tile), tile)
            terms = dot32(gl[...], w_three[0, cols, :], NT) + dot32(ul[...], w_three[1, cols, :], NT)
            flat[:, cols] = terms.astype(bf16)

    def branch_terms(c):
        @pl.loop(0, width // tile)
        def _(j):
            cols = pl.ds(pl.multiple_of(j * tile, tile), tile)
            ul[:, cols] = dot32(hid[...], w_three[2, cols, :], NT).astype(bf16)

    def norm_back(c):
        def work(piece, rows):
            m = mid[rows, :]
            inv = inverse_rms(m)
            u = m * inv
            gn = total[piece, :]
            e = gn * gain[1:2, :]
            ggain_ref[...] += jnp.sum(gn * u, axis=0, keepdims=True)
            gm = stream[rows, :].astype(f32) + inv * (e - u * jnp.mean(e * u, axis=-1, keepdims=True))
            total[piece, :] = gm
            x[c, t, piece, :] = gm.astype(bf16)

        by_piece(c, work)

    def scatter(kind, c, k):
        line.scatter_step(ph(kind, c), k, *lands(c))

    def gather(kind, c, k):
        line.gather_step(ph(kind, c), k, x_at(c) if kind != COT else cot_at(c))

    project(0)
    scatter(RS1, 0, 0)
    project(1)
    scatter(RS1, 1, 0)
    attn_save.wait()
    cube.sent(0, block_of(0))
    gate_load = pltpu.make_async_copy(mlp_hbm.at[0], w_three.at[0], load_sem.at[0])
    gate_load.start()
    gather(COT, 1, 1)
    update_memory()
    scatter(RS1, 0, 1)
    push(2, cube.levels)
    push(3, 1)
    one_save.wait()
    all_save.wait()
    qkv_save.wait()
    up_load = pltpu.make_async_copy(mlp_hbm.at[1], w_three.at[1], load_sem.at[1])
    up_load.start()
    gather(COT, 0, 2)
    for k in range(2, n - 1):
        scatter(RS1, 0, k)
    for item in comb_saves:
        item.wait()
    line.scatter_end(ph(RS1, 0), *lands(0), total)
    norm_two(0)
    gather(AG2, 0, 0)
    scatter(RS1, 1, 1)
    gather(COT, 1, 2)
    for stage in range(2, cube.levels):
        push(3, stage)
    for k in range(1, n - 1):
        gather(AG2, 0, k)
        if k + 1 < n - 1:
            scatter(RS1, 1, k + 1)
    gather(COT, 0, 3)
    cot_loads = [pltpu.make_async_copy(cot_all.at[c], cot, load_sem.at[3 + c]) for c in range(chunks)]
    cot_loads[0].start()
    push(3, cube.levels)
    line.gather_sent(AG1, stream_at)
    down_load = pltpu.make_async_copy(mlp_hbm.at[2], w_three.at[2], load_sem.at[2])
    down_load.start()
    line.scatter_end(ph(RS1, 1), *lands(1), total)
    norm_two(1)
    cot_own = pltpu.make_async_copy(cot_hbm, stream, own_sem.at[5])
    cot_own.start()
    gather(AG2, 1, 0)
    gather(AG2, 0, n - 1)
    gather(COT, 1, 3)
    gate_load.wait()
    up_load.wait()
    down_load.wait()
    cot_own.wait()
    outs = {}

    def send_out(name, c, src, dst, sem):
        outs[name, c] = pltpu.make_async_copy(src, dst, out_sem.at[sem])
        outs[name, c].start()

    def save_terms(c):
        for s in range(n):
            outs[("terms", s), c] = pltpu.make_async_copy(
                ul.at[s * c_rows : (s + 1) * c_rows, :], terms_hbm.at[c, s], term_sem.at[c * n + s]
            )
            outs[("terms", s), c].start()

    def await_terms(c):
        for s in range(n):
            outs[("terms", s), c].wait()

    def rows_of(ref, c):
        return ref.at[pl.ds(c * c_rows, c_rows), :]

    def save_chunk(c):
        send_out("x", c, x.at[c], x_out.at[c], 0)
        send_out("hid", c, hid, hid_out.at[c], 1)
        send_out("gl", c, gl, gl_out.at[c], 2)
        send_out("ul", c, ul, ul_out.at[c], 3)

    def finish_back(c):
        line.scatter_end(ph(RS3, c), *lands(c), total)
        norm_back(c)
        send_out("gmid", c, total, rows_of(gmid_out, c), 5)
        gather(AG4, c, 0)
        outs["gmid", c].wait()

    def start_branch(c):
        line.scatter_sent(ph(RS3, c), *lands(c))
        load = pltpu.make_async_copy(terms_hbm.at[c], part.at[c], load_sem.at[5])
        load.start()
        load.wait()
        scatter(RS2, c, 0)

    def finish_branch(c):
        line.scatter_end(ph(RS2, c), *lands(c), total)

        def work(piece, rows):
            branch = total[piece, :]
            result = mid[rows, :] + branch
            live = live_ref[rows, :]
            stat_ref[1:2, :] += square_sum(result, live)
            stat_ref[2:3, :] += square_sum(branch, live)
            part[c, t, piece, :] = result.astype(bf16)

        by_piece(c, work)
        send_out("result", c, part.at[c, t], result_out, 6)
        outs["result", c].wait()

    def during(*steps):
        def service(j):
            for at, step in enumerate(steps):
                @pl.when(j == at)
                def _():
                    step()

        return service

    half_rows = shard // 2
    flat_w = w_three.reshape(3 * width, units)
    cot_flat = cot.reshape(n * c_rows, width)
    trade_orders = [[1] + [1 << b for b in range(1, cube.levels)], [1] + [1 << b for b in range(cube.levels - 1, 0, -1)]]
    spare = width // 2
    sources = ((x_out, gl_out), (x_out, ul_out), (cot_all, hid_out))

    def grad_loads(g):
        left, right = sources[g]
        loads = [
            pltpu.make_async_copy(right.at[0], hid, grad_sem.at[0]),
            pltpu.make_async_copy(right.at[1], gl, grad_sem.at[1]),
            pltpu.make_async_copy(left.at[1], cot, grad_sem.at[2]),
        ]
        for s in range(n):
            loads.append(pltpu.make_async_copy(left.at[0, s], ul.at[s * c_rows : (s + 1) * c_rows, :], grad_sem.at[8 + s]))
        return loads

    def weight_grad(g, service=lambda j: None, wide=256):
        for item in grad_loads(g):
            item.start()
        for item in grad_loads(g):
            item.wait()
        if g > 0:
            first_trade(g - 1).wait_send()

        @pl.loop(0, width // wide)
        def _(j):
            cols = pl.ds(pl.multiple_of(j * wide, wide), wide)
            for first in range(0, units, units // 2):
                span = slice(first, first + units // 2)
                terms = dot32(ul[:, cols], hid[:, span], TN) + dot32(cot_flat[:, cols], gl[:, span], TN)
                for q in range(wide // shard):
                    mask = lax.bitwise_xor(j * (wide // shard) + q, f)
                    row = lax.rem(mask, 2) * spare + (1 - lax.rem(mask, 2)) * (g * width) + (mask // 2) * shard
                    flat_w[pl.ds(pl.multiple_of(row, shard), shard), span] = terms[q * shard : (q + 1) * shard].astype(bf16)
            service(j)

        first_trade(g).start()

    def first_trade(g):
        return pltpu.make_async_remote_copy(
            src_ref=flat_w.at[spare : 2 * spare, :],
            dst_ref=land.at[g, 0],
            send_sem=trade_send.at[g, 0, 0, 0],
            recv_sem=trade_recv.at[g, 0, 0, 0],
            device_id={"fsdp": cube.peer(1)},
            device_id_type=MESH,
        )

    def trades(g, i):
        for half in range(2):
            order = trade_orders[half]
            bit = order[i]
            for mask in range(fsdp_size):
                if all(mask & b == 0 for b in order[: i + 1]):
                    there = pl.ds((mask // 2) * shard + half * half_rows, half_rows)
                    here = pl.ds(g * width + ((mask ^ bit) // 2) * shard + half * half_rows, half_rows)
                    yield mask, half, pltpu.make_async_remote_copy(
                        src_ref=flat_w.at[here, :],
                        dst_ref=land.at[g, i, there, :],
                        send_sem=trade_send.at[g, i, half, mask // 2],
                        recv_sem=trade_recv.at[g, i, half, mask // 2],
                        device_id={"fsdp": cube.peer(bit)},
                        device_id_type=MESH,
                    )

    def trade_start(g, i):
        for _, _, item in trades(g, i):
            item.start()

    def add_first(g):
        first_trade(g).wait_recv()
        load = pltpu.make_async_copy(land.at[g, 0], flat_w.at[width + spare : width + 2 * spare, :], grad_sem.at[3])
        load.start()
        load.wait()

        @pl.loop(0, spare // half_rows)
        def _(r):
            mine = pl.ds(pl.multiple_of(g * width + r * half_rows, half_rows), half_rows)
            came = pl.ds(pl.multiple_of(width + spare + r * half_rows, half_rows), half_rows)
            flat_w[mine, :] = (flat_w[mine, :].astype(f32) + flat_w[came, :].astype(f32)).astype(bf16)

        trade_start(g, 1)

    def save_last(g):
        send_out("kept", g, flat_w.at[g * width : g * width + shard, :], kept_out.at[g], 8 + 3 * g)
        for half in range(2):
            row = g * width + (trade_orders[half][-1] // 2) * shard + half * half_rows
            send_out(("last", half), g, flat_w.at[row : row + half_rows, :], to_send.at[g, half], 9 + 3 * g + half)

    def add_next(g, i):
        places = []
        for mask, half, item in trades(g, i):
            item.wait_recv()
            places.append((mask // 2) * shard + half * half_rows)
        loads = [
            pltpu.make_async_copy(
                land.at[g, i, place : place + half_rows, :],
                flat_w.at[2 * width + spare + place : 2 * width + spare + place + half_rows, :],
                grad_sem.at[4 + at % 4],
            )
            for at, place in enumerate(places)
        ]
        for base in range(0, len(loads), 4):
            for item in loads[base : base + 4]:
                item.start()
            for item in loads[base : base + 4]:
                item.wait()
        for place in places:
            mine = slice(g * width + place, g * width + place + half_rows)
            came = slice(2 * width + spare + place, 2 * width + spare + place + half_rows)
            flat_w[mine, :] = (flat_w[mine, :].astype(f32) + flat_w[came, :].astype(f32)).astype(bf16)
        if i + 1 < cube.levels - 1:
            trade_start(g, i + 1)
        else:
            save_last(g)

    def trade_end(g):
        outs["kept", g].wait()
        for half in range(2):
            outs[("last", half), g].wait()

    def trade_sent(g):
        for i in range(1, cube.levels - 1):
            for _, _, item in trades(g, i):
                item.wait_send()

    def skip():
        pass

    cot_loads[0].wait()
    first_half(0, during(skip, functools.partial(gather, AG2, 1, 1), skip, functools.partial(gather, AG2, 1, 2)))
    cot_loads[1].start()
    save_chunk(0)
    line.scatter_sent(ph(RS1, 0), *lands(0))
    second_half(0)
    line.gather_sent(ph(AG2, 0), x_at(0))
    outs["x", 0].wait()
    outs["ul", 0].wait()
    scatter(RS3, 0, 0)
    branch_terms(0)
    for k in range(3, n):
        gather(AG2, 1, k)
    save_terms(0)
    outs["hid", 0].wait()
    outs["gl", 0].wait()
    await_terms(0)
    cot_loads[1].wait()
    first_half(1, during(functools.partial(scatter, RS3, 0, 1), skip, functools.partial(scatter, RS3, 0, 2)))
    save_chunk(1)
    line.scatter_sent(ph(RS1, 1), *lands(1))
    second_half(1)
    line.gather_sent(ph(AG2, 1), x_at(1))
    outs["x", 1].wait()
    outs["ul", 1].wait()
    scatter(RS3, 1, 0)
    finish_back(0)
    branch_terms(1)
    save_terms(1)
    outs["hid", 1].wait()
    outs["gl", 1].wait()
    for item in range(1, 4):
        cube.sent(item, block_of(item))
    scatter(RS3, 1, 1)
    gather(AG4, 0, 1)
    start_branch(0)
    await_terms(1)

    def z_one():
        for k in range(2, n - 1):
            scatter(RS3, 1, k)
        gather(AG4, 0, 2)

    weight_grad(0, during(*[skip] * 3, z_one))
    scatter(RS2, 0, 1)
    weight_grad(1, during(*[skip] * 4, functools.partial(finish_back, 1), functools.partial(add_first, 0)))
    mid_save = pltpu.make_async_copy(mid, mid_out, own_sem.at[5])
    mid_save.start()
    for k in range(3, n):
        gather(AG4, 0, k)
    send_out("branch", 0, x.at[0], branch_out.at[:, 0], 0)
    for k in range(2, n - 1):
        scatter(RS2, 0, k)
    weight_grad(2, during(skip, functools.partial(gather, AG4, 1, 1), skip, functools.partial(add_first, 1)))
    finish_branch(0)
    gather(AG4, 1, 2)
    add_first(2)
    for i in range(1, cube.levels - 1):
        add_next(0, i)
    for k in range(3, n):
        gather(AG4, 1, k)
    send_out("branch", 1, x.at[1], branch_out.at[:, 1], 7)
    for g in (1, 2):
        for i in range(1, cube.levels - 1):
            add_next(g, i)
    for g in range(3):
        trade_end(g)
        trade_sent(g)
    first_trade(2).wait_send()
    mid_save.wait()
    line.scatter_sent(ph(RS3, 1), *lands(1))
    for c in range(chunks):
        outs["branch", c].wait()
    for c in range(chunks):
        line.gather_sent(ph(COT, c), cot_at(c))
        line.gather_sent(ph(AG4, c), x_at(c))
        if c == 0:
            line.scatter_sent(ph(RS2, c), *lands(c))


def whole_layer(bounds, gains, live, memory, norm, gate, stream, cot, attn_weights, mlp_weights, tp_size, fsdp_size, collective_id, tile=512):
    chunks = 2
    rows, width = stream.shape
    inner = attn_weights[0].shape[1]
    units = mlp_weights[0].shape[1]
    heads, hd = memory.shape[:2]
    length = rows * tp_size
    c_rows = rows // chunks
    bf, f32 = jnp.bfloat16, jnp.float32
    S = jax.ShapeDtypeStruct
    any_space = pl.BlockSpec(memory_space=pl.ANY)
    vmem = pl.BlockSpec(memory_space=pltpu.VMEM)
    smem = pl.BlockSpec(memory_space=pltpu.SMEM)
    grid_rows = (chunks, tp_size, c_rows)
    flat_rows = (chunks, tp_size * c_rows)
    levels = fsdp_size.bit_length() - 1
    V, DMA = pltpu.VMEM, pltpu.SemaphoreType.DMA
    return pl.pallas_call(
        functools.partial(layer_kernel, chunks=chunks, tp_size=tp_size, fsdp_size=fsdp_size, tile=tile),
        in_specs=[smem] + [vmem] * 5 + [any_space] * 9,
        out_specs=[any_space] * 20 + [vmem] * 6,
        out_shape=[
            S((3, width, units), bf),
            S((width, 4 * inner), bf),
            S((length, width), bf),
            S((length, 3 * inner), bf),
            S((tp_size, chunks, c_rows, inner), bf),
            S((length, inner), f32),
            S(grid_rows + (width,), bf),
            S(grid_rows + (width,), bf),
            S(flat_rows + (units,), bf), S(flat_rows + (units,), bf), S(flat_rows + (units,), bf),
            S(grid_rows + (width,), bf),
            S((rows // chunks, width), bf),
            S((rows, width), f32),
            S((tp_size, chunks, c_rows, width), bf),
            S((3, width // fsdp_size, units), bf),
            S((3, levels - 1, width // 2, units), bf),
            S((length, width), bf),
            S((rows, width), f32),
            S((3, 2, width // fsdp_size // 2, units), bf),
            S((1, width), f32), S((8, 128), f32), S((heads, 1, length), f32), S((heads, hd, hd), f32), S((heads, 1, hd), f32), S((8, width), f32),
        ],
        scratch_shapes=[
            V((3, width, units), bf),
            V(grid_rows + (width,), bf),
            V((tp_size, c_rows, width), bf),
            V(flat_rows[1:] + (units,), bf), V(flat_rows[1:] + (units,), bf), V(flat_rows[1:] + (units,), bf),
            V(grid_rows + (width,), bf),
            V((chunks, tp_size - 1, c_rows, width), bf), V((chunks, tp_size - 1, c_rows, width), bf),
            V((rows, width), bf),
            V((rows, width), f32), V((c_rows, width), f32),
            DMA((9 + chunks,)), DMA((6,)), DMA((max(17, 3 + tp_size + tp_size * chunks),)),
            DMA((2 * tp_size,)), DMA((8 + tp_size,)),
            DMA((3, levels - 1, 2, fsdp_size // 2)), DMA((3, levels - 1, 2, fsdp_size // 2)),
            DMA((levels,)), DMA((levels,)),
            DMA((4, 2, fsdp_size)), DMA((4, 2, fsdp_size)),
            DMA((1 + 6 * chunks, 2, tp_size - 1)), DMA((1 + 6 * chunks, 2, tp_size - 1)),
        ],
        compiler_params=pltpu.CompilerParams(
            collective_id=collective_id, has_side_effects=True, vmem_limit_bytes=60 * 2**20
        ),
        name="layer_kernel",
    )(
        bounds, gains, live, memory, norm.reshape(heads, 1, hd), jnp.broadcast_to(gate[:, None, None], (heads, 1, hd)),
        stream, cot, *attn_weights, *mlp_weights,
    )


def tail_kernel(
    bounds, gains, live_ref, mem_ref, norm_ref, gate_ref, lse_ref, gain_two_ref, stat_ref,
    branch_hbm, attn_hbm, qkv_hbm, mix_hbm, one_hbm, comb_hbm, stream_hbm, all_hbm, gmid_hbm, mid_hbm, terms_hbm, send_hbm,
    grad_out, result_out, land_mlp, land, kept_out,
    dmem_ref, dnorm_ref, sums,
    attn_w, g_ref, spare_ref, rows_ref, one_ref, qkv, dqkv, mixed_ref, gc_ref, part, land_r, land_l, dk_acc, dv_acc,
    sums_land,
    load_sem, out_sem, mlp_send, mlp_recv, sums_send, sums_recv, trade_send, trade_recv, line_send, line_recv,
    *, chunks, tp_size, fsdp_size, tile,
):
    n = tp_size
    bf16, f32 = jnp.bfloat16, jnp.float32
    t, f = lax.axis_index("tp"), lax.axis_index("fsdp")
    c_rows, width = part.shape[2], part.shape[3]
    rows_dev = c_rows * chunks
    length = n * rows_dev
    heads, hd = mem_ref.shape[0], mem_ref.shape[2]
    inner = heads * hd
    shard = width // fsdp_size
    half_rows = shard // 2
    spare = width // 2
    levels, tp_levels = fsdp_size.bit_length() - 1, n.bit_length() - 1
    orders = [[1] + [1 << b for b in range(1, levels)], [1] + [1 << b for b in range(levels - 1, 0, -1)]]
    line = Line(n, line_send, line_recv)
    total, extra = gc_ref.at[0:c_rows, :], gc_ref.at[c_rows : 2 * c_rows, :]
    count = [0]

    def load(src, dst):
        item = pltpu.make_async_copy(src, dst, load_sem.at[count[0]])
        count[0] += 1
        item.start()
        return item

    def peer(bit):
        return lax.bitwise_xor(f, bit)

    def place(s, c):
        return slice(c * n * c_rows + s * c_rows, c * n * c_rows + (s + 1) * c_rows)

    def origin(s, c):
        return slice(s * rows_dev + c * c_rows, s * rows_dev + (c + 1) * c_rows)

    weight_load = load(attn_hbm, attn_w)
    branch_load = load(branch_hbm, rows_ref)
    terms_load = load(terms_hbm.at[chunks - 1], part.at[chunks])
    comb_load = load(comb_hbm, spare_ref.at[:, 0:inner])
    qkv_load = load(qkv_hbm, qkv)
    mix_load = load(mix_hbm, mixed_ref)
    one_loads = [load(one_hbm.at[origin(s, c), :], one_ref.at[place(s, c), :]) for c in range(chunks) for s in range(n)]

    barrier = pltpu.get_barrier_semaphore()
    for k in range(1, n):
        pl.semaphore_signal(barrier, inc=1, device_id={"tp": lax.rem(t + k, n)}, device_id_type=MESH)
    for b in range(levels):
        pl.semaphore_signal(barrier, inc=1, device_id={"fsdp": peer(1 << b)}, device_id_type=MESH)
    pl.semaphore_wait(barrier, n - 1 + levels)

    mlp_trades = [
        pltpu.make_async_remote_copy(
            src_ref=send_hbm.at[g, half],
            dst_ref=land_mlp.at[g, half],
            send_sem=mlp_send.at[g, half],
            recv_sem=mlp_recv.at[g, half],
            device_id={"fsdp": peer(orders[half][-1])},
            device_id_type=MESH,
        )
        for g in range(3)
        for half in range(2)
    ]
    for item in mlp_trades:
        item.start()

    def lands(c):
        return part.at[c], land_r.at[c], land_l.at[c]

    def scatter(c, k):
        line.scatter_step(c, k, *lands(c))

    terms_load.wait()
    scatter(chunks, 0)

    for item in (weight_load, branch_load, comb_load):
        item.wait()

    def store_grad(j, wide, cols, terms):
        for q in range(wide // shard):
            mask = lax.bitwise_xor(j * (wide // shard) + q, f)
            row = lax.rem(mask, 2) * spare + (mask // 2) * shard
            g_ref[pl.ds(pl.multiple_of(row, shard), shard), cols] = terms[q * shard : (q + 1) * shard].astype(bf16)

    wide = 256

    @pl.loop(0, n)
    def _(s):
        rows = pl.ds(pl.multiple_of(s * rows_dev, rows_dev), rows_dev)
        gc_ref[:, pl.ds(pl.multiple_of(s * inner, inner), inner)] = dot32(
            rows_ref[rows, :], attn_w[:, 3 * inner : 4 * inner], NN
        )

    sums[...] = jnp.zeros_like(sums)
    sums[1:2, :] = gain_two_ref[...]
    lane = lax.broadcasted_iota(jnp.int32, (1, width), 1)
    qkv_load.wait()
    mix_load.wait()

    prefix, valid = bounds[0], bounds[1]
    scale = hd ** -0.5

    @pl.loop(0, heads)
    def _(h):
        def lanes(group):
            return pl.ds(pl.multiple_of(group * inner + h * hd, hd), hd)

        gate = jax.nn.sigmoid(gate_ref[h])
        memory, norm = mem_ref[h], norm_ref[h]
        dmem_ref[h] = jnp.zeros((hd, hd), f32)
        dnorm_ref[h] = jnp.zeros((1, hd), f32)
        dgate = jnp.zeros((1, hd), f32)
        for s in range(n - 1, -1, -1):
            first = s * rows_dev
            reach = key_reach(first, rows_dev, length)
            rows = slice(first, first + rows_dev)
            q = qkv[rows, lanes(0)]
            gc = gc_ref[:, pl.ds(pl.multiple_of(s * inner + h * hd, hd), hd)]
            mixed = mixed_ref[rows, lanes(0)]
            qm = mapped(q.astype(f32))
            inverse = 1.0 / jnp.sum(qm * norm, axis=-1, keepdims=True)
            retrieved = dot_three(qm, memory, NN) * inverse
            dgate = dgate + jnp.sum(gc * (retrieved - mixed), axis=0, keepdims=True)
            gnum = gate * gc * inverse
            gden = -jnp.sum(gnum * retrieved, axis=-1, keepdims=True)
            dmem_ref[h] += dot_three(qm, gnum, TN)
            dnorm_ref[h] += jnp.sum(gden * qm, axis=0, keepdims=True)
            dq_mem = (dot_three(gnum, memory, NT) + gden * norm) * jnp.minimum(qm, 1.0)
            low = ((1.0 - gate) * gc).astype(bf16)
            delta = jnp.sum((low.astype(f32) * mixed).T, axis=0, keepdims=True)
            keys = qkv[0:reach, lanes(1)]
            scores = dot32(keys, q, NT) * (scale * LOG2E)
            limit = key_limit(first, rows_dev, prefix, valid)
            scores = jnp.where(
                lax.broadcasted_iota(jnp.int32, scores.shape, 0) <= limit, scores - lse_ref[h, :, rows], NEG
            )
            probs = jnp.exp2(scores)
            gp = dot32(qkv[0:reach, lanes(2)], low, NT)
            gs = (probs * (gp - delta)).astype(bf16)
            dv = dot32(probs.astype(bf16), low, NN)
            dk = dot32(gs, q, NN)
            if s == n - 1:
                dv_acc[...] = dv
                dk_acc[...] = dk
            else:
                dv_acc[0:reach, :] += dv
                dk_acc[0:reach, :] += dk
            dq = (dot32(keys, gs, TN).T * scale + dq_mem).astype(bf16)
            for c in range(chunks):
                dqkv[place(s, c), lanes(0)] = dq[c * c_rows : (c + 1) * c_rows]
        for s in range(n):
            for c in range(chunks):
                dqkv[place(s, c), lanes(1)] = (dk_acc[origin(s, c), :] * scale).astype(bf16)
                dqkv[place(s, c), lanes(2)] = dv_acc[origin(s, c), :].astype(bf16)
        dgate_sum = jnp.sum(dgate * (gate * (1.0 - gate)), axis=-1, keepdims=True)
        sums[2:3, :] += jnp.where(lane == t * heads + h, dgate_sum, 0.0)
        for k in range(1, n - 1):
            @pl.when(h == k)
            def _():
                scatter(chunks, k)

    @pl.loop(0, width // wide)
    def _(j):
        cols = pl.ds(pl.multiple_of(j * wide, wide), wide)
        store_grad(j, wide, slice(3 * inner, 4 * inner), dot32(rows_ref[:, cols], spare_ref[:, 0:inner], TN))

    all_loads = [load(all_hbm.at[origin(s, c), :], rows_ref.at[place(s, c), :]) for c in range(chunks) for s in range(n)]
    for item in all_loads:
        item.wait()

    for c in range(chunks):
        here = slice(c * n * c_rows, (c + 1) * n * c_rows)
        inverse_all = inverse_rms(rows_ref[here, :].astype(f32))
        flat = part.at[c].reshape(n * c_rows, width)

        @pl.loop(0, width // tile)
        def _(j):
            cols = pl.ds(pl.multiple_of(j * tile, tile), tile)
            terms = dot32(dqkv[here, :], attn_w[cols, 0 : 3 * inner], NT)
            flat[:, cols] = terms.astype(bf16)
            unit = rows_ref[here, cols].astype(f32) * inverse_all
            sums[0:1, cols] += jnp.sum(terms * unit, axis=0, keepdims=True)

        scatter(c, 0)

    own_rows = slice(rows_dev - c_rows, rows_dev)
    mid_load = load(mid_hbm.at[own_rows, :], extra)
    line.scatter_end(chunks, *lands(chunks), total)
    mid_load.wait()

    def by_piece(work):
        @pl.loop(0, c_rows // PIECE)
        def _(r):
            work(pl.ds(pl.multiple_of(r * PIECE, PIECE), PIECE), r * PIECE)

    def close_branch(piece, first):
        branch = total[piece, :]
        result = extra[piece, :] + branch
        live = live_ref[pl.ds(pl.multiple_of(rows_dev - c_rows + first, PIECE), PIECE), :]
        part[chunks, t, piece, :] = result.astype(bf16)
        values = (result, branch)
        for at, value in zip((0, 2), values):
            squares = jnp.sum(jnp.sum(value * value, axis=-1, keepdims=True) * live, axis=0, keepdims=True)
            sums[3:4, :] += jnp.where(lane == 3 * f + at, squares, 0.0)

    by_piece(close_branch)
    result_save = pltpu.make_async_copy(part.at[chunks, t], result_out, out_sem.at[0])
    result_save.start()
    for at, row in enumerate((1, 0, 2)):
        sums[3:4, :] += jnp.where(lane == 3 * f + at, stat_ref[row : row + 1, 0:1], 0.0)

    def sums_step(at):
        target = {"fsdp": peer(1 << at)} if at < levels else {"tp": lax.bitwise_xor(t, 1 << (at - levels))}
        return pltpu.make_async_remote_copy(
            src_ref=sums,
            dst_ref=sums_land.at[at],
            send_sem=sums_send.at[at],
            recv_sem=sums_recv.at[at],
            device_id=target,
            device_id_type=MESH,
        )

    def sums_add(at):
        sums_step(at).wait()
        sums[...] += sums_land[at]

    sums_step(0).start()

    for item in one_loads:
        item.wait()

    @pl.loop(0, width // wide)
    def _(j):
        cols = pl.ds(pl.multiple_of(j * wide, wide), wide)
        store_grad(j, wide, slice(0, 3 * inner), dot32(one_ref[:, cols], dqkv[...], TN))

    first_trade = pltpu.make_async_remote_copy(
        src_ref=g_ref.at[spare : 2 * spare, :],
        dst_ref=land.at[0],
        send_sem=trade_send.at[0, 0, 0],
        recv_sem=trade_recv.at[0, 0, 0],
        device_id={"fsdp": peer(1)},
        device_id_type=MESH,
    )
    first_trade.start()

    def trades(i):
        for half in range(2):
            order = orders[half]
            bit = order[i]
            for mask in range(fsdp_size):
                if all(mask & b == 0 for b in order[: i + 1]):
                    there = (mask // 2) * shard + half * half_rows
                    here = ((mask ^ bit) // 2) * shard + half * half_rows
                    yield there, pltpu.make_async_remote_copy(
                        src_ref=g_ref.at[here : here + half_rows, :],
                        dst_ref=land.at[i, there : there + half_rows, :],
                        send_sem=trade_send.at[i, half, mask // 2],
                        recv_sem=trade_recv.at[i, half, mask // 2],
                        device_id={"fsdp": peer(bit)},
                        device_id_type=MESH,
                    )

    def add_rows(mine, came):
        g_ref[mine, :] = (g_ref[mine, :].astype(f32) + spare_ref[came, :].astype(f32)).astype(bf16)

    scatter(0, 1)
    sums_add(0)
    sums_step(1).start()
    scatter(1, 1)
    first_trade.wait_recv()
    first_load = load(land.at[0], spare_ref)
    first_load.wait()

    @pl.loop(0, spare // half_rows)
    def _(r):
        rows = pl.ds(pl.multiple_of(r * half_rows, half_rows), half_rows)
        add_rows(rows, rows)

    for _, item in trades(1):
        item.start()
    for k in range(2, n - 1):
        scatter(0, k)
    sums_add(1)
    sums_step(2).start()

    one_gain = gains[0:1, :]

    def finish(c):
        rows = slice(c * c_rows, (c + 1) * c_rows)
        gmid_load = load(gmid_hbm.at[rows, :], extra)
        stream_load = load(stream_hbm.at[rows, :], part.at[chunks, 0])
        line.scatter_end(c, *lands(c), total)
        gmid_load.wait()
        stream_load.wait()

        def close(piece, first):
            v = part[chunks, 0, piece, :].astype(f32)
            inv = inverse_rms(v)
            u = v * inv
            e = total[piece, :] * one_gain
            total[piece, :] = extra[piece, :] + inv * (e - u * jnp.mean(e * u, axis=-1, keepdims=True))

        by_piece(close)
        save = pltpu.make_async_copy(total, grad_out.at[rows, :], out_sem.at[1])
        save.start()
        save.wait()

    result_save.wait()
    line.scatter_sent(chunks, *lands(chunks))
    for at in range(2, levels):
        sums_add(at)
        sums_step(at + 1).start()
    for k in range(2, n - 1):
        scatter(1, k)
    for i in range(1, levels - 1):
        arrived = list(trades(i))
        loads = []
        for there, item in arrived:
            item.wait_recv()
            loads.append(load(land.at[i, there : there + half_rows, :], spare_ref.at[there : there + half_rows, :]))
        for item in loads:
            item.wait()
        for there, _ in arrived:
            rows = slice(there, there + half_rows)
            add_rows(rows, rows)
        for _, item in trades(i + 1):
            item.start()
    kept_save = pltpu.make_async_copy(g_ref.at[0:shard, :], kept_out, out_sem.at[2])
    kept_save.start()
    finish(0)
    for at in range(levels, levels + tp_levels):
        sums_add(at)
        if at + 1 < levels + tp_levels:
            sums_step(at + 1).start()
    finish(1)
    for _, item in trades(levels - 1):
        item.wait_recv()
    kept_save.wait()
    for item in mlp_trades:
        item.wait()
    first_trade.wait_send()
    for i in range(1, levels):
        for _, item in trades(i):
            item.wait_send()
    for c in range(chunks):
        line.scatter_sent(c, *lands(c))


def whole_tail(
    bounds, gains, live, memory, norm, gate, lse, gain_two, stat,
    branch, attn_full, qkv, mix, flat_one, comb, stream, stream_all, gmid, mid, terms, to_send, tp_size, fsdp_size, collective_id, tile=512,
):
    chunks = 2
    rows, width = stream.shape
    length = rows * tp_size
    c_rows = rows // chunks
    heads, hd = memory.shape[:2]
    inner = heads * hd
    units = to_send.shape[-1]
    shard = width // fsdp_size
    levels, tp_levels = fsdp_size.bit_length() - 1, tp_size.bit_length() - 1
    bf, f32 = jnp.bfloat16, jnp.float32
    S, V, DMA = jax.ShapeDtypeStruct, pltpu.VMEM, pltpu.SemaphoreType.DMA
    any_space = pl.BlockSpec(memory_space=pl.ANY)
    vmem = pl.BlockSpec(memory_space=pltpu.VMEM)
    smem = pl.BlockSpec(memory_space=pltpu.SMEM)
    adds = sum(2 * (fsdp_size >> (i + 1)) for i in range(1, levels - 1))
    loads = 6 + 2 * length // c_rows + 2 + 4 + adds
    return pl.pallas_call(
        functools.partial(tail_kernel, chunks=chunks, tp_size=tp_size, fsdp_size=fsdp_size, tile=tile),
        in_specs=[smem] + [vmem] * 8 + [any_space] * 12,
        out_specs=[any_space] * 5 + [vmem] * 3,
        out_shape=[
            S((rows, width), f32),
            S((c_rows, width), bf),
            S(to_send.shape, bf),
            S((levels, width // 2, 4 * inner), bf),
            S((shard, 4 * inner), bf),
            S((heads, hd, hd), f32), S((heads, 1, hd), f32), S((8, width), f32),
        ],
        scratch_shapes=[
            V((width, 4 * inner), bf),
            V((width, 4 * inner), bf),
            V((width // 2, 4 * inner), bf),
            V((length, width), bf),
            V((length, width), bf),
            V((length, 3 * inner), bf), V((length, 3 * inner), bf),
            V((length, inner), f32), V((rows, tp_size * inner), f32),
            V((chunks + 1, tp_size, c_rows, width), bf),
            V((chunks + 1, tp_size - 1, c_rows, width), bf), V((chunks + 1, tp_size - 1, c_rows, width), bf),
            V((length, hd), f32), V((length, hd), f32),
            V((levels + tp_levels, 8, width), f32),
            DMA((loads,)), DMA((3,)),
            DMA((3, 2)), DMA((3, 2)),
            DMA((levels + tp_levels,)), DMA((levels + tp_levels,)),
            DMA((levels, 2, fsdp_size // 2)), DMA((levels, 2, fsdp_size // 2)),
            DMA((chunks + 1, 2, tp_size - 1)), DMA((chunks + 1, 2, tp_size - 1)),
        ],
        compiler_params=pltpu.CompilerParams(
            collective_id=collective_id, has_side_effects=True, vmem_limit_bytes=60 * 2**20
        ),
        name="tail_kernel",
    )(
        bounds, gains, live, memory, norm.reshape(heads, 1, hd), jnp.broadcast_to(gate[:, None, None], (heads, 1, hd)),
        lse, gain_two, stat, branch, attn_full, qkv, mix, flat_one, comb, stream, stream_all, gmid, mid, terms, to_send,
    )


def on_device(
    stream,
    attn_gain,
    w_query,
    w_key,
    w_value,
    w_out,
    mem_gate,
    mlp_gain,
    w_gate,
    w_up,
    w_down,
    memory,
    normalizer,
    prefix,
    valid,
    cotangent,
):
    f32, bf16 = jnp.float32, jnp.bfloat16
    len_dev, width = (stream.shape[1], stream.shape[2])
    tp_size, fsdp_size = lax.axis_size("tp"), lax.axis_size("fsdp")
    tp_here, seq_here = lax.axis_index("tp"), lax.axis_index("fsdp")
    seq_len = len_dev * tp_size
    heads_here = mem_gate.shape[0]
    prefix_len = prefix[seq_here]
    valid_len = valid[seq_here]
    stream, cotangent = stream[0], cotangent[0]

    shard = width // fsdp_size
    gains = jnp.zeros((8, width), f32)
    gains = lax.dynamic_update_slice(
        gains, jnp.stack([attn_gain, mlp_gain]).astype(f32), (0, seq_here * shard)
    )
    bounds = jnp.stack([prefix_len, valid_len])
    local_position = tp_here * len_dev + jnp.arange(len_dev, dtype=jnp.int32)
    live_here = (local_position < valid_len).astype(f32)[:, None]
    (
        _, attn_full, flat_one, qkv_rows, combined, local_mix, _, _, _, _, _, mlp_terms,
        first_out, grad_middle, branch_low, kept, _, stream_all, middle_rows, to_send,
        gain_two_terms, stats, log_total, memory_next, normalizer_next, gains,
    ) = whole_layer(
        bounds, gains, live_here, memory[0], normalizer[0], mem_gate, stream, cotangent,
        (w_query, w_key, w_value, w_out), (w_gate, w_up, w_down), tp_size, fsdp_size, 1,
    )
    inner = w_query.shape[1]
    stream_grad, second_out, landed, attn_landed, attn_kept, grad_memory, grad_normalizer, joined = whole_tail(
        bounds, gains, live_here, memory[0], normalizer[0], mem_gate, log_total, gain_two_terms, stats,
        branch_low.reshape(seq_len, width), attn_full, qkv_rows, local_mix, flat_one, combined.reshape(seq_len, inner),
        stream, stream_all, grad_middle, middle_rows, mlp_terms, to_send, tp_size, fsdp_size, 2,
    )
    stream_out = jnp.concatenate([first_out, second_out], axis=0)
    gate_grad, up_grad, down_grad = (
        kept[g].astype(f32) + landed[g].reshape(shard, -1).astype(f32) for g in range(3)
    )
    query_grad, key_grad, value_grad, out_grad = (
        attn_kept[:, p * inner : (p + 1) * inner].astype(f32)
        + attn_landed[-1, :shard, p * inner : (p + 1) * inner].astype(f32)
        for p in range(4)
    )
    gain_one_grad = lax.dynamic_slice(joined, (0, seq_here * shard), (1, shard))[0]
    gain_two_grad = lax.dynamic_slice(joined, (1, seq_here * shard), (1, shard))[0]
    gate_grad_logit = lax.dynamic_slice(joined, (2, tp_here * heads_here), (1, heads_here))[0]
    stat_sums = lax.dynamic_slice(joined, (3, seq_here * 3), (1, 3))
    token_count = valid_len.astype(f32) * width
    rms_stats = jnp.sqrt(stat_sums / token_count + rms_eps)
    return (
        stream_out[None],
        stream_grad[None],
        gain_one_grad,
        query_grad,
        key_grad,
        value_grad,
        out_grad,
        gate_grad_logit,
        gain_two_grad,
        gate_grad,
        up_grad,
        down_grad,
        memory_next[None],
        normalizer_next[:, 0][None],
        grad_memory[None],
        grad_normalizer[:, 0][None],
        rms_stats,
    )


def solution(mesh):
    placed = (
        P("fsdp", "tp", None),
        P("fsdp"),
        P("fsdp", "tp"),
        P("fsdp", "tp"),
        P("fsdp", "tp"),
        P("fsdp", "tp"),
        P("tp"),
        P("fsdp"),
        P("fsdp", "tp"),
        P("fsdp", "tp"),
        P("fsdp", "tp"),
        P("fsdp", "tp", None, None),
        P("fsdp", "tp", None),
        P(),
        P(),
        P("fsdp", "tp", None),
    )
    return jax.shard_map(
        on_device,
        mesh=mesh,
        in_specs=placed,
        out_specs=(
            P("fsdp", "tp", None),
            P("fsdp", "tp", None),
            P("fsdp"),
            P("fsdp", "tp"),
            P("fsdp", "tp"),
            P("fsdp", "tp"),
            P("fsdp", "tp"),
            P("tp"),
            P("fsdp"),
            P("fsdp", "tp"),
            P("fsdp", "tp"),
            P("fsdp", "tp"),
            P("fsdp", "tp", None, None),
            P("fsdp", "tp", None),
            P("fsdp", "tp", None, None),
            P("fsdp", "tp", None),
            P("fsdp", None),
        ),
        check_vma=False,
    )
```

```python
import functools

import jax
import jax.numpy as jnp
from jax import lax
from jax.experimental import pallas as pl
from jax.experimental.pallas import tpu as pltpu
from jax.sharding import PartitionSpec as P

rms_eps = 1e-06
NEG = -1e30
LOG2E = 1.4426950408889634


def split_two(x):
    high = x.astype(jnp.bfloat16)
    return high, (x - high.astype(jnp.float32)).astype(jnp.bfloat16)


def dot32(a, b, dims):
    return lax.dot_general(a, b, (dims, ((), ())), preferred_element_type=jnp.float32)


def dot_three(a, b, dims):
    ah, al = split_two(a)
    bh, bl = split_two(b)
    return dot32(ah, bh, dims) + dot32(ah, bl, dims) + dot32(al, bh, dims)


NN, NT, TN = ((1,), (0,)), ((1,), (1,)), ((0,), (0,))


def mapped(v):
    return jnp.where(v > 0, v + 1.0, jnp.exp(jnp.minimum(v, 0.0)))


def key_reach(first, rows, keys):
    return min(keys, max(keys // 2, first + rows))


def key_limit(first, rows, prefix, valid):
    row = first + lax.broadcasted_iota(jnp.int32, (1, rows), 1)
    return jnp.minimum(valid - 1, jnp.maximum(row, prefix - 1))


norm_eps = 1e-06
MESH = pl.DeviceIdType.MESH
RIGHT, LEFT = 0, 1
PIECE = 32


class Line:
    def __init__(self, size, send_sem, recv_sem):
        self.size, self.send_sem, self.recv_sem = size, send_sem, recv_sem
        self.here = lax.axis_index("tp")

    def copy(self, phase, way, slot, src, dst):
        to = self.here + 1 if way == RIGHT else self.here - 1
        return pltpu.make_async_remote_copy(
            src_ref=src,
            dst_ref=dst,
            send_sem=self.send_sem.at[phase, way, slot],
            recv_sem=self.recv_sem.at[phase, way, slot],
            device_id={"tp": to},
            device_id_type=MESH,
        )

    def arrived(self, phase, way, slot, dst):
        self.copy(phase, way, slot, dst, dst).wait_recv()

    def scatter_step(self, phase, step, part, land_right, land_left):
        n, t = self.size, self.here

        def pass_on(way, slot, shard, land, first):
            @pl.when(jnp.logical_not(first))
            def _():
                self.arrived(phase, way, slot, land)

                @pl.loop(0, part.shape[1] // PIECE)
                def _(r):
                    rows = pl.ds(pl.multiple_of(r * PIECE, PIECE), PIECE)
                    came = land[rows, :].astype(jnp.float32)
                    part[shard, rows, :] = (part[shard, rows, :].astype(jnp.float32) + came).astype(part.dtype)

            self.copy(phase, way, slot, part.at[shard], land).start()

        right, left = step - t, step - (n - 1 - t)
        far, near = n - 1 - right, left

        @pl.when((right >= 0) & (far > t))
        def _():
            pass_on(RIGHT, right, far, land_right.at[far - 1], t == 0)

        @pl.when((left >= 0) & (near < t))
        def _():
            pass_on(LEFT, left, near, land_left.at[near], t == n - 1)

    def scatter_end(self, phase, part, land_right, land_left, total):
        n, t = self.size, self.here

        def over(work):
            @pl.loop(0, part.shape[1] // PIECE)
            def _(r):
                work(pl.ds(pl.multiple_of(r * PIECE, PIECE), PIECE))

        def own(rows):
            total[rows, :] = part[t, rows, :].astype(jnp.float32)

        def from_left(rows):
            total[rows, :] += land_right[t - 1, rows, :].astype(jnp.float32)

        def from_right(rows):
            total[rows, :] += land_left[t, rows, :].astype(jnp.float32)

        over(own)

        @pl.when(t > 0)
        def _():
            self.arrived(phase, RIGHT, n - 1 - t, land_right.at[t - 1])
            over(from_left)

        @pl.when(t < n - 1)
        def _():
            self.arrived(phase, LEFT, t, land_left.at[t])
            over(from_right)

    def scatter_sent(self, phase, part, land_right, land_left):
        n, t = self.size, self.here
        for k in range(n - 1):
            far, near = n - 1 - k, k

            @pl.when(t < far)
            def _():
                self.copy(phase, RIGHT, k, part.at[far], land_right.at[far - 1]).wait_send()

            @pl.when(t > near)
            def _():
                self.copy(phase, LEFT, k, part.at[near], land_left.at[near]).wait_send()

    def gather_step(self, phase, k, shard_at):
        n, t = self.size, self.here

        @pl.when(t >= k)
        def _():
            shard = shard_at(t - k)
            if k > 0:
                self.arrived(phase, RIGHT, k - 1, shard)
            if k < n - 1:
                @pl.when(t < n - 1)
                def _():
                    self.copy(phase, RIGHT, k, shard, shard).start()

        @pl.when(t + k <= n - 1)
        def _():
            shard = shard_at(t + k)
            if k > 0:
                self.arrived(phase, LEFT, k - 1, shard)
            if k < n - 1:
                @pl.when(t > 0)
                def _():
                    self.copy(phase, LEFT, k, shard, shard).start()

    def gather_sent(self, phase, shard_at):
        n, t = self.size, self.here
        for k in range(n - 1):
            @pl.when((t >= k) & (t < n - 1))
            def _():
                self.copy(phase, RIGHT, k, shard_at(t - k), shard_at(t - k)).wait_send()

            @pl.when((t + k <= n - 1) & (t > 0))
            def _():
                self.copy(phase, LEFT, k, shard_at(t + k), shard_at(t + k)).wait_send()


class Cube:
    def __init__(self, size, send_sem, recv_sem):
        self.size, self.send_sem, self.recv_sem = size, send_sem, recv_sem
        self.here = lax.axis_index("fsdp")
        self.levels = size.bit_length() - 1
        ups = [1 << b for b in range(1, self.levels)]
        self.orders = [ups[::-1] + [1], ups + [1]]

    def peer(self, bit):
        return lax.bitwise_xor(self.here, bit)

    def held(self, half, stage):
        masks = [0]
        for bit in self.orders[half][:stage]:
            masks += [mask ^ bit for mask in masks]
        return masks

    def copy(self, item, half, mask, bit, block_at):
        owner = self.peer(mask) if mask else self.here
        block = block_at(owner, half)
        return pltpu.make_async_remote_copy(
            src_ref=block,
            dst_ref=block,
            send_sem=self.send_sem.at[item, half, mask ^ bit],
            recv_sem=self.recv_sem.at[item, half, mask ^ bit],
            device_id={"fsdp": self.peer(bit)},
            device_id_type=MESH,
        )

    def await_stage(self, item, stage, block_at):
        for half in range(2):
            bit = self.orders[half][stage]
            for mask in self.held(half, stage):
                block = block_at(self.peer(mask ^ bit), half)
                pltpu.make_async_remote_copy(
                    src_ref=block,
                    dst_ref=block,
                    send_sem=self.send_sem.at[item, half, mask ^ bit],
                    recv_sem=self.recv_sem.at[item, half, mask ^ bit],
                    device_id={"fsdp": self.peer(bit)},
                    device_id_type=MESH,
                ).wait_recv()

    def stage(self, item, stage, block_at):
        if stage > 0:
            self.await_stage(item, stage - 1, block_at)
        if stage == self.levels:
            return
        for half in range(2):
            bit = self.orders[half][stage]
            for mask in self.held(half, stage):
                self.copy(item, half, mask, bit, block_at).start()

    def sent(self, item, block_at):
        for stage in range(self.levels):
            for half in range(2):
                bit = self.orders[half][stage]
                for mask in self.held(half, stage):
                    self.copy(item, half, mask, bit, block_at).wait_send()


GELU_A, GELU_B = 0.7978845608028654, 0.044715


def gelu_pair(v):
    square = v * v
    curve = jnp.tanh(v * (GELU_A + GELU_A * GELU_B * square))
    half = 0.5 + 0.5 * curve
    slope = half + (0.5 * v) * (1.0 - curve * curve) * (GELU_A + 3.0 * GELU_A * GELU_B * square)
    return v * half, slope


def inverse_rms(v):
    return lax.rsqrt(jnp.mean(v * v, axis=-1, keepdims=True) + norm_eps)


def layer_kernel(
    bounds, gain_in, live_ref, mem_ref, norm_ref, gate_ref,
    stream_hbm, cot_hbm, wq_hbm, wk_hbm, wv_hbm, wo_hbm, wg_hbm, wu_hbm, wd_hbm,
    mlp_hbm, attn_out, one_out, qkv_out, comb_out, mix_out, cot_all, x_out, hid_out, gl_out, ul_out, terms_hbm,
    result_out, gmid_out, branch_out, kept_out, land, all_out, mid_out, to_send,
    ggain_ref, stat_ref, lse_ref, memo_ref, normo_ref, gain,
    w_three, x, cot, hid, gl, ul, part, land_r, land_l, stream, mid, total,
    own_sem, load_sem, out_sem, term_sem, grad_sem, trade_send, trade_recv, gain_send, gain_recv, cube_send, cube_recv, line_send, line_recv,
    *, chunks, tp_size, fsdp_size, tile,
):
    n = tp_size
    bf16, f32 = jnp.bfloat16, jnp.float32
    t, f = lax.axis_index("tp"), lax.axis_index("fsdp")
    c_rows, width = x.shape[2], x.shape[3]
    units = hid.shape[1]
    rows_dev = stream.shape[0]
    length = rows_dev * n
    heads, hd = mem_ref.shape[0], mem_ref.shape[2]
    inner = heads * hd
    shard = width // fsdp_size
    line = Line(n, line_send, line_recv)
    cube = Cube(fsdp_size, cube_send, cube_recv)
    bits = [1 << b for b in range(cube.levels)]
    AG1 = 0

    def ph(kind, c):
        return 1 + kind * chunks + c

    COT, RS1, AG2, RS3, AG4, RS2 = range(6)

    attn_w = w_three.at[0]
    qkv = w_three.at[1]
    flat_one = w_three.at[2]

    def stream_at(s):
        return w_three.at[2, pl.ds(pl.multiple_of(length + s * rows_dev, rows_dev), rows_dev), :]

    def x_at(c):
        return lambda s: x.at[c, s]

    def cot_at(c):
        return lambda s: cot_all.at[c, s]

    def lands(c):
        return part.at[c], land_r.at[c], land_l.at[c]

    def block_of(item):
        whole = attn_w if item == 0 else mlp_hbm.at[item - 1]

        def at(owner, half):
            rows = shard // 2
            return whole.at[pl.ds(pl.multiple_of(owner * shard + half * rows, rows), rows), :]

        return at

    def push(item, stage):
        cube.stage(item, stage, block_of(item))

    own_rows = pl.ds(pl.multiple_of(f * shard, shard), shard)
    own = [
        pltpu.make_async_copy(w, w_three.at[0, own_rows, p * inner : (p + 1) * inner], own_sem.at[p])
        for p, w in enumerate((wq_hbm, wk_hbm, wv_hbm, wo_hbm))
    ]
    own += [pltpu.make_async_copy(stream_hbm, stream_at(t), own_sem.at[4]), pltpu.make_async_copy(stream_hbm, stream, own_sem.at[5])]
    homes = [hid.at[0:shard, :], hid.at[shard : 2 * shard, :], gl.at[0:shard, :]]
    own += [pltpu.make_async_copy(w, homes[m], own_sem.at[6 + m]) for m, w in enumerate((wg_hbm, wu_hbm, wd_hbm))]
    own.append(pltpu.make_async_copy(cot_hbm, ul.at[0:rows_dev, :], own_sem.at[9]))
    placed = [pltpu.make_async_copy(homes[m], mlp_hbm.at[m, own_rows, :], own_sem.at[6 + m]) for m in range(3)]
    placed += [
        pltpu.make_async_copy(ul.at[c * c_rows : (c + 1) * c_rows, :], cot_all.at[c, t], own_sem.at[9 + c])
        for c in range(chunks)
    ]
    for item in own:
        item.start()
    gain[...] = gain_in[...]
    ggain_ref[...] = jnp.zeros_like(ggain_ref)
    stat_ref[...] = jnp.zeros_like(stat_ref)

    barrier = pltpu.get_barrier_semaphore()

    @pl.when(t > 0)
    def _():
        pl.semaphore_signal(barrier, inc=1, device_id={"tp": t - 1}, device_id_type=MESH)

    @pl.when(t < n - 1)
    def _():
        pl.semaphore_signal(barrier, inc=1, device_id={"tp": t + 1}, device_id_type=MESH)

    for bit in bits:
        pl.semaphore_signal(barrier, inc=1, device_id={"fsdp": cube.peer(bit)}, device_id_type=MESH)
    peers = (t > 0).astype(jnp.int32) + (t < n - 1).astype(jnp.int32) + len(bits)
    pl.semaphore_wait(barrier, peers)

    for item in own[:6]:
        item.wait()
    push(0, 0)
    line.gather_step(AG1, 0, stream_at)
    for item in own[6:]:
        item.wait()
    for item in placed:
        item.start()
    for level, bit in enumerate(bits):
        trade = pltpu.make_async_remote_copy(
            src_ref=gain,
            dst_ref=total.at[8 * level : 8 * level + 8, :],
            send_sem=gain_send.at[level],
            recv_sem=gain_recv.at[level],
            device_id={"fsdp": cube.peer(bit)},
            device_id_type=MESH,
        )
        trade.start()
        trade.wait()
        gain[...] += total[8 * level : 8 * level + 8, :]
    for item in placed:
        item.wait()

    def norm_one(s):
        raw = stream_at(s)

        @pl.loop(0, rows_dev // PIECE)
        def _(r):
            v = raw[pl.ds(pl.multiple_of(r * PIECE, PIECE), PIECE), :].astype(f32)
            flat_one[pl.ds(pl.multiple_of(s * rows_dev + r * PIECE, PIECE), PIECE), :] = (
                v * inverse_rms(v) * gain[0:1, :]
            ).astype(bf16)

    def project_one(s):
        rows = pl.ds(pl.multiple_of(s * rows_dev, rows_dev), rows_dev)

        @pl.loop(0, 3)
        def _(p):
            cols = pl.ds(pl.multiple_of(p * inner, inner), inner)
            qkv[rows, cols] = dot32(flat_one[rows, :], attn_w[:, cols], NN).astype(bf16)

    def arrived_pair(k, work):
        @pl.when(t >= k)
        def _():
            work(t - k)

        @pl.when(t + k <= n - 1)
        def _():
            work(t + k)

    norm_one(t)
    push(0, 1)
    push(1, 0)
    line.gather_step(AG1, 1, stream_at)
    for stage in range(2, cube.levels):
        push(0, stage)
    arrived_pair(1, norm_one)
    push(0, cube.levels)
    attn_save = pltpu.make_async_copy(attn_w, attn_out, out_sem.at[0])
    attn_save.start()
    project_one(t)
    push(1, 1)
    push(2, 0)
    line.gather_step(AG1, 2, stream_at)
    arrived_pair(1, project_one)

    def both(s):
        norm_one(s)
        project_one(s)

    for k in range(2, n):
        if k > 2:
            line.gather_step(AG1, k, stream_at)
        if k == n - 1:
            for c in range(chunks):
                line.gather_step(ph(COT, c), 0, cot_at(c))
        arrived_pair(k, both)
    one_save = pltpu.make_async_copy(flat_one.at[0:length, :], one_out, out_sem.at[1])
    one_save.start()
    all_save = pltpu.make_async_copy(flat_one.at[length : 2 * length, :], all_out, own_sem.at[4])
    all_save.start()
    qkv_save = pltpu.make_async_copy(qkv.at[0:length, 0 : 3 * inner], qkv_out, out_sem.at[2])
    qkv_save.start()
    for stage in range(2, cube.levels):
        push(1, stage)
    push(2, 1)
    push(3, 0)
    push(1, cube.levels)

    prefix, valid = bounds[0], bounds[1]
    score_scale = hd ** -0.5 * LOG2E

    def attend_rows(s):
        first = s * rows_dev
        reach = key_reach(first, rows_dev, length)
        limit = key_limit(first, rows_dev, prefix, valid)

        @pl.loop(0, heads)
        def _(h):
            def lanes(group):
                return pl.ds(pl.multiple_of(group * inner + h * hd, hd), hd)

            q = qkv[first : first + rows_dev, lanes(0)]
            scores = dot32(qkv[0:reach, lanes(1)], q, NT) * score_scale
            scores = jnp.where(lax.broadcasted_iota(jnp.int32, scores.shape, 0) <= limit, scores, NEG)
            top = jnp.max(scores, axis=0, keepdims=True)
            probs = jnp.exp2(scores - top)
            row_total = jnp.sum(probs, axis=0, keepdims=True)
            mixed = (dot32(qkv[0:reach, lanes(2)], probs.astype(bf16), TN) / row_total).T
            lse_ref[h, :, first : first + rows_dev] = top + jnp.log2(row_total)
            gate = jax.nn.sigmoid(gate_ref[h])
            qm = mapped(q.astype(f32))
            denominator = jnp.sum(qm * norm_ref[h], axis=-1, keepdims=True)
            retrieved = dot_three(qm, mem_ref[h], NN) / denominator
            mid[:, pl.ds(pl.multiple_of(s * inner + h * hd, hd), hd)] = mixed
            both_mix = (gate * retrieved + (1.0 - gate) * mixed).astype(bf16)
            for c in range(chunks):
                hid[s * c_rows : (s + 1) * c_rows, pl.ds(pl.multiple_of(c * inner + h * hd, hd), hd)] = both_mix[
                    c * c_rows : (c + 1) * c_rows
                ]

    def update_memory():
        @pl.loop(0, heads)
        def _(h):
            km = mapped(qkv[0:length, pl.ds(pl.multiple_of(inner + h * hd, hd), hd)].astype(f32))
            km = jnp.where(lax.broadcasted_iota(jnp.int32, km.shape, 0) < valid, km, 0.0)
            kh, kl = split_two(km)
            values = qkv[0:length, pl.ds(pl.multiple_of(2 * inner + h * hd, hd), hd)]
            memo_ref[h] = mem_ref[h] + dot32(kh, values, TN) + dot32(kl, values, TN)
            normo_ref[h] = norm_ref[h] + jnp.sum(km, axis=0, keepdims=True)

    for s in range(n):
        attend_rows(s)
        if s == n - 2:
            line.gather_step(ph(COT, 0), 1, cot_at(0))
    for stage in range(2, cube.levels):
        push(2, stage)
    comb_saves = []
    for s in range(n):
        comb_saves.append(
            pltpu.make_async_copy(mid.at[:, s * inner : (s + 1) * inner], mix_out.at[s * rows_dev : (s + 1) * rows_dev, :], out_sem.at[3 + s])
        )
        for c in range(chunks):
            comb_saves.append(
                pltpu.make_async_copy(
                    hid.at[s * c_rows : (s + 1) * c_rows, c * inner : (c + 1) * inner],
                    comb_out.at[s, c],
                    out_sem.at[3 + n + s * chunks + c],
                )
            )
    for item in comb_saves:
        item.start()

    def project(c):
        flat = part.at[c].reshape(n * c_rows, width)

        @pl.loop(0, width // tile)
        def _(j):
            cols = pl.ds(pl.multiple_of(j * tile, tile), tile)
            flat[:, cols] = dot32(
                hid[:, c * inner : (c + 1) * inner], attn_w[cols, 3 * inner : 4 * inner], NT
            ).astype(bf16)

    def by_piece(c, work):
        @pl.loop(0, c_rows // PIECE)
        def _(r):
            piece = pl.ds(pl.multiple_of(r * PIECE, PIECE), PIECE)
            work(piece, pl.ds(pl.multiple_of(c * c_rows + r * PIECE, PIECE), PIECE))

    def square_sum(v, live):
        return jnp.sum(jnp.sum(v * v, axis=-1, keepdims=True) * live, axis=0, keepdims=True)

    def norm_two(c):
        def work(piece, rows):
            branch = total[piece, :]
            stat_ref[0:1, :] += square_sum(branch, live_ref[rows, :])
            m = stream[rows, :].astype(f32) + branch
            mid[rows, :] = m
            x[c, t, piece, :] = (m * inverse_rms(m) * gain[1:2, :]).astype(bf16)

        by_piece(c, work)

    def first_half(c, service):
        flat = x.at[c].reshape(n * c_rows, width)
        cot_flat = cot.reshape(n * c_rows, width)

        @pl.loop(0, units // tile)
        def _(j):
            cols = pl.ds(pl.multiple_of(j * tile, tile), tile)
            gate_pre = dot32(flat[...], w_three[0, :, cols], NN)
            up_pre = dot32(flat[...], w_three[1, :, cols], NN)
            grad_hidden = dot32(cot_flat[...], w_three[2, :, cols], NN)
            value, slope = gelu_pair(gate_pre)
            hid[:, cols] = (value * up_pre).astype(bf16)
            ul[:, cols] = (grad_hidden * value).astype(bf16)
            gl[:, cols] = (grad_hidden * up_pre * slope).astype(bf16)
            service(j)

    def second_half(c):
        flat = part.at[c].reshape(n * c_rows, width)

        @pl.loop(0, width // tile)
        def _(j):
            cols = pl.ds(pl.multiple_of(j * tile, tile), tile)
            terms = dot32(gl[...], w_three[0, cols, :], NT) + dot32(ul[...], w_three[1, cols, :], NT)
            flat[:, cols] = terms.astype(bf16)

    def branch_terms(c):
        @pl.loop(0, width // tile)
        def _(j):
            cols = pl.ds(pl.multiple_of(j * tile, tile), tile)
            ul[:, cols] = dot32(hid[...], w_three[2, cols, :], NT).astype(bf16)

    def norm_back(c):
        def work(piece, rows):
            m = mid[rows, :]
            inv = inverse_rms(m)
            u = m * inv
            gn = total[piece, :]
            e = gn * gain[1:2, :]
            ggain_ref[...] += jnp.sum(gn * u, axis=0, keepdims=True)
            gm = stream[rows, :].astype(f32) + inv * (e - u * jnp.mean(e * u, axis=-1, keepdims=True))
            total[piece, :] = gm
            x[c, t, piece, :] = gm.astype(bf16)

        by_piece(c, work)

    def scatter(kind, c, k):
        line.scatter_step(ph(kind, c), k, *lands(c))

    def gather(kind, c, k):
        line.gather_step(ph(kind, c), k, x_at(c) if kind != COT else cot_at(c))

    project(0)
    scatter(RS1, 0, 0)
    project(1)
    scatter(RS1, 1, 0)
    attn_save.wait()
    cube.sent(0, block_of(0))
    gate_load = pltpu.make_async_copy(mlp_hbm.at[0], w_three.at[0], load_sem.at[0])
    gate_load.start()
    gather(COT, 1, 1)
    update_memory()
    scatter(RS1, 0, 1)
    push(2, cube.levels)
    push(3, 1)
    one_save.wait()
    all_save.wait()
    qkv_save.wait()
    up_load = pltpu.make_async_copy(mlp_hbm.at[1], w_three.at[1], load_sem.at[1])
    up_load.start()
    gather(COT, 0, 2)
    for k in range(2, n - 1):
        scatter(RS1, 0, k)
    for item in comb_saves:
        item.wait()
    line.scatter_end(ph(RS1, 0), *lands(0), total)
    norm_two(0)
    gather(AG2, 0, 0)
    scatter(RS1, 1, 1)
    gather(COT, 1, 2)
    for stage in range(2, cube.levels):
        push(3, stage)
    for k in range(1, n - 1):
        gather(AG2, 0, k)
        if k + 1 < n - 1:
            scatter(RS1, 1, k + 1)
    gather(COT, 0, 3)
    cot_loads = [pltpu.make_async_copy(cot_all.at[c], cot, load_sem.at[3 + c]) for c in range(chunks)]
    cot_loads[0].start()
    push(3, cube.levels)
    line.gather_sent(AG1, stream_at)
    down_load = pltpu.make_async_copy(mlp_hbm.at[2], w_three.at[2], load_sem.at[2])
    down_load.start()
    line.scatter_end(ph(RS1, 1), *lands(1), total)
    norm_two(1)
    cot_own = pltpu.make_async_copy(cot_hbm, stream, own_sem.at[5])
    cot_own.start()
    gather(AG2, 1, 0)
    gather(AG2, 0, n - 1)
    gather(COT, 1, 3)
    gate_load.wait()
    up_load.wait()
    down_load.wait()
    cot_own.wait()
    outs = {}

    def send_out(name, c, src, dst, sem):
        outs[name, c] = pltpu.make_async_copy(src, dst, out_sem.at[sem])
        outs[name, c].start()

    def save_terms(c):
        for s in range(n):
            outs[("terms", s), c] = pltpu.make_async_copy(
                ul.at[s * c_rows : (s + 1) * c_rows, :], terms_hbm.at[c, s], term_sem.at[c * n + s]
            )
            outs[("terms", s), c].start()

    def await_terms(c):
        for s in range(n):
            outs[("terms", s), c].wait()

    def rows_of(ref, c):
        return ref.at[pl.ds(c * c_rows, c_rows), :]

    def save_chunk(c):
        send_out("x", c, x.at[c], x_out.at[c], 0)
        send_out("hid", c, hid, hid_out.at[c], 1)
        send_out("gl", c, gl, gl_out.at[c], 2)
        send_out("ul", c, ul, ul_out.at[c], 3)

    def finish_back(c):
        line.scatter_end(ph(RS3, c), *lands(c), total)
        norm_back(c)
        send_out("gmid", c, total, rows_of(gmid_out, c), 5)
        gather(AG4, c, 0)
        outs["gmid", c].wait()

    def start_branch(c):
        line.scatter_sent(ph(RS3, c), *lands(c))
        load = pltpu.make_async_copy(terms_hbm.at[c], part.at[c], load_sem.at[5])
        load.start()
        load.wait()
        scatter(RS2, c, 0)

    def finish_branch(c):
        line.scatter_end(ph(RS2, c), *lands(c), total)

        def work(piece, rows):
            branch = total[piece, :]
            result = mid[rows, :] + branch
            live = live_ref[rows, :]
            stat_ref[1:2, :] += square_sum(result, live)
            stat_ref[2:3, :] += square_sum(branch, live)
            part[c, t, piece, :] = result.astype(bf16)

        by_piece(c, work)
        send_out("result", c, part.at[c, t], result_out, 6)
        outs["result", c].wait()

    def during(*steps):
        def service(j):
            for at, step in enumerate(steps):
                @pl.when(j == at)
                def _():
                    step()

        return service

    half_rows = shard // 2
    flat_w = w_three.reshape(3 * width, units)
    cot_flat = cot.reshape(n * c_rows, width)
    trade_orders = [[1] + [1 << b for b in range(1, cube.levels)], [1] + [1 << b for b in range(cube.levels - 1, 0, -1)]]
    spare = width // 2
    sources = ((x_out, gl_out), (x_out, ul_out), (cot_all, hid_out))

    def grad_loads(g):
        left, right = sources[g]
        loads = [
            pltpu.make_async_copy(right.at[0], hid, grad_sem.at[0]),
            pltpu.make_async_copy(right.at[1], gl, grad_sem.at[1]),
            pltpu.make_async_copy(left.at[1], cot, grad_sem.at[2]),
        ]
        for s in range(n):
            loads.append(pltpu.make_async_copy(left.at[0, s], ul.at[s * c_rows : (s + 1) * c_rows, :], grad_sem.at[8 + s]))
        return loads

    def weight_grad(g, service=lambda j: None, wide=256):
        for item in grad_loads(g):
            item.start()
        for item in grad_loads(g):
            item.wait()
        if g > 0:
            first_trade(g - 1).wait_send()

        @pl.loop(0, width // wide)
        def _(j):
            cols = pl.ds(pl.multiple_of(j * wide, wide), wide)
            for first in range(0, units, units // 2):
                span = slice(first, first + units // 2)
                terms = dot32(ul[:, cols], hid[:, span], TN) + dot32(cot_flat[:, cols], gl[:, span], TN)
                for q in range(wide // shard):
                    mask = lax.bitwise_xor(j * (wide // shard) + q, f)
                    row = lax.rem(mask, 2) * spare + (1 - lax.rem(mask, 2)) * (g * width) + (mask // 2) * shard
                    flat_w[pl.ds(pl.multiple_of(row, shard), shard), span] = terms[q * shard : (q + 1) * shard].astype(bf16)
            service(j)

        first_trade(g).start()

    def first_trade(g):
        return pltpu.make_async_remote_copy(
            src_ref=flat_w.at[spare : 2 * spare, :],
            dst_ref=land.at[g, 0],
            send_sem=trade_send.at[g, 0, 0, 0],
            recv_sem=trade_recv.at[g, 0, 0, 0],
            device_id={"fsdp": cube.peer(1)},
            device_id_type=MESH,
        )

    def trades(g, i):
        for half in range(2):
            order = trade_orders[half]
            bit = order[i]
            for mask in range(fsdp_size):
                if all(mask & b == 0 for b in order[: i + 1]):
                    there = pl.ds((mask // 2) * shard + half * half_rows, half_rows)
                    here = pl.ds(g * width + ((mask ^ bit) // 2) * shard + half * half_rows, half_rows)
                    yield mask, half, pltpu.make_async_remote_copy(
                        src_ref=flat_w.at[here, :],
                        dst_ref=land.at[g, i, there, :],
                        send_sem=trade_send.at[g, i, half, mask // 2],
                        recv_sem=trade_recv.at[g, i, half, mask // 2],
                        device_id={"fsdp": cube.peer(bit)},
                        device_id_type=MESH,
                    )

    def trade_start(g, i):
        for _, _, item in trades(g, i):
            item.start()

    def add_first(g):
        first_trade(g).wait_recv()
        load = pltpu.make_async_copy(land.at[g, 0], flat_w.at[width + spare : width + 2 * spare, :], grad_sem.at[3])
        load.start()
        load.wait()

        @pl.loop(0, spare // half_rows)
        def _(r):
            mine = pl.ds(pl.multiple_of(g * width + r * half_rows, half_rows), half_rows)
            came = pl.ds(pl.multiple_of(width + spare + r * half_rows, half_rows), half_rows)
            flat_w[mine, :] = (flat_w[mine, :].astype(f32) + flat_w[came, :].astype(f32)).astype(bf16)

        trade_start(g, 1)

    def save_last(g):
        send_out("kept", g, flat_w.at[g * width : g * width + shard, :], kept_out.at[g], 8 + 3 * g)
        for half in range(2):
            row = g * width + (trade_orders[half][-1] // 2) * shard + half * half_rows
            send_out(("last", half), g, flat_w.at[row : row + half_rows, :], to_send.at[g, half], 9 + 3 * g + half)

    def add_next(g, i):
        places = []
        for mask, half, item in trades(g, i):
            item.wait_recv()
            places.append((mask // 2) * shard + half * half_rows)
        loads = [
            pltpu.make_async_copy(
                land.at[g, i, place : place + half_rows, :],
                flat_w.at[2 * width + spare + place : 2 * width + spare + place + half_rows, :],
                grad_sem.at[4 + at % 4],
            )
            for at, place in enumerate(places)
        ]
        for base in range(0, len(loads), 4):
            for item in loads[base : base + 4]:
                item.start()
            for item in loads[base : base + 4]:
                item.wait()
        for place in places:
            mine = slice(g * width + place, g * width + place + half_rows)
            came = slice(2 * width + spare + place, 2 * width + spare + place + half_rows)
            flat_w[mine, :] = (flat_w[mine, :].astype(f32) + flat_w[came, :].astype(f32)).astype(bf16)
        if i + 1 < cube.levels - 1:
            trade_start(g, i + 1)
        else:
            save_last(g)

    def trade_end(g):
        outs["kept", g].wait()
        for half in range(2):
            outs[("last", half), g].wait()

    def trade_sent(g):
        for i in range(1, cube.levels - 1):
            for _, _, item in trades(g, i):
                item.wait_send()

    def skip():
        pass

    cot_loads[0].wait()
    first_half(0, during(skip, functools.partial(gather, AG2, 1, 1), skip, functools.partial(gather, AG2, 1, 2)))
    cot_loads[1].start()
    save_chunk(0)
    line.scatter_sent(ph(RS1, 0), *lands(0))
    second_half(0)
    line.gather_sent(ph(AG2, 0), x_at(0))
    outs["x", 0].wait()
    outs["ul", 0].wait()
    scatter(RS3, 0, 0)
    branch_terms(0)
    for k in range(3, n):
        gather(AG2, 1, k)
    save_terms(0)
    outs["hid", 0].wait()
    outs["gl", 0].wait()
    await_terms(0)
    cot_loads[1].wait()
    first_half(1, during(functools.partial(scatter, RS3, 0, 1), skip, functools.partial(scatter, RS3, 0, 2)))
    save_chunk(1)
    line.scatter_sent(ph(RS1, 1), *lands(1))
    second_half(1)
    line.gather_sent(ph(AG2, 1), x_at(1))
    outs["x", 1].wait()
    outs["ul", 1].wait()
    scatter(RS3, 1, 0)
    finish_back(0)
    branch_terms(1)
    save_terms(1)
    outs["hid", 1].wait()
    outs["gl", 1].wait()
    for item in range(1, 4):
        cube.sent(item, block_of(item))
    scatter(RS3, 1, 1)
    gather(AG4, 0, 1)
    start_branch(0)
    await_terms(1)

    def z_one():
        for k in range(2, n - 1):
            scatter(RS3, 1, k)
        gather(AG4, 0, 2)

    weight_grad(0, during(*[skip] * 3, z_one))
    scatter(RS2, 0, 1)
    weight_grad(1, during(*[skip] * 4, functools.partial(finish_back, 1), functools.partial(add_first, 0)))
    mid_save = pltpu.make_async_copy(mid, mid_out, own_sem.at[5])
    mid_save.start()
    for k in range(3, n):
        gather(AG4, 0, k)
    send_out("branch", 0, x.at[0], branch_out.at[:, 0], 0)
    for k in range(2, n - 1):
        scatter(RS2, 0, k)
    weight_grad(2, during(skip, functools.partial(gather, AG4, 1, 1), skip, functools.partial(add_first, 1)))
    finish_branch(0)
    gather(AG4, 1, 2)
    add_first(2)
    for i in range(1, cube.levels - 1):
        add_next(0, i)
    for k in range(3, n):
        gather(AG4, 1, k)
    send_out("branch", 1, x.at[1], branch_out.at[:, 1], 7)
    for g in (1, 2):
        for i in range(1, cube.levels - 1):
            add_next(g, i)
    for g in range(3):
        trade_end(g)
        trade_sent(g)
    first_trade(2).wait_send()
    mid_save.wait()
    line.scatter_sent(ph(RS3, 1), *lands(1))
    for c in range(chunks):
        outs["branch", c].wait()
    for c in range(chunks):
        line.gather_sent(ph(COT, c), cot_at(c))
        line.gather_sent(ph(AG4, c), x_at(c))
        if c == 0:
            line.scatter_sent(ph(RS2, c), *lands(c))


def whole_layer(bounds, gains, live, memory, norm, gate, stream, cot, attn_weights, mlp_weights, tp_size, fsdp_size, collective_id, tile=512):
    chunks = 2
    rows, width = stream.shape
    inner = attn_weights[0].shape[1]
    units = mlp_weights[0].shape[1]
    heads, hd = memory.shape[:2]
    length = rows * tp_size
    c_rows = rows // chunks
    bf, f32 = jnp.bfloat16, jnp.float32
    S = jax.ShapeDtypeStruct
    any_space = pl.BlockSpec(memory_space=pl.ANY)
    vmem = pl.BlockSpec(memory_space=pltpu.VMEM)
    smem = pl.BlockSpec(memory_space=pltpu.SMEM)
    grid_rows = (chunks, tp_size, c_rows)
    flat_rows = (chunks, tp_size * c_rows)
    levels = fsdp_size.bit_length() - 1
    V, DMA = pltpu.VMEM, pltpu.SemaphoreType.DMA
    return pl.pallas_call(
        functools.partial(layer_kernel, chunks=chunks, tp_size=tp_size, fsdp_size=fsdp_size, tile=tile),
        in_specs=[smem] + [vmem] * 5 + [any_space] * 9,
        out_specs=[any_space] * 20 + [vmem] * 6,
        out_shape=[
            S((3, width, units), bf),
            S((width, 4 * inner), bf),
            S((length, width), bf),
            S((length, 3 * inner), bf),
            S((tp_size, chunks, c_rows, inner), bf),
            S((length, inner), f32),
            S(grid_rows + (width,), bf),
            S(grid_rows + (width,), bf),
            S(flat_rows + (units,), bf), S(flat_rows + (units,), bf), S(flat_rows + (units,), bf),
            S(grid_rows + (width,), bf),
            S((rows // chunks, width), bf),
            S((rows, width), f32),
            S((tp_size, chunks, c_rows, width), bf),
            S((3, width // fsdp_size, units), bf),
            S((3, levels - 1, width // 2, units), bf),
            S((length, width), bf),
            S((rows, width), f32),
            S((3, 2, width // fsdp_size // 2, units), bf),
            S((1, width), f32), S((8, 128), f32), S((heads, 1, length), f32), S((heads, hd, hd), f32), S((heads, 1, hd), f32), S((8, width), f32),
        ],
        scratch_shapes=[
            V((3, width, units), bf),
            V(grid_rows + (width,), bf),
            V((tp_size, c_rows, width), bf),
            V(flat_rows[1:] + (units,), bf), V(flat_rows[1:] + (units,), bf), V(flat_rows[1:] + (units,), bf),
            V(grid_rows + (width,), bf),
            V((chunks, tp_size - 1, c_rows, width), bf), V((chunks, tp_size - 1, c_rows, width), bf),
            V((rows, width), bf),
            V((rows, width), f32), V((c_rows, width), f32),
            DMA((9 + chunks,)), DMA((6,)), DMA((max(17, 3 + tp_size + tp_size * chunks),)),
            DMA((2 * tp_size,)), DMA((8 + tp_size,)),
            DMA((3, levels - 1, 2, fsdp_size // 2)), DMA((3, levels - 1, 2, fsdp_size // 2)),
            DMA((levels,)), DMA((levels,)),
            DMA((4, 2, fsdp_size)), DMA((4, 2, fsdp_size)),
            DMA((1 + 6 * chunks, 2, tp_size - 1)), DMA((1 + 6 * chunks, 2, tp_size - 1)),
        ],
        compiler_params=pltpu.CompilerParams(
            collective_id=collective_id, has_side_effects=True, vmem_limit_bytes=60 * 2**20
        ),
        name="layer_kernel",
    )(
        bounds, gains, live, memory, norm.reshape(heads, 1, hd), jnp.broadcast_to(gate[:, None, None], (heads, 1, hd)),
        stream, cot, *attn_weights, *mlp_weights,
    )


def tail_kernel(
    bounds, gains, live_ref, mem_ref, norm_ref, gate_ref, lse_ref, gain_two_ref, stat_ref,
    branch_hbm, attn_hbm, qkv_hbm, mix_hbm, one_hbm, comb_hbm, stream_hbm, all_hbm, gmid_hbm, mid_hbm, terms_hbm, send_hbm,
    grad_out, result_out, land_mlp, land, kept_out,
    dmem_ref, dnorm_ref, sums,
    attn_w, g_ref, spare_ref, rows_ref, one_ref, qkv, dqkv, mixed_ref, gc_ref, part, land_r, land_l, dk_acc, dv_acc,
    sums_land,
    load_sem, out_sem, mlp_send, mlp_recv, sums_send, sums_recv, trade_send, trade_recv, line_send, line_recv,
    *, chunks, tp_size, fsdp_size, tile,
):
    n = tp_size
    bf16, f32 = jnp.bfloat16, jnp.float32
    t, f = lax.axis_index("tp"), lax.axis_index("fsdp")
    c_rows, width = part.shape[2], part.shape[3]
    rows_dev = c_rows * chunks
    length = n * rows_dev
    heads, hd = mem_ref.shape[0], mem_ref.shape[2]
    inner = heads * hd
    shard = width // fsdp_size
    half_rows = shard // 2
    spare = width // 2
    levels, tp_levels = fsdp_size.bit_length() - 1, n.bit_length() - 1
    orders = [[1] + [1 << b for b in range(1, levels)], [1] + [1 << b for b in range(levels - 1, 0, -1)]]
    line = Line(n, line_send, line_recv)
    total, extra = gc_ref.at[0:c_rows, :], gc_ref.at[c_rows : 2 * c_rows, :]
    count = [0]

    def load(src, dst):
        item = pltpu.make_async_copy(src, dst, load_sem.at[count[0]])
        count[0] += 1
        item.start()
        return item

    def peer(bit):
        return lax.bitwise_xor(f, bit)

    def place(s, c):
        return slice(c * n * c_rows + s * c_rows, c * n * c_rows + (s + 1) * c_rows)

    def origin(s, c):
        return slice(s * rows_dev + c * c_rows, s * rows_dev + (c + 1) * c_rows)

    weight_load = load(attn_hbm, attn_w)
    branch_load = load(branch_hbm, rows_ref)
    terms_load = load(terms_hbm.at[chunks - 1], part.at[chunks])
    comb_load = load(comb_hbm, spare_ref.at[:, 0:inner])
    qkv_load = load(qkv_hbm, qkv)
    mix_load = load(mix_hbm, mixed_ref)
    one_loads = [load(one_hbm.at[origin(s, c), :], one_ref.at[place(s, c), :]) for c in range(chunks) for s in range(n)]

    barrier = pltpu.get_barrier_semaphore()
    for k in range(1, n):
        pl.semaphore_signal(barrier, inc=1, device_id={"tp": lax.rem(t + k, n)}, device_id_type=MESH)
    for b in range(levels):
        pl.semaphore_signal(barrier, inc=1, device_id={"fsdp": peer(1 << b)}, device_id_type=MESH)
    pl.semaphore_wait(barrier, n - 1 + levels)

    mlp_trades = [
        pltpu.make_async_remote_copy(
            src_ref=send_hbm.at[g, half],
            dst_ref=land_mlp.at[g, half],
            send_sem=mlp_send.at[g, half],
            recv_sem=mlp_recv.at[g, half],
            device_id={"fsdp": peer(orders[half][-1])},
            device_id_type=MESH,
        )
        for g in range(3)
        for half in range(2)
    ]
    for item in mlp_trades:
        item.start()

    def lands(c):
        return part.at[c], land_r.at[c], land_l.at[c]

    def scatter(c, k):
        line.scatter_step(c, k, *lands(c))

    terms_load.wait()
    scatter(chunks, 0)

    for item in (weight_load, branch_load, comb_load):
        item.wait()

    def store_grad(j, wide, cols, terms):
        for q in range(wide // shard):
            mask = lax.bitwise_xor(j * (wide // shard) + q, f)
            row = lax.rem(mask, 2) * spare + (mask // 2) * shard
            g_ref[pl.ds(pl.multiple_of(row, shard), shard), cols] = terms[q * shard : (q + 1) * shard].astype(bf16)

    wide = 256

    @pl.loop(0, n)
    def _(s):
        rows = pl.ds(pl.multiple_of(s * rows_dev, rows_dev), rows_dev)
        gc_ref[:, pl.ds(pl.multiple_of(s * inner, inner), inner)] = dot32(
            rows_ref[rows, :], attn_w[:, 3 * inner : 4 * inner], NN
        )

    sums[...] = jnp.zeros_like(sums)
    sums[1:2, :] = gain_two_ref[...]
    lane = lax.broadcasted_iota(jnp.int32, (1, width), 1)
    qkv_load.wait()
    mix_load.wait()

    prefix, valid = bounds[0], bounds[1]
    scale = hd ** -0.5

    @pl.loop(0, heads)
    def _(h):
        def lanes(group):
            return pl.ds(pl.multiple_of(group * inner + h * hd, hd), hd)

        gate = jax.nn.sigmoid(gate_ref[h])
        memory, norm = mem_ref[h], norm_ref[h]
        dmem_ref[h] = jnp.zeros((hd, hd), f32)
        dnorm_ref[h] = jnp.zeros((1, hd), f32)
        dgate = jnp.zeros((1, hd), f32)
        for s in range(n - 1, -1, -1):
            first = s * rows_dev
            reach = key_reach(first, rows_dev, length)
            rows = slice(first, first + rows_dev)
            q = qkv[rows, lanes(0)]
            gc = gc_ref[:, pl.ds(pl.multiple_of(s * inner + h * hd, hd), hd)]
            mixed = mixed_ref[rows, lanes(0)]
            qm = mapped(q.astype(f32))
            inverse = 1.0 / jnp.sum(qm * norm, axis=-1, keepdims=True)
            retrieved = dot_three(qm, memory, NN) * inverse
            dgate = dgate + jnp.sum(gc * (retrieved - mixed), axis=0, keepdims=True)
            gnum = gate * gc * inverse
            gden = -jnp.sum(gnum * retrieved, axis=-1, keepdims=True)
            dmem_ref[h] += dot_three(qm, gnum, TN)
            dnorm_ref[h] += jnp.sum(gden * qm, axis=0, keepdims=True)
            dq_mem = (dot_three(gnum, memory, NT) + gden * norm) * jnp.minimum(qm, 1.0)
            low = ((1.0 - gate) * gc).astype(bf16)
            delta = jnp.sum((low.astype(f32) * mixed).T, axis=0, keepdims=True)
            keys = qkv[0:reach, lanes(1)]
            scores = dot32(keys, q, NT) * (scale * LOG2E)
            limit = key_limit(first, rows_dev, prefix, valid)
            scores = jnp.where(
                lax.broadcasted_iota(jnp.int32, scores.shape, 0) <= limit, scores - lse_ref[h, :, rows], NEG
            )
            probs = jnp.exp2(scores)
            gp = dot32(qkv[0:reach, lanes(2)], low, NT)
            gs = (probs * (gp - delta)).astype(bf16)
            dv = dot32(probs.astype(bf16), low, NN)
            dk = dot32(gs, q, NN)
            if s == n - 1:
                dv_acc[...] = dv
                dk_acc[...] = dk
            else:
                dv_acc[0:reach, :] += dv
                dk_acc[0:reach, :] += dk
            dq = (dot32(keys, gs, TN).T * scale + dq_mem).astype(bf16)
            for c in range(chunks):
                dqkv[place(s, c), lanes(0)] = dq[c * c_rows : (c + 1) * c_rows]
        for s in range(n):
            for c in range(chunks):
                dqkv[place(s, c), lanes(1)] = (dk_acc[origin(s, c), :] * scale).astype(bf16)
                dqkv[place(s, c), lanes(2)] = dv_acc[origin(s, c), :].astype(bf16)
        dgate_sum = jnp.sum(dgate * (gate * (1.0 - gate)), axis=-1, keepdims=True)
        sums[2:3, :] += jnp.where(lane == t * heads + h, dgate_sum, 0.0)
        for k in range(1, n - 1):
            @pl.when(h == k)
            def _():
                scatter(chunks, k)

    @pl.loop(0, width // wide)
    def _(j):
        cols = pl.ds(pl.multiple_of(j * wide, wide), wide)
        store_grad(j, wide, slice(3 * inner, 4 * inner), dot32(rows_ref[:, cols], spare_ref[:, 0:inner], TN))

    all_loads = [load(all_hbm.at[origin(s, c), :], rows_ref.at[place(s, c), :]) for c in range(chunks) for s in range(n)]
    for item in all_loads:
        item.wait()

    for c in range(chunks):
        here = slice(c * n * c_rows, (c + 1) * n * c_rows)
        inverse_all = inverse_rms(rows_ref[here, :].astype(f32))
        flat = part.at[c].reshape(n * c_rows, width)

        @pl.loop(0, width // tile)
        def _(j):
            cols = pl.ds(pl.multiple_of(j * tile, tile), tile)
            terms = dot32(dqkv[here, :], attn_w[cols, 0 : 3 * inner], NT)
            flat[:, cols] = terms.astype(bf16)
            unit = rows_ref[here, cols].astype(f32) * inverse_all
            sums[0:1, cols] += jnp.sum(terms * unit, axis=0, keepdims=True)

        scatter(c, 0)

    own_rows = slice(rows_dev - c_rows, rows_dev)
    mid_load = load(mid_hbm.at[own_rows, :], extra)
    line.scatter_end(chunks, *lands(chunks), total)
    mid_load.wait()

    def by_piece(work):
        @pl.loop(0, c_rows // PIECE)
        def _(r):
            work(pl.ds(pl.multiple_of(r * PIECE, PIECE), PIECE), r * PIECE)

    def close_branch(piece, first):
        branch = total[piece, :]
        result = extra[piece, :] + branch
        live = live_ref[pl.ds(pl.multiple_of(rows_dev - c_rows + first, PIECE), PIECE), :]
        part[chunks, t, piece, :] = result.astype(bf16)
        values = (result, branch)
        for at, value in zip((0, 2), values):
            squares = jnp.sum(jnp.sum(value * value, axis=-1, keepdims=True) * live, axis=0, keepdims=True)
            sums[3:4, :] += jnp.where(lane == 3 * f + at, squares, 0.0)

    by_piece(close_branch)
    result_save = pltpu.make_async_copy(part.at[chunks, t], result_out, out_sem.at[0])
    result_save.start()
    for at, row in enumerate((1, 0, 2)):
        sums[3:4, :] += jnp.where(lane == 3 * f + at, stat_ref[row : row + 1, 0:1], 0.0)

    def sums_step(at):
        target = {"fsdp": peer(1 << at)} if at < levels else {"tp": lax.bitwise_xor(t, 1 << (at - levels))}
        return pltpu.make_async_remote_copy(
            src_ref=sums,
            dst_ref=sums_land.at[at],
            send_sem=sums_send.at[at],
            recv_sem=sums_recv.at[at],
            device_id=target,
            device_id_type=MESH,
        )

    def sums_add(at):
        sums_step(at).wait()
        sums[...] += sums_land[at]

    sums_step(0).start()

    for item in one_loads:
        item.wait()

    @pl.loop(0, width // wide)
    def _(j):
        cols = pl.ds(pl.multiple_of(j * wide, wide), wide)
        store_grad(j, wide, slice(0, 3 * inner), dot32(one_ref[:, cols], dqkv[...], TN))

        @pl.when(j == 4)
        def _():
            scatter(0, 1)

    first_trade = pltpu.make_async_remote_copy(
        src_ref=g_ref.at[spare : 2 * spare, :],
        dst_ref=land.at[0],
        send_sem=trade_send.at[0, 0, 0],
        recv_sem=trade_recv.at[0, 0, 0],
        device_id={"fsdp": peer(1)},
        device_id_type=MESH,
    )
    first_trade.start()

    def trades(i):
        for half in range(2):
            order = orders[half]
            bit = order[i]
            for mask in range(fsdp_size):
                if all(mask & b == 0 for b in order[: i + 1]):
                    there = (mask // 2) * shard + half * half_rows
                    here = ((mask ^ bit) // 2) * shard + half * half_rows
                    yield there, pltpu.make_async_remote_copy(
                        src_ref=g_ref.at[here : here + half_rows, :],
                        dst_ref=land.at[i, there : there + half_rows, :],
                        send_sem=trade_send.at[i, half, mask // 2],
                        recv_sem=trade_recv.at[i, half, mask // 2],
                        device_id={"fsdp": peer(bit)},
                        device_id_type=MESH,
                    )

    def add_rows(mine, came):
        g_ref[mine, :] = (g_ref[mine, :].astype(f32) + spare_ref[came, :].astype(f32)).astype(bf16)

    scatter(1, 1)
    sums_add(0)
    sums_step(1).start()
    first_trade.wait_recv()
    first_load = load(land.at[0], spare_ref)
    first_load.wait()

    @pl.loop(0, spare // half_rows)
    def _(r):
        rows = pl.ds(pl.multiple_of(r * half_rows, half_rows), half_rows)
        add_rows(rows, rows)

    for _, item in trades(1):
        item.start()
    for k in range(2, n - 1):
        scatter(0, k)
    sums_add(1)
    sums_step(2).start()

    one_gain = gains[0:1, :]

    def finish(c):
        rows = slice(c * c_rows, (c + 1) * c_rows)
        gmid_load = load(gmid_hbm.at[rows, :], extra)
        stream_load = load(stream_hbm.at[rows, :], part.at[chunks, 0])
        line.scatter_end(c, *lands(c), total)
        gmid_load.wait()
        stream_load.wait()

        def close(piece, first):
            v = part[chunks, 0, piece, :].astype(f32)
            inv = inverse_rms(v)
            u = v * inv
            e = total[piece, :] * one_gain
            total[piece, :] = extra[piece, :] + inv * (e - u * jnp.mean(e * u, axis=-1, keepdims=True))

        by_piece(close)
        save = pltpu.make_async_copy(total, grad_out.at[rows, :], out_sem.at[1])
        save.start()
        save.wait()

    result_save.wait()
    line.scatter_sent(chunks, *lands(chunks))
    for at in range(2, levels):
        sums_add(at)
        sums_step(at + 1).start()
    for k in range(2, n - 1):
        scatter(1, k)
    for i in range(1, levels - 1):
        arrived = list(trades(i))
        loads = []
        for there, item in arrived:
            item.wait_recv()
            loads.append(load(land.at[i, there : there + half_rows, :], spare_ref.at[there : there + half_rows, :]))
        for item in loads:
            item.wait()
        for there, _ in arrived:
            rows = slice(there, there + half_rows)
            add_rows(rows, rows)
        for _, item in trades(i + 1):
            item.start()
    kept_save = pltpu.make_async_copy(g_ref.at[0:shard, :], kept_out, out_sem.at[2])
    kept_save.start()
    finish(0)
    for at in range(levels, levels + tp_levels):
        sums_add(at)
        if at + 1 < levels + tp_levels:
            sums_step(at + 1).start()
    finish(1)
    for _, item in trades(levels - 1):
        item.wait_recv()
    kept_save.wait()
    for item in mlp_trades:
        item.wait()
    first_trade.wait_send()
    for i in range(1, levels):
        for _, item in trades(i):
            item.wait_send()
    for c in range(chunks):
        line.scatter_sent(c, *lands(c))


def whole_tail(
    bounds, gains, live, memory, norm, gate, lse, gain_two, stat,
    branch, attn_full, qkv, mix, flat_one, comb, stream, stream_all, gmid, mid, terms, to_send, tp_size, fsdp_size, collective_id, tile=512,
):
    chunks = 2
    rows, width = stream.shape
    length = rows * tp_size
    c_rows = rows // chunks
    heads, hd = memory.shape[:2]
    inner = heads * hd
    units = to_send.shape[-1]
    shard = width // fsdp_size
    levels, tp_levels = fsdp_size.bit_length() - 1, tp_size.bit_length() - 1
    bf, f32 = jnp.bfloat16, jnp.float32
    S, V, DMA = jax.ShapeDtypeStruct, pltpu.VMEM, pltpu.SemaphoreType.DMA
    any_space = pl.BlockSpec(memory_space=pl.ANY)
    vmem = pl.BlockSpec(memory_space=pltpu.VMEM)
    smem = pl.BlockSpec(memory_space=pltpu.SMEM)
    adds = sum(2 * (fsdp_size >> (i + 1)) for i in range(1, levels - 1))
    loads = 6 + 2 * length // c_rows + 2 + 4 + adds
    return pl.pallas_call(
        functools.partial(tail_kernel, chunks=chunks, tp_size=tp_size, fsdp_size=fsdp_size, tile=tile),
        in_specs=[smem] + [vmem] * 8 + [any_space] * 12,
        out_specs=[any_space] * 5 + [vmem] * 3,
        out_shape=[
            S((rows, width), f32),
            S((c_rows, width), bf),
            S(to_send.shape, bf),
            S((levels, width // 2, 4 * inner), bf),
            S((shard, 4 * inner), bf),
            S((heads, hd, hd), f32), S((heads, 1, hd), f32), S((8, width), f32),
        ],
        scratch_shapes=[
            V((width, 4 * inner), bf),
            V((width, 4 * inner), bf),
            V((width // 2, 4 * inner), bf),
            V((length, width), bf),
            V((length, width), bf),
            V((length, 3 * inner), bf), V((length, 3 * inner), bf),
            V((length, inner), f32), V((rows, tp_size * inner), f32),
            V((chunks + 1, tp_size, c_rows, width), bf),
            V((chunks + 1, tp_size - 1, c_rows, width), bf), V((chunks + 1, tp_size - 1, c_rows, width), bf),
            V((length, hd), f32), V((length, hd), f32),
            V((levels + tp_levels, 8, width), f32),
            DMA((loads,)), DMA((3,)),
            DMA((3, 2)), DMA((3, 2)),
            DMA((levels + tp_levels,)), DMA((levels + tp_levels,)),
            DMA((levels, 2, fsdp_size // 2)), DMA((levels, 2, fsdp_size // 2)),
            DMA((chunks + 1, 2, tp_size - 1)), DMA((chunks + 1, 2, tp_size - 1)),
        ],
        compiler_params=pltpu.CompilerParams(
            collective_id=collective_id, has_side_effects=True, vmem_limit_bytes=60 * 2**20
        ),
        name="tail_kernel",
    )(
        bounds, gains, live, memory, norm.reshape(heads, 1, hd), jnp.broadcast_to(gate[:, None, None], (heads, 1, hd)),
        lse, gain_two, stat, branch, attn_full, qkv, mix, flat_one, comb, stream, stream_all, gmid, mid, terms, to_send,
    )


def on_device(
    stream,
    attn_gain,
    w_query,
    w_key,
    w_value,
    w_out,
    mem_gate,
    mlp_gain,
    w_gate,
    w_up,
    w_down,
    memory,
    normalizer,
    prefix,
    valid,
    cotangent,
):
    f32, bf16 = jnp.float32, jnp.bfloat16
    len_dev, width = (stream.shape[1], stream.shape[2])
    tp_size, fsdp_size = lax.axis_size("tp"), lax.axis_size("fsdp")
    tp_here, seq_here = lax.axis_index("tp"), lax.axis_index("fsdp")
    seq_len = len_dev * tp_size
    heads_here = mem_gate.shape[0]
    prefix_len = prefix[seq_here]
    valid_len = valid[seq_here]
    stream, cotangent = stream[0], cotangent[0]

    shard = width // fsdp_size
    gains = jnp.zeros((8, width), f32)
    gains = lax.dynamic_update_slice(
        gains, jnp.stack([attn_gain, mlp_gain]).astype(f32), (0, seq_here * shard)
    )
    bounds = jnp.stack([prefix_len, valid_len])
    local_position = tp_here * len_dev + jnp.arange(len_dev, dtype=jnp.int32)
    live_here = (local_position < valid_len).astype(f32)[:, None]
    (
        _, attn_full, flat_one, qkv_rows, combined, local_mix, _, _, _, _, _, mlp_terms,
        first_out, grad_middle, branch_low, kept, _, stream_all, middle_rows, to_send,
        gain_two_terms, stats, log_total, memory_next, normalizer_next, gains,
    ) = whole_layer(
        bounds, gains, live_here, memory[0], normalizer[0], mem_gate, stream, cotangent,
        (w_query, w_key, w_value, w_out), (w_gate, w_up, w_down), tp_size, fsdp_size, 1,
    )
    inner = w_query.shape[1]
    stream_grad, second_out, landed, attn_landed, attn_kept, grad_memory, grad_normalizer, joined = whole_tail(
        bounds, gains, live_here, memory[0], normalizer[0], mem_gate, log_total, gain_two_terms, stats,
        branch_low.reshape(seq_len, width), attn_full, qkv_rows, local_mix, flat_one, combined.reshape(seq_len, inner),
        stream, stream_all, grad_middle, middle_rows, mlp_terms, to_send, tp_size, fsdp_size, 2,
    )
    stream_out = jnp.concatenate([first_out, second_out], axis=0)
    gate_grad, up_grad, down_grad = (
        kept[g].astype(f32) + landed[g].reshape(shard, -1).astype(f32) for g in range(3)
    )
    query_grad, key_grad, value_grad, out_grad = (
        attn_kept[:, p * inner : (p + 1) * inner].astype(f32)
        + attn_landed[-1, :shard, p * inner : (p + 1) * inner].astype(f32)
        for p in range(4)
    )
    gain_one_grad = lax.dynamic_slice(joined, (0, seq_here * shard), (1, shard))[0]
    gain_two_grad = lax.dynamic_slice(joined, (1, seq_here * shard), (1, shard))[0]
    gate_grad_logit = lax.dynamic_slice(joined, (2, tp_here * heads_here), (1, heads_here))[0]
    stat_sums = lax.dynamic_slice(joined, (3, seq_here * 3), (1, 3))
    token_count = valid_len.astype(f32) * width
    rms_stats = jnp.sqrt(stat_sums / token_count + rms_eps)
    return (
        stream_out[None],
        stream_grad[None],
        gain_one_grad,
        query_grad,
        key_grad,
        value_grad,
        out_grad,
        gate_grad_logit,
        gain_two_grad,
        gate_grad,
        up_grad,
        down_grad,
        memory_next[None],
        normalizer_next[:, 0][None],
        grad_memory[None],
        grad_normalizer[:, 0][None],
        rms_stats,
    )


def solution(mesh):
    placed = (
        P("fsdp", "tp", None),
        P("fsdp"),
        P("fsdp", "tp"),
        P("fsdp", "tp"),
        P("fsdp", "tp"),
        P("fsdp", "tp"),
        P("tp"),
        P("fsdp"),
        P("fsdp", "tp"),
        P("fsdp", "tp"),
        P("fsdp", "tp"),
        P("fsdp", "tp", None, None),
        P("fsdp", "tp", None),
        P(),
        P(),
        P("fsdp", "tp", None),
    )
    return jax.shard_map(
        on_device,
        mesh=mesh,
        in_specs=placed,
        out_specs=(
            P("fsdp", "tp", None),
            P("fsdp", "tp", None),
            P("fsdp"),
            P("fsdp", "tp"),
            P("fsdp", "tp"),
            P("fsdp", "tp"),
            P("fsdp", "tp"),
            P("tp"),
            P("fsdp"),
            P("fsdp", "tp"),
            P("fsdp", "tp"),
            P("fsdp", "tp"),
            P("fsdp", "tp", None, None),
            P("fsdp", "tp", None),
            P("fsdp", "tp", None, None),
            P("fsdp", "tp", None),
            P("fsdp", None),
        ),
        check_vma=False,
    )
```
